32 devices in a mesh: ctx: 4 (over y, core), fsdp: 8 (over z, x).
Axes of the slice: x: 2, y: 2, z: 4, core: 2. Of those that a mesh axis runs over, the one named last changes fastest.
Arguments:
- inputs: bfloat16 [2, 8, 512, 1024], P(None, 'fsdp', 'ctx'), may hold values from -7.1875 to 7.1875
- timestep: bfloat16 [2, 8, 1024], P(None, 'fsdp'), may hold values from -0.59765625 to 0.59765625
- doc_ids: int32 [2, 8, 512], P(None, 'fsdp', 'ctx'), may hold values from 0 to 3, never falling along the last dimension, each value on 1 to 384 neighbouring positions
- w_qkv: bfloat16 [1024, 3072], P('fsdp'), may hold values from -0.1875 to 0.1875
- w_out: bfloat16 [1024, 1024], P('fsdp'), may hold values from -3 to 3
- w_up: bfloat16 [1024, 4096], P('fsdp'), may hold values from -0.1875 to 0.1875
- w_down: bfloat16 [4096, 1024], P('fsdp'), may hold values from -0.09375 to 0.09375
- bias_model: bfloat16 [4096], P('fsdp'), may hold values from -0.29882812 to 0.29882812
- bias_up: bfloat16 [4096], P('fsdp'), may hold values from -3 to 3
- norm_gains: bfloat16 [2048], P('fsdp'), may hold values from 0.099609375 to 1.8984375
- norm_shifts: bfloat16 [2048], P('fsdp'), may hold values from -3 to 3
- cotangent: bfloat16 [2, 8, 512, 1024], P(None, 'fsdp', 'ctx'), may hold values from -6 to 6
Outputs:
- block_output: bfloat16 [2, 8, 512, 1024], P(None, 'fsdp', 'ctx')
- input_grad: float32 [2, 8, 512, 1024], P(None, 'fsdp', 'ctx')
- grad_qkv: float32 [1024, 3072], P('fsdp')
- grad_out: float32 [1024, 1024], P('fsdp')
- grad_up: float32 [1024, 4096], P('fsdp')
- grad_down: float32 [4096, 1024], P('fsdp')
- grad_bias_model: float32 [4096], P('fsdp')
- grad_bias_up: float32 [4096], P('fsdp')
- grad_gains: float32 [2048], P('fsdp')
- grad_shifts: float32 [2048], P('fsdp')
The draws below stay inside these ranges and needn't reach their ends.
Inputs may be any that keep to these rules, and one draw needn't show every extreme that they name: `doc_ids`: document numbers along a stream never fall; each document holds 1 to 384 consecutive tokens and one holds exactly 384; attention stays within a document.
All inputs are finite; a program needn't handle non-finite values.
Results may differ from the reference program's by a relative error of at most 0.014.
The reference program's roundings to bfloat16 on the way count: a program that leaves them out, or rounds other values in their place, can miss the bound.
Values may be sent and summed in bfloat16 or wider, within the bound.
No kernel may reach another device: no remote copies, remote signals or barrier semaphores. Data moves between devices by JAX's collectives and lax.ppermute only.
A program may use at most 192 MiB of HBM per device.

```python
import math
import jax
import jax.numpy as jnp
import numpy as np
from jax import lax

D = 1024
HEADS = 16
FF = 4096
MB = 2
DOCS = 4
HEAD_SIZE = 64
LEN = 512
STREAMS = 8
DOC_MOST = 384


def levels(key, shape, pieces, least, high):
    level = 1.0
    for position, parts in pieces:
        draws = jax.random.uniform(jax.random.fold_in(jax.random.fold_in(key, 6), position), (parts,), jnp.float32, least / len(pieces), high / len(pieces))
        level = level * jnp.repeat(jnp.exp(draws), shape[position] // parts).reshape((-1,) + (1,) * (len(shape) - 1 - position))
    return level


def length_profile(amount, total, most, slope):
    weights = [(1 << 20) // math.isqrt(standing ** slope) + 1 for standing in range(2, amount + 1)]
    rest, counts = total - most - (amount - 1), [1] * (amount - 1)
    while rest > 0:
        free = [i for i in range(amount - 1) if counts[i] < most]
        pool, left = sum([weights[i] for i in free]), rest
        for i in free:
            more = min(most - counts[i], max(1, left * weights[i] // pool), rest)
            counts[i] = counts[i] + more
            rest = rest - more
    return np.array([most] + counts)


def uneven_parts(rng, amount, total, bound, lean):
    if amount == 2:
        one = jax.random.randint(rng, (), max(1, total - bound), min(bound, total - 1) + 1)
        return jnp.stack([one, total - one])
    lengths = jnp.asarray(length_profile(amount, total, bound, lean), jnp.int32)
    pairs = (amount - 1) // 2
    giver, taker = lengths[1:1 + 2 * pairs:2], lengths[2:2 + 2 * pairs:2]
    margin = jnp.minimum(giver - 1, bound - taker)
    passed = jax.random.randint(jax.random.fold_in(rng, 1), (pairs,), 0, 1 << 20) % (margin + 1)
    lengths = lengths.at[1:1 + 2 * pairs:2].set(giver - passed).at[2:2 + 2 * pairs:2].set(taker + passed)
    return lengths[jax.random.permutation(jax.random.fold_in(rng, 2), amount)]


def bell_draw(stream_key, extent, width, most, shards=(), kind=jnp.bfloat16):
    level = levels(stream_key, extent, shards, -0.22, 0.18) if shards else 1.0
    array = jax.random.normal(stream_key, extent, jnp.float32) * width * level
    return jnp.minimum(jnp.maximum(array, -most), most).astype(kind)


def setup_inputs(seed: int = 0) -> dict:
    seeds = jax.random.split(jax.random.key(seed), 13)
    return {
        "inputs": bell_draw(seeds[0], (MB, STREAMS, LEN, D), 1.2, 7.1875, ((1, 8), (2, 4))),
        "timestep": bell_draw(seeds[1], (MB, STREAMS, D), 0.1, 0.59765625, ((1, 8),)),
        "doc_ids": jax.vmap(lambda own: jnp.searchsorted(jnp.cumsum(uneven_parts(own, DOCS, LEN, DOC_MOST, 2)), jnp.arange(LEN), side="right"))(jax.random.split(seeds[2], MB * STREAMS)).reshape((MB, STREAMS, LEN)).astype(jnp.int32),
        "w_qkv": bell_draw(seeds[3], (D, 3 * D), D ** -0.5, 0.1875, ((0, 8),)),
        "w_out": bell_draw(seeds[4], (D, D), (max(D // 256, 1)) ** -0.5, 3.0, ((0, 8),)),
        "w_up": bell_draw(seeds[5], (D, FF), D ** -0.5, 0.1875, ((0, 8),)),
        "w_down": bell_draw(seeds[6], (FF, D), FF ** -0.5, 0.09375, ((0, 8),)),
        "bias_model": bell_draw(seeds[7], (4 * D,), 0.05, 0.29882812, ((0, 8),)),
        "bias_up": bell_draw(seeds[8], (FF,), 0.5, 3.0, ((0, 8),)),
        "norm_gains": jnp.clip(1.0 + 0.18 * jax.random.normal(seeds[9], (2 * D,), jnp.float32), 0.099609375, 1.8984375).astype(jnp.bfloat16),
        "norm_shifts": bell_draw(seeds[10], (2 * D,), 0.5, 3.0, ((0, 8),)),
        "cotangent": bell_draw(seeds[11], (MB, STREAMS, LEN, D), 1.0, 6.0, ((1, 8), (2, 4))),
    }


norm_epsilon = 1e-05

@jax.custom_vjp
def low(v):
    return lax.optimization_barrier(v.astype(jnp.bfloat16)).astype(jnp.float32)

@jax.custom_vjp
def low_back(v):
    return v

def low_keep(v):
    return (low(v), None)

def low_pass(kept, grad):
    return (grad,)

def back_keep(v):
    return (v, None)

def back_low(kept, grad):
    return (low(grad),)
low.defvjp(low_keep, low_pass)
low_back.defvjp(back_keep, back_low)

def layer_norm(value_in, gain, shift):
    row_mean = lax.optimization_barrier(jnp.mean(value_in, axis=-1, keepdims=True))
    centred = value_in - row_mean
    spread = lax.optimization_barrier(jnp.mean(centred * centred, axis=-1, keepdims=True))
    return centred * lax.rsqrt(spread + norm_epsilon) * gain + shift

def product(left, right):
    return jnp.dot(left, right, precision=lax.Precision.HIGHEST)

def stream_forward(weights_in, hidden_in, timestep_row, doc_row):
    w_qkv, w_out, w_up, w_down, bias_model, bias_up, norm_gains, norm_shifts = weights_in
    hidden0 = hidden_in + timestep_row[None, :]
    rounded0 = low(hidden0)
    projected = product(rounded0, w_qkv)
    query_low = low(low_back(projected[:, :D] + bias_model[:D]))
    key_low = low(low_back(projected[:, D:2 * D]))
    value_low = low(low_back(projected[:, 2 * D:] + bias_model[D:2 * D]))
    same_doc = doc_row[:, None] == doc_row[None, :]
    score_scale = 1.0 / math.sqrt(HEAD_SIZE)

    def attend(head_index):
        col_start = head_index * HEAD_SIZE
        q_head = lax.dynamic_slice_in_dim(query_low, col_start, HEAD_SIZE, 1)
        k_head = lax.dynamic_slice_in_dim(key_low, col_start, HEAD_SIZE, 1)
        v_head = lax.dynamic_slice_in_dim(value_low, col_start, HEAD_SIZE, 1)
        scores = low_back(product(q_head, k_head.T) * score_scale)
        attn_probs = jax.nn.softmax(jnp.where(same_doc, scores, -1e+30), axis=1)
        return product(low(attn_probs), v_head)
    heads_out = lax.map(jax.checkpoint(attend), jnp.arange(HEADS, dtype=jnp.int32))
    attended = low(low_back(jnp.transpose(heads_out, (1, 0, 2)).reshape(LEN, D)))
    branch = low_back(product(attended, w_out) + bias_model[2 * D:3 * D])
    hidden1 = hidden0 + branch
    normed1 = layer_norm(hidden1, norm_gains[:D], norm_shifts[:D])
    upward = low_back(product(low(normed1), w_up) + bias_up)
    activated = jax.nn.gelu(upward, approximate=False)
    feed_out = low_back(product(low(activated), w_down) + bias_model[3 * D:])
    return layer_norm(normed1 + feed_out, norm_gains[D:], norm_shifts[D:])

def reference(inputs, timestep, doc_ids, w_qkv, w_out, w_up, w_down, bias_model, bias_up, norm_gains, norm_shifts, cotangent):
    weights_all = tuple((item.astype(jnp.float32) for item in (w_qkv, w_out, w_up, w_down, bias_model, bias_up, norm_gains, norm_shifts)))
    stream_count = MB * STREAMS
    stream_inputs = inputs.astype(jnp.float32).reshape(stream_count, LEN, D)
    stream_times = timestep.astype(jnp.float32).reshape(stream_count, D)
    stream_docs = doc_ids.reshape(stream_count, LEN)
    stream_cotan = cotangent.astype(jnp.float32).reshape(stream_count, LEN, D)

    def per_stream(grad_sum, stream_item):
        hidden_in, timestep_row, doc_row, cotan_row = stream_item

        def forward(weights_arg, hidden_arg):
            return stream_forward(weights_arg, hidden_arg, timestep_row, doc_row)
        result, pullback = jax.vjp(forward, weights_all, hidden_in)
        grad_weights, grad_input = pullback(cotan_row)
        grad_sum = jax.tree.map(jnp.add, grad_sum, grad_weights)
        return (grad_sum, (result.astype(jnp.bfloat16), grad_input))
    zero_grads = tuple((jnp.zeros_like(item) for item in weights_all))
    totals, (results, input_grads) = lax.scan(per_stream, zero_grads, (stream_inputs, stream_times, stream_docs, stream_cotan))
    return (results.reshape(MB, STREAMS, LEN, D), input_grads.reshape(MB, STREAMS, LEN, D), totals[0], totals[1], totals[2], totals[3], totals[4], totals[5], totals[6], totals[7])
```

```python
import functools
import math

import jax
import jax.numpy as jnp
from jax import lax
from jax.experimental import pallas as pl
from jax.experimental.pallas import tpu as pltpu
from jax.sharding import PartitionSpec as P

HEADS = 16
EPS = 1e-05
LOG2E = math.log2(math.e)
PAD = 16
f32 = jnp.float32
bf16 = jnp.bfloat16


def dot(left, right, dims=((1,), (0,)), out=f32):
    return lax.dot_general(left, right, (dims, ((), ())), preferred_element_type=out)


def over_ctx(value, mask):
    size = lax.axis_size("ctx")
    return lax.ppermute(value, "ctx", [(i, i ^ mask) for i in range(size)])


def over_fsdp(value, mask):
    size = lax.axis_size("fsdp")
    return lax.ppermute(value, "fsdp", [(i, i ^ mask) for i in range(size)])


def attend_kernel(head_size, scale, block_ref, whole_ref, key_doc_ref, query_doc_ref, out_ref, log_ref):
    width = out_ref.shape[1]
    same = key_doc_ref[...] == query_doc_ref[...]
    for head in range(width // head_size):
        cut = head * head_size
        query = block_ref[:, cut : cut + head_size]
        key = whole_ref[:, width + cut : width + cut + head_size]
        value = whole_ref[:, 2 * width + cut : 2 * width + cut + head_size]
        scores = jnp.where(same, dot(key, query, ((1,), (1,))), -1e30)
        top = jnp.max(scores, axis=0, keepdims=True)
        expo = jnp.exp2((scores - top) * (scale * LOG2E))
        total = jnp.sum(expo, axis=0, keepdims=True)
        probs = (expo * (1.0 / total)).astype(bf16)
        out_ref[:, cut : cut + head_size] = dot(value, probs, ((0,), (0,))).T.astype(bf16)
        log_ref[head : head + 1, :] = top * (scale * LOG2E) + jnp.log2(total)


def attend(projected, key_docs, query_docs, head_size):
    length, width = projected.shape[0], projected.shape[1] // 3
    heads = width // head_size
    block = min(512, length)
    return pl.pallas_call(
        functools.partial(attend_kernel, head_size, 1.0 / math.sqrt(head_size)),
        grid=(length // block,),
        in_specs=[
            pl.BlockSpec((block, 3 * width), lambda i: (i, 0)),
            pl.BlockSpec((length, 3 * width), lambda i: (0, 0)),
            pl.BlockSpec((length, 1), lambda i: (0, 0)),
            pl.BlockSpec((1, block), lambda i: (0, i)),
        ],
        out_specs=[
            pl.BlockSpec((block, width), lambda i: (i, 0)),
            pl.BlockSpec((heads, block), lambda i: (0, i)),
        ],
        out_shape=[
            jax.ShapeDtypeStruct((length, width), bf16),
            jax.ShapeDtypeStruct((heads, length), f32),
        ],
        compiler_params=pltpu.CompilerParams(vmem_limit_bytes=48 * 2**20),
        cost_estimate=pl.CostEstimate(
            flops=4 * length * length * width,
            bytes_accessed=8 * length * width,
            transcendentals=heads * length * length,
        ),
    )(projected, projected, key_docs, query_docs)


def attend_back_kernel(
    head_size, scale, steps, block_ref, whole_ref, grad_ref, key_doc_ref, query_doc_ref, log_ref,
    query_out, pair_out, pair_sum,
):
    width = grad_ref.shape[1]
    step = pl.program_id(0)
    same = key_doc_ref[...] == query_doc_ref[...]

    @pl.when(step == 0)
    def _():
        pair_sum[...] = jnp.zeros_like(pair_sum)

    for head in range(width // head_size):
        cut = head * head_size
        query = block_ref[:, cut : cut + head_size]
        key = whole_ref[:, width + cut : width + cut + head_size]
        value = whole_ref[:, 2 * width + cut : 2 * width + cut + head_size]
        grad = grad_ref[:, cut : cut + head_size]
        scores = dot(key, query, ((1,), (1,)))
        probs = jnp.where(
            same, jnp.exp2(scores * (scale * LOG2E) - log_ref[head : head + 1, :]), 0.0
        )
        d_probs = dot(value, grad, ((1,), (1,)))
        inner = jnp.sum(probs * d_probs, axis=0, keepdims=True)
        d_scores = (probs * (d_probs - inner)).astype(bf16)
        query_out[:, cut : cut + head_size] = (
            dot(key, d_scores, ((0,), (0,))).T * scale
        ).astype(bf16)
        pair_sum[:, cut : cut + head_size] += dot(d_scores, query) * scale
        pair_sum[:, width + cut : width + cut + head_size] += dot(probs.astype(bf16), grad)

    @pl.when(step == steps - 1)
    def _():
        pair_out[...] = pair_sum[...].astype(bf16)


def attend_back(projected, grad, key_docs, query_docs, logs, head_size):
    length, width = grad.shape
    heads = width // head_size
    block = min(512, length)
    steps = length // block
    query_grad, pair_grad = pl.pallas_call(
        functools.partial(attend_back_kernel, head_size, 1.0 / math.sqrt(head_size), steps),
        grid=(steps,),
        in_specs=[
            pl.BlockSpec((block, 3 * width), lambda i: (i, 0)),
            pl.BlockSpec((length, 3 * width), lambda i: (0, 0)),
            pl.BlockSpec((block, width), lambda i: (i, 0)),
            pl.BlockSpec((length, 1), lambda i: (0, 0)),
            pl.BlockSpec((1, block), lambda i: (0, i)),
            pl.BlockSpec((heads, block), lambda i: (0, i)),
        ],
        out_specs=[
            pl.BlockSpec((block, width), lambda i: (i, 0)),
            pl.BlockSpec((length, 2 * width), lambda i: (0, 0)),
        ],
        out_shape=[
            jax.ShapeDtypeStruct((length, width), bf16),
            jax.ShapeDtypeStruct((length, 2 * width), bf16),
        ],
        scratch_shapes=[pltpu.VMEM((length, 2 * width), f32)],
        compiler_params=pltpu.CompilerParams(vmem_limit_bytes=56 * 2**20),
        cost_estimate=pl.CostEstimate(
            flops=10 * length * length * width,
            bytes_accessed=16 * length * width,
            transcendentals=heads * length * length,
        ),
    )(projected, projected, grad, key_docs, query_docs, logs)
    return jnp.concatenate([query_grad, pair_grad], axis=1)


def place_kernel(count, rows, spare, where_ref, *refs):
    pieces, outs = refs[:count], refs[count:]
    for j in range(count):
        start = pl.multiple_of(where_ref[j] * rows, rows)
        outs[0][pl.ds(start, rows), :] = pieces[j][:rows, :]
        if spare:
            start = pl.multiple_of(where_ref[j] * spare, spare)
            outs[1][pl.ds(start, spare), :] = pieces[j][rows:, :]


def place(pieces, blocks, spare=0):
    count, rows, columns = len(pieces), pieces[0].shape[0] - spare, pieces[0].shape[1]
    shapes = [jax.ShapeDtypeStruct((count * rows, columns), pieces[0].dtype)]
    if spare:
        shapes.append(jax.ShapeDtypeStruct((count * spare, columns), pieces[0].dtype))
    out = pl.pallas_call(
        functools.partial(place_kernel, count, rows, spare),
        in_specs=[pl.BlockSpec(memory_space=pltpu.SMEM)]
        + [pl.BlockSpec(memory_space=pltpu.VMEM)] * count,
        out_specs=[pl.BlockSpec(memory_space=pltpu.VMEM)] * len(shapes),
        out_shape=shapes,
        compiler_params=pltpu.CompilerParams(vmem_limit_bytes=24 * 2**20),
        cost_estimate=pl.CostEstimate(
            flops=0, bytes_accessed=2 * count * rows * columns * 2, transcendentals=0
        ),
    )(blocks.astype(jnp.int32), *pieces)
    return out if spare else out[0]


def gather_pieces(shard):
    size = lax.axis_size("fsdp")
    pieces = []
    for k in range(size // 2):
        near = over_fsdp(shard, 2 * k) if k else shard
        pieces += [near, over_fsdp(near, 1)]
    return pieces


def reduce_fsdp(near, far):
    index = lax.axis_index("fsdp") // 2
    size = lax.axis_size("fsdp")
    partial = near.astype(f32) + over_fsdp(far.astype(bf16), 1).astype(f32)
    total = lax.dynamic_index_in_dim(partial, index, 0, False)
    for k in range(1, size // 2):
        total = total + over_fsdp(
            lax.dynamic_index_in_dim(partial, index ^ k, 0, False).astype(bf16), 2 * k
        ).astype(f32)
    return total


def by_parity(grad):
    size = lax.axis_size("fsdp")
    odd = lax.axis_index("fsdp") % 2
    blocks = grad.reshape(size // 2, 2, grad.shape[0] // size, grad.shape[1])
    return (
        lax.dynamic_index_in_dim(blocks, odd, 1, False),
        lax.dynamic_index_in_dim(blocks, 1 - odd, 1, False),
    )


def gather_tokens(own):
    have, mask = own, 1
    while 2 * mask < lax.axis_size("ctx"):
        got = over_ctx(have, 2 * mask)
        have = got if mask == 1 and lax.axis_size("ctx") == 4 else jnp.concatenate([have, got])
        mask *= 2
    return have if lax.axis_size("ctx") == 4 else have[own.shape[0] :]


def reduce_tokens(own, rest):
    ways = lax.axis_size("ctx") // 2
    if ways == 2:
        return own + over_ctx(rest.astype(bf16), 2).astype(f32)
    have, mask = jnp.concatenate([own, rest]), ways // 2
    while mask:
        half = have.shape[0] // 2
        have = have[:half] + over_ctx(have[half:].astype(bf16), 2 * mask).astype(f32)
        mask //= 2
    return have


def norm_parts(value):
    centred = value - jnp.mean(value, axis=-1, keepdims=True)
    inverse = lax.rsqrt(jnp.mean(centred * centred, axis=-1, keepdims=True) + EPS)
    return centred * inverse, inverse


def norm_back(grad, normal, inverse, gain):
    inner = grad * gain
    return inverse * (
        inner
        - jnp.mean(inner, axis=-1, keepdims=True)
        - normal * jnp.mean(inner * normal, axis=-1, keepdims=True)
    )


def gelu_and_slope(upward):
    lower = 0.5 * lax.erfc(upward * -math.sqrt(0.5))
    density = jnp.exp(-0.5 * upward * upward) * (1.0 / math.sqrt(2.0 * math.pi))
    return upward * lower, lower + upward * density


def per_device(
    inputs, timestep, doc_ids, w_qkv, w_out, w_up, w_down, bias_model, bias_up,
    norm_gains, norm_shifts, cotangent,
):
    ctx, ctx_size = lax.axis_index("ctx"), lax.axis_size("ctx")
    fsdp, fsdp_size = lax.axis_index("fsdp"), lax.axis_size("fsdp")
    core, ways = ctx % 2, ctx_size // 2
    tokens, width = inputs.shape[2], w_out.shape[1]
    hidden = w_up.shape[1]
    head_size = width // HEADS
    own_rows = 2 * tokens
    group = width // ctx_size
    group_ff = hidden // ctx_size
    shard = w_out.shape[0]
    shard_ff = w_down.shape[0]
    fsdp_range = jnp.arange(fsdp_size)

    small = jnp.concatenate([bias_model, bias_up, norm_gains, norm_shifts])
    small_count = small.shape[0]
    qkv_group = lax.dynamic_index_in_dim(
        w_qkv.reshape(shard, 3, ctx_size, group), ctx, 2, False
    ).reshape(shard, 3 * group)
    small_rows = jnp.pad(small, (0, PAD * 3 * group - small_count)).reshape(PAD, 3 * group)
    qkv_pieces = gather_pieces(jnp.concatenate([qkv_group, small_rows]))
    out_send = lax.dynamic_index_in_dim(w_out.reshape(shard, 2, width // 2), core, 1, False)
    up_send = lax.dynamic_index_in_dim(
        w_up.reshape(shard, fsdp_size, ctx_size, hidden // (fsdp_size * ctx_size)), ctx, 2, False
    ).reshape(shard, group_ff)
    down_send = lax.dynamic_index_in_dim(
        w_down.reshape(ctx_size, shard_ff // ctx_size, width), ctx, 0, False
    )
    natural = fsdp_range ^ fsdp

    mine = lax.dynamic_index_in_dim(inputs[:, 0], core, 0, False)
    theirs = lax.dynamic_index_in_dim(inputs[:, 0], 1 - core, 0, False)
    docs = doc_ids[:, 0].astype(bf16)
    doc_rows = jnp.pad(docs[:, None, :], ((0, 0), (0, PAD - 1), (0, width - tokens)))
    cot_mine = lax.dynamic_index_in_dim(cotangent[:, 0], core, 0, False)
    cot_theirs = lax.dynamic_index_in_dim(cotangent[:, 0], 1 - core, 0, False)
    doc_mine = lax.dynamic_index_in_dim(doc_rows, core, 0, False)
    doc_theirs = lax.dynamic_index_in_dim(doc_rows, 1 - core, 0, False)
    swapped = over_ctx(jnp.concatenate([theirs, doc_theirs, cot_theirs]), 1)
    got_x, got_doc, got_cot = (
        swapped[:tokens], swapped[tokens : tokens + PAD], swapped[tokens + PAD :],
    )
    x_own = jnp.concatenate([mine, got_x])
    cot_own = jnp.concatenate([cot_mine, got_cot]).astype(f32)
    doc_own = jnp.concatenate([doc_mine[:1, :tokens], got_doc[:1, :tokens]], axis=1)
    packed = jnp.concatenate([x_own, jnp.pad(doc_own, ((0, PAD - 1), (0, width - own_rows)))])
    rest = gather_tokens(packed).reshape(ways - 1, own_rows + PAD, width)
    x_rest = rest[:, :own_rows].reshape((ways - 1) * own_rows, width)
    doc_all = jnp.concatenate([doc_own[0], rest[:, own_rows, :own_rows].reshape(-1)]).astype(f32)
    key_docs, query_docs = doc_all[:, None], doc_all[None, :]
    time_row = lax.dynamic_index_in_dim(timestep[:, 0], core, 0, True).astype(f32)
    hidden0 = x_own.astype(f32) + time_row
    rounded0 = jnp.concatenate([hidden0, x_rest.astype(f32) + time_row]).astype(bf16)

    w_qkv_mine, small_all = place(qkv_pieces, natural, PAD)
    w_qkv_pair = (w_qkv_mine, over_ctx(w_qkv_mine, 1))
    small_all = small_all.reshape(fsdp_size, PAD * 3 * group)[:, :small_count].astype(f32)
    starts = [0, bias_model.shape[0]]
    starts.append(starts[1] + bias_up.shape[0])
    starts.append(starts[2] + norm_gains.shape[0])
    starts.append(small_count)
    b_model, b_up, gains, shifts = (
        small_all[:, a:b].reshape(-1) for a, b in zip(starts[:-1], starts[1:])
    )
    b_up_groups = b_up.reshape(fsdp_size, ctx_size, -1)

    projected, attended, logs = [], [], []
    for i in range(2):
        who = ctx ^ i
        b_query = lax.dynamic_slice_in_dim(b_model, who * group, group)
        b_value = lax.dynamic_slice_in_dim(b_model, width + who * group, group)
        bias = jnp.concatenate([b_query, jnp.zeros_like(b_query), b_value])
        proj = (dot(rounded0, w_qkv_pair[i]) + bias[None]).astype(bf16)
        out, log = attend(proj, key_docs, query_docs, head_size)
        projected.append(proj)
        attended.append(out)
        logs.append(log)
    attended_pair = jnp.concatenate(attended, axis=1)
    attended_cols = [attended_pair[:own_rows]]
    for k in range(1, ways):
        attended_cols.append(over_ctx(attended_pair[k * own_rows : (k + 1) * own_rows], 2 * k))
    attended_own = jnp.concatenate(attended_cols, axis=1)

    ratio = fsdp_size // ctx_size if fsdp_size >= ctx_size else 1
    out_blocks = ((natural // ratio) ^ ctx) * ratio + natural % ratio
    out_half = place(gather_pieces(out_send), out_blocks)
    out_other = over_ctx(out_half, 1)
    out_other = out_other.reshape(ctx_size // 2, 2, group, width // 2)[:, ::-1].reshape(
        width, width // 2
    )
    w_out_all = jnp.concatenate(
        [jnp.where(core == 0, out_half, out_other), jnp.where(core == 0, out_other, out_half)],
        axis=1,
    )
    hidden1 = hidden0 + dot(attended_own, w_out_all) + b_model[2 * width : 3 * width][None]
    normal1, inverse1 = norm_parts(hidden1)
    normed1 = normal1 * gains[None, :width] + shifts[None, :width]
    normed_own = normed1.astype(bf16)
    normed_rest = gather_tokens(normed_own)

    up_mine = place(gather_pieces(up_send), natural)
    up_pair = (up_mine, over_ctx(up_mine, 1))
    down_mine = place(gather_pieces(down_send), natural)
    down_pair = (down_mine, over_ctx(down_mine, 1))
    b_up_pair = [
        lax.dynamic_index_in_dim(b_up_groups, ctx ^ i, 1, False).reshape(1, group_ff)
        for i in range(2)
    ]
    acts, slopes, feeds = {}, {}, []
    for part, rows in (("rest", normed_rest), ("own", normed_own)):
        feed = 0.0
        for i in range(2):
            act, slope = gelu_and_slope(dot(rows, up_pair[i]) + b_up_pair[i])
            acts[part, i], slopes[part, i] = act.astype(bf16), slope
            feed = feed + dot(acts[part, i], down_pair[i])
        feeds.append(feed)
    feed_own = reduce_tokens(feeds[1], feeds[0]) + b_model[3 * width :][None]

    normal2, inverse2 = norm_parts(normed1 + feed_own)
    result = (normal2 * gains[None, width:] + shifts[None, width:]).astype(bf16)
    d_gain2, d_shift2 = jnp.sum(cot_own * normal2, axis=0), jnp.sum(cot_own, axis=0)
    d_hidden2 = norm_back(cot_own, normal2, inverse2, gains[None, width:])
    d_feed_own = d_hidden2.astype(bf16)
    d_feed_rest = gather_tokens(d_feed_own)

    d_ups, d_normed = {}, []
    for part, rows in (("rest", d_feed_rest), ("own", d_feed_own)):
        total = 0.0
        for i in range(2):
            d_act = dot(rows, down_pair[i], ((1,), (1,)))
            d_ups[part, i] = (d_act * slopes[part, i]).astype(bf16)
            total = total + dot(d_ups[part, i], up_pair[i], ((1,), (1,)))
        d_normed.append(total)
    d_normed1 = d_hidden2 + reduce_tokens(d_normed[1], d_normed[0])

    d_feed_all = jnp.concatenate([d_feed_own, d_feed_rest])
    normed_all = jnp.concatenate([normed_own, normed_rest])
    g_down, g_up, d_up_sums = [], [], []
    for i in range(2):
        act_all = jnp.concatenate([acts["own", i], acts["rest", i]])
        d_up_all = jnp.concatenate([d_ups["own", i], d_ups["rest", i]])
        g_down.append(dot(act_all, d_feed_all, ((0,), (0,))))
        g_up.append(dot(normed_all, d_up_all, ((0,), (0,))))
        d_up_sums.append(jnp.sum(d_up_all.astype(f32), axis=0))
    down_sum = g_down[0] + over_ctx(g_down[1].astype(bf16), 1).astype(f32)
    up_sum = g_up[0] + over_ctx(g_up[1].astype(bf16), 1).astype(f32)
    down_total = reduce_fsdp(*by_parity(down_sum))
    up_total = reduce_fsdp(*by_parity(up_sum))

    d_gain1, d_shift1 = jnp.sum(d_normed1 * normal1, axis=0), jnp.sum(d_normed1, axis=0)
    d_hidden1 = norm_back(d_normed1, normal1, inverse1, gains[None, :width])
    d_branch = d_hidden1.astype(bf16)
    d_attended = dot(d_branch, w_out_all, ((1,), (1,))).astype(bf16)
    d_attended_rows = [d_attended[:, : 2 * group]]
    for k in range(1, ways):
        d_attended_rows.append(
            over_ctx(d_attended[:, 2 * k * group : 2 * (k + 1) * group], 2 * k)
        )
    d_attended_pair = jnp.concatenate(d_attended_rows)

    g_out = dot(attended_own, d_branch, ((0,), (0,))).reshape(ctx_size, group, width)
    g_out = jnp.concatenate(
        [lax.dynamic_index_in_dim(g_out, ctx ^ i, 0, False) for i in range(ctx_size)]
    )
    part = g_out.reshape(width, 2, width // 2)
    out_sum = lax.dynamic_index_in_dim(part, core, 1, False) + over_ctx(
        lax.dynamic_index_in_dim(part, 1 - core, 1, False).astype(bf16), 1
    ).astype(f32)
    for k in range(int(math.log2(ways))):
        half = out_sum.shape[1] // 2
        part = out_sum.reshape(width, 2, half)
        high = (ctx >> (k + 1)) % 2
        out_sum = lax.dynamic_index_in_dim(part, high, 1, False) + over_ctx(
            lax.dynamic_index_in_dim(part, 1 - high, 1, False).astype(bf16), 2 << k
        ).astype(f32)
    out_total = reduce_fsdp(*by_parity(out_sum))

    g_qkv, d_projected, dx_own, dx_rest = [], [], 0.0, 0.0
    for i in range(2):
        grad = attend_back(
            projected[i], d_attended_pair[:, i * group : (i + 1) * group],
            key_docs, query_docs, logs[i], head_size,
        )
        d_projected.append(grad)
        dx_rest = dx_rest + dot(grad[own_rows:], w_qkv_pair[i], ((1,), (1,)))
        dx_own = dx_own + dot(grad[:own_rows], w_qkv_pair[i], ((1,), (1,)))
        g_qkv.append(dot(rounded0, grad, ((0,), (0,))))
    d_input = d_hidden1 + reduce_tokens(dx_own, dx_rest)

    proj_sums = [jnp.sum(grad.astype(f32), axis=0) for grad in d_projected]

    def in_groups(pair, axis_size):
        stacked = jnp.stack(pair)
        base = jnp.zeros((ctx_size, axis_size), f32)
        ordered = jnp.where(core == 0, stacked, stacked[::-1])
        return lax.dynamic_update_slice_in_dim(base, ordered, ctx - core, 0)

    vec_query = in_groups([s[:group] for s in proj_sums], group).reshape(-1)
    vec_value = in_groups([s[2 * group :] for s in proj_sums], group).reshape(-1)
    vec_up = jnp.swapaxes(
        in_groups(d_up_sums, group_ff).reshape(ctx_size, fsdp_size, -1), 0, 1
    ).reshape(fsdp_size, -1)
    column = functools.partial(jnp.sum, axis=0)
    vec_model = jnp.concatenate(
        [vec_query, vec_value, column(d_branch.astype(f32)), column(d_feed_own.astype(f32))]
    ).reshape(fsdp_size, -1)
    vec_gain = jnp.concatenate([d_gain1, d_gain2]).reshape(fsdp_size, -1)
    vec_shift = jnp.concatenate([d_shift1, d_shift2]).reshape(fsdp_size, -1)
    vectors = jnp.concatenate([vec_model, vec_up, vec_gain, vec_shift], axis=1)
    half_count = small_count // 2

    halves = vectors.reshape(fsdp_size, 2, half_count)
    vec_mine = lax.dynamic_index_in_dim(halves, core, 1, False)
    vec_theirs = lax.dynamic_index_in_dim(halves, 1 - core, 1, False)
    send = jnp.concatenate(
        [g_qkv[1].astype(bf16).reshape(fsdp_size, shard, 3 * group), rows_of_half(vec_theirs, group)], axis=1
    )
    got = over_ctx(send, 1)
    qkv_sum = g_qkv[0].reshape(fsdp_size, shard, 3 * group) + got[:, :shard].astype(f32)
    odd = fsdp % 2

    def values_of(rows):
        flat = rows.astype(f32).reshape(rows.shape[0], PAD * 3 * group)
        return flat[:, :half_count] + flat[:, half_count : 2 * half_count]

    vec_sum = vec_mine + values_of(got[:, shard:])

    def pick(array, parity):
        return lax.dynamic_index_in_dim(
            array.reshape((fsdp_size // 2, 2) + array.shape[1:]), parity, 1, False
        )

    far = jnp.concatenate(
        [pick(qkv_sum, 1 - odd).astype(bf16), rows_of_half(pick(vec_sum, 1 - odd), group)], axis=1
    )
    got = over_fsdp(far, 1)
    qkv_sum = pick(qkv_sum, odd) + got[:, :shard].astype(f32)
    vec_sum = pick(vec_sum, odd) + values_of(got[:, shard:])
    place_z = fsdp // 2
    qkv_total = lax.dynamic_index_in_dim(qkv_sum, place_z, 0, False)
    vec_total = lax.dynamic_index_in_dim(vec_sum, place_z, 0, True)
    for k in range(1, fsdp_size // 2):
        block = lax.dynamic_index_in_dim(qkv_sum, place_z ^ k, 0, False).astype(bf16)
        vec_rows = rows_of_half(lax.dynamic_index_in_dim(vec_sum, place_z ^ k, 0, True), group)[0]
        got = over_fsdp(jnp.concatenate([block, vec_rows]), 2 * k)
        qkv_total = qkv_total + got[:shard].astype(f32)
        vec_total = vec_total + values_of(got[None, shard:])

    def spread(total):
        have = total.astype(bf16)[None]
        mask = 1
        while mask < ctx_size:
            got = over_ctx(have, mask)
            first = (ctx // mask) % 2 == 0
            have = jnp.concatenate([jnp.where(first, have, got), jnp.where(first, got, have)])
            mask *= 2
        return have

    tail = spread(jnp.concatenate([qkv_total.astype(bf16), rows_of_half(vec_total, group)[0]]))
    grad_qkv = jnp.transpose(
        tail[:, :shard].reshape(ctx_size, shard, 3, group), (1, 2, 0, 3)
    ).reshape(shard, 3 * width).astype(f32)
    vec_halves = values_of(tail[:, shard:]).reshape(ways, 2, half_count)
    vec_done = jnp.sum(vec_halves, axis=0).reshape(small_count)
    downs = spread(down_total)
    grad_down = downs.reshape(shard_ff, width).astype(f32)
    ups = spread(up_total).reshape(ctx_size, shard, fsdp_size, -1)
    grad_up = jnp.transpose(ups, (1, 2, 0, 3)).reshape(shard, hidden).astype(f32)
    outs = spread(out_total)
    order = []
    for place_index in range(ctx_size):
        bits, device = place_index, 0
        for level in range(int(math.log2(ctx_size))):
            device |= ((bits >> (int(math.log2(ctx_size)) - 1 - level)) & 1) << level
        order.append(device)
    grad_out = jnp.concatenate([outs[d] for d in order], axis=1).astype(f32)

    def give_back(value):
        keep, got = value[:tokens], over_ctx(value[tokens:], 1)
        return jnp.stack([jnp.where(core == 0, keep, got), jnp.where(core == 0, got, keep)])

    block_output = give_back(result)[:, None]
    input_grad = give_back(d_input)[:, None]
    return (
        block_output, input_grad, grad_qkv, grad_out, grad_up, grad_down,
        *(vec_done[a:b] for a, b in zip(starts[:-1], starts[1:])),
    )


def rows_of_half(values, group):
    high = values.astype(bf16)
    low = (values - high.astype(f32)).astype(bf16)
    both = jnp.concatenate([high, low], axis=1)
    both = jnp.pad(both, ((0, 0), (0, PAD * 3 * group - both.shape[1])))
    return both.reshape(values.shape[0], PAD, 3 * group)


def solution(mesh):
    token = P(None, "fsdp", "ctx", None)
    rows = P("fsdp", None)
    flat = P("fsdp")
    return jax.shard_map(
        per_device,
        mesh=mesh,
        in_specs=(
            token, P(None, "fsdp", None), P(None, "fsdp", "ctx"), rows, rows, rows, rows,
            flat, flat, flat, flat, token,
        ),
        out_specs=(token, token, rows, rows, rows, rows, flat, flat, flat, flat),
        check_vma=False,
    )
```

```python
import functools
import math

import jax
import jax.numpy as jnp
from jax import lax
from jax.experimental import pallas as pl
from jax.experimental.pallas import tpu as pltpu
from jax.sharding import PartitionSpec as P

HEADS = 16
EPS = 1e-05
LOG2E = math.log2(math.e)
VEC = 8
PAD = 2 * VEC
f32 = jnp.float32
bf16 = jnp.bfloat16


def dot(left, right, dims=((1,), (0,))):
    return lax.dot_general(left, right, (dims, ((), ())), preferred_element_type=f32)


def over_ctx(value, mask):
    size = lax.axis_size("ctx")
    return lax.ppermute(value, "ctx", [(i, i ^ mask) for i in range(size)])


def over_fsdp(value, mask):
    size = lax.axis_size("fsdp")
    return lax.ppermute(value, "fsdp", [(i, i ^ mask) for i in range(size)])


def after(value, *others):
    return lax.optimization_barrier((value, *others))[0]


def shape(dims, dtype=f32):
    return jax.ShapeDtypeStruct(tuple(dims), dtype)


def kernel_call(body, outs, args, scalars=(), scratch=(), flops=50_000_000_000):
    scalars = [jnp.asarray(s, jnp.int32).reshape(-1) for s in scalars]
    specs = [pl.BlockSpec(memory_space=pltpu.SMEM)] * len(scalars)
    specs += [pl.BlockSpec(memory_space=pltpu.VMEM)] * len(args)
    largest = max(math.prod(a.shape) * 4 for a in [*args, *outs])
    held = sum(math.prod(a.shape) * jnp.dtype(a.dtype).itemsize for a in scratch)
    limit = min(held + max(6 * 2**20, 2 * largest), 56 * 2**20)
    return pl.pallas_call(
        body,
        in_specs=specs,
        out_specs=[pl.BlockSpec(memory_space=pltpu.VMEM)] * len(outs),
        out_shape=list(outs),
        scratch_shapes=list(scratch),
        compiler_params=pltpu.CompilerParams(vmem_limit_bytes=limit),
        cost_estimate=pl.CostEstimate(flops=flops, bytes_accessed=1024, transcendentals=0),
    )(*scalars, *args)


def attend_kernel(head_size, scale, block_ref, whole_ref, key_doc_ref, query_doc_ref, out_ref, log_ref):
    width = out_ref.shape[1]
    same = key_doc_ref[...] == query_doc_ref[...]
    for head in range(width // head_size):
        cut = head * head_size
        query = block_ref[:, cut : cut + head_size]
        key = whole_ref[:, width + cut : width + cut + head_size]
        value = whole_ref[:, 2 * width + cut : 2 * width + cut + head_size]
        scores = jnp.where(same, dot(key, query, ((1,), (1,))), -1e30)
        top = jnp.max(scores, axis=0, keepdims=True)
        expo = jnp.exp2((scores - top) * (scale * LOG2E))
        total = jnp.sum(expo, axis=0, keepdims=True)
        probs = (expo * (1.0 / total)).astype(bf16)
        out_ref[:, cut : cut + head_size] = dot(value, probs, ((0,), (0,))).T.astype(bf16)
        log_ref[head : head + 1, :] = top * (scale * LOG2E) + jnp.log2(total)


def attend(projected, key_docs, query_docs, head_size):
    length, width = projected.shape[0], projected.shape[1] // 3
    heads = width // head_size
    block = min(512, length)
    return pl.pallas_call(
        functools.partial(attend_kernel, head_size, 1.0 / math.sqrt(head_size)),
        grid=(length // block,),
        in_specs=[
            pl.BlockSpec((block, 3 * width), lambda i: (i, 0)),
            pl.BlockSpec((length, 3 * width), lambda i: (0, 0)),
            pl.BlockSpec((length, 1), lambda i: (0, 0)),
            pl.BlockSpec((1, block), lambda i: (0, i)),
        ],
        out_specs=[
            pl.BlockSpec((block, width), lambda i: (i, 0)),
            pl.BlockSpec((heads, block), lambda i: (0, i)),
        ],
        out_shape=[shape((length, width), bf16), shape((heads, length))],
        compiler_params=pltpu.CompilerParams(vmem_limit_bytes=(24 if length <= 512 else 48) * 2**20),
        cost_estimate=pl.CostEstimate(
            flops=0, bytes_accessed=1024, transcendentals=0,
        ),
    )(projected, projected, key_docs, query_docs)


def attend_back_kernel(head_size, scale, steps, first, pieces, *refs):
    block_ref, whole_ref, key_doc_ref, query_doc_ref, log_ref = refs[:5]
    grad_refs, (query_out, pair_out, pair_sum) = refs[5 : 5 + pieces], refs[5 + pieces :]
    width = query_out.shape[1]
    step = pl.program_id(0)
    same = key_doc_ref[...] == query_doc_ref[...]

    if steps > 1:
        @pl.when(step == 0)
        def _():
            pair_sum[...] = jnp.zeros_like(pair_sum)

    def add(place, value):
        if steps > 1:
            pair_sum[:, place : place + head_size] += value
        else:
            pair_out[:, place : place + head_size] = value.astype(bf16)

    for head in range(width // head_size):
        cut = head * head_size
        query = block_ref[:, cut : cut + head_size]
        key = whole_ref[:, width + cut : width + cut + head_size]
        value = whole_ref[:, 2 * width + cut : 2 * width + cut + head_size]
        span = slice(first + cut, first + cut + head_size)
        grad = jnp.concatenate([ref[:, span] for ref in grad_refs]) if pieces > 1 else grad_refs[0][:, span]
        scores = dot(key, query, ((1,), (1,)))
        probs = jnp.where(
            same, jnp.exp2(scores * (scale * LOG2E) - log_ref[head : head + 1, :]), 0.0
        )
        d_probs = dot(value, grad, ((1,), (1,)))
        inner = jnp.sum(probs * d_probs, axis=0, keepdims=True)
        d_scores = (probs * (d_probs - inner)).astype(bf16)
        query_out[:, cut : cut + head_size] = (
            dot(key, d_scores, ((0,), (0,))).T * scale
        ).astype(bf16)
        add(cut, dot(d_scores, query) * scale)
        add(width + cut, dot(probs.astype(bf16), grad))

    if steps > 1:
        @pl.when(step == steps - 1)
        def _():
            pair_out[...] = pair_sum[...].astype(bf16)


def attend_back(projected, grads, first, key_docs, query_docs, logs, head_size):
    length, width = projected.shape[0], projected.shape[1] // 3
    heads = width // head_size
    block = min(512, length)
    steps = length // block
    if steps > 1:
        grads = [jnp.concatenate(grads)]
    grad_rows = [grad.shape[0] // steps for grad in grads]
    return pl.pallas_call(
        functools.partial(
            attend_back_kernel, head_size, 1.0 / math.sqrt(head_size), steps, first, len(grads)
        ),
        grid=(steps,),
        in_specs=[
            pl.BlockSpec((block, 3 * width), lambda i: (i, 0)),
            pl.BlockSpec((length, 3 * width), lambda i: (0, 0)),
            pl.BlockSpec((length, 1), lambda i: (0, 0)),
            pl.BlockSpec((1, block), lambda i: (0, i)),
            pl.BlockSpec((heads, block), lambda i: (0, i)),
        ]
        + [pl.BlockSpec((rows, grads[0].shape[1]), lambda i: (i, 0)) for rows in grad_rows],
        out_specs=[
            pl.BlockSpec((block, width), lambda i: (i, 0)),
            pl.BlockSpec((length, 2 * width), lambda i: (0, 0)),
        ],
        out_shape=[shape((length, width), bf16), shape((length, 2 * width), bf16)],
        scratch_shapes=[pltpu.VMEM((length if steps > 1 else 8, 2 * width), f32)],
        compiler_params=pltpu.CompilerParams(vmem_limit_bytes=(24 if length <= 512 else 56) * 2**20),
        cost_estimate=pl.CostEstimate(flops=0, bytes_accessed=1024, transcendentals=0),
    )(projected, projected, key_docs, query_docs, logs, *grads)


def place_kernel(count, rows, columns, where_ref, *refs):
    pieces, (qkv_ref, small_ref, mine_ref, theirs_ref) = refs[:count], refs[count:]
    for j, piece in enumerate(pieces):
        spare = piece.shape[0] - rows
        start = pl.multiple_of(where_ref[j] * rows, rows)
        qkv_ref[pl.ds(start, rows), :] = piece[:rows, :columns]
        start = pl.multiple_of(where_ref[j] * spare, spare)
        small_ref[pl.ds(start, spare), :] = piece[rows:, :columns]
        for way, ref in enumerate((mine_ref, theirs_ref), 1):
            start = pl.multiple_of(where_ref[way * count + j] * rows, rows)
            ref[pl.ds(start, rows), :] = piece[:rows, columns:]


def place(pieces, orders, rows, columns):
    count, spare = len(pieces), pieces[0].shape[0] - rows
    rest = pieces[0].shape[1] - columns
    return kernel_call(
        functools.partial(place_kernel, count, rows, columns),
        [
            shape((count * rows, columns), bf16), shape((count * spare, columns), bf16),
            shape((count * rows, rest), bf16), shape((count * rows, rest), bf16),
        ],
        pieces,
        scalars=[jnp.concatenate(orders)],
    )


def gather_near(shard):
    size = lax.axis_size("fsdp")
    return [shard] + [over_fsdp(shard, 2 * k) for k in range(1, size // 2)]


def gather_far(near):
    pieces = []
    for value in near:
        pieces += [value, over_fsdp(value, 1)]
    return pieces


def gather_tokens(own):
    have, mask = own, 1
    while 2 * mask < lax.axis_size("ctx"):
        got = over_ctx(have, 2 * mask)
        if lax.axis_size("ctx") == 4:
            return got
        have = jnp.concatenate([have, got])
        mask *= 2
    return have[own.shape[0] :]


def reduce_tokens(own, rest):
    ways = lax.axis_size("ctx") // 2
    if ways == 2:
        return own, over_ctx(rest, 2)
    have, mask = jnp.concatenate([own, rest.astype(f32)]), ways // 2
    while mask > 1:
        half = have.shape[0] // 2
        have = have[:half] + over_ctx(have[half:].astype(bf16), 2 * mask).astype(f32)
        mask //= 2
    half = have.shape[0] // 2
    return have[:half], over_ctx(have[half:].astype(bf16), 2)


def norm_parts(value):
    centred = value - jnp.mean(value, axis=-1, keepdims=True)
    inverse = lax.rsqrt(jnp.mean(centred * centred, axis=-1, keepdims=True) + EPS)
    return centred * inverse, inverse


def norm_back(grad, normal, inverse, gain):
    inner = grad * gain
    return inverse * (
        inner
        - jnp.mean(inner, axis=-1, keepdims=True)
        - normal * jnp.mean(inner * normal, axis=-1, keepdims=True)
    )


def column_sums(*values):
    rows = [jnp.sum(value, axis=0, keepdims=True) for value in values]
    return jnp.concatenate(rows + [jnp.zeros_like(rows[0])] * (8 - len(rows)))


def out_kernel(
    core_ref, att_ref, mine_ref, other_ref, x_ref, vec_ref, normal_ref, inverse_ref, normed_ref, hidden_ref
):
    half = mine_ref.shape[1]
    core = core_ref[0]
    for way, ref in ((core, mine_ref), (1 - core, other_ref)):
        hidden_ref[:, pl.ds(pl.multiple_of(way * half, half), half)] = dot(att_ref[...], ref[...])
    hidden1 = hidden_ref[...] + (x_ref[...].astype(f32) + vec_ref[0:1, :]) + vec_ref[1:2, :]
    normal, inverse = norm_parts(hidden1)
    normal_ref[...] = normal
    inverse_ref[...] = inverse
    normed_ref[...] = (normal * vec_ref[2:3, :] + vec_ref[3:4, :]).astype(bf16)


def views(refs, width):
    if len(refs) == 2:
        return refs
    return refs[0].at[:, : refs[0].shape[1] - width], refs[0].at[:, refs[0].shape[1] - width :]


def forward_kernel(count, first, rows_ref, bias_ref, *refs):
    up_ref, down_ref = views(refs[:count], rows_ref.shape[1])
    act_ref, slope_ref, feed_ref = refs[-3:]
    upward = dot(rows_ref[...], up_ref[...]) + bias_ref[...]
    lower = 0.5 + 0.5 * lax.erf(upward * math.sqrt(0.5))
    density = jnp.exp2(upward * upward * (-0.5 * LOG2E)) * (1.0 / math.sqrt(2.0 * math.pi))
    act = (upward * lower).astype(bf16)
    act_ref[...] = act
    slope_ref[...] = lower + upward * density
    feed = dot(act, down_ref[...])
    if not first:
        feed = feed + refs[count][...]
    feed_ref[...] = feed.astype(feed_ref.dtype)


def feed_forward(rows, weights, bias, feed, dtype):
    count, group_ff = rows.shape[0], bias.shape[1]
    return kernel_call(
        functools.partial(forward_kernel, len(weights), feed is None),
        [shape((count, group_ff), bf16), shape((count, group_ff)), shape(rows.shape, dtype)],
        [rows, bias, *weights] + ([] if feed is None else [feed]),
    )


def backward_kernel(count, first, rows_ref, slope_ref, *refs):
    up_ref, down_ref = views(refs[:count], rows_ref.shape[1])
    d_up_ref, sum_ref, total_ref = refs[-3:]
    d_up = (dot(rows_ref[...], down_ref[...], ((1,), (1,))) * slope_ref[...]).astype(bf16)
    d_up_ref[...] = d_up
    sum_ref[...] = column_sums(d_up.astype(f32))
    total = dot(d_up, up_ref[...], ((1,), (1,)))
    if not first:
        total = total + refs[count][...]
    total_ref[...] = total.astype(total_ref.dtype)


def feed_backward(rows, weights, slope, total, dtype):
    count, group_ff = slope.shape
    return kernel_call(
        functools.partial(backward_kernel, len(weights), total is None),
        [shape((count, group_ff), bf16), shape((8, group_ff)), shape(rows.shape, dtype)],
        [rows, slope, *weights] + ([] if total is None else [total]),
    )


def turn_kernel(
    normal_ref, feed_ref, got_ref, cot_ref, vec_ref, keep_ref, send_ref, d_hidden_ref, d_feed_ref, sum_ref
):
    normed1 = normal_ref[...] * vec_ref[2:3, :] + vec_ref[3:4, :]
    hidden2 = normed1 + (feed_ref[...] + got_ref[...].astype(f32) + vec_ref[4:5, :])
    normal, inverse = norm_parts(hidden2)
    gain = vec_ref[5:6, :]
    result = (normal * gain + vec_ref[6:7, :]).astype(bf16)
    keep_ref[...] = result[: keep_ref.shape[0]]
    send_ref[...] = result[keep_ref.shape[0] :]
    cot = cot_ref[...].astype(f32)
    d_hidden2 = norm_back(cot, normal, inverse, gain)
    d_hidden_ref[...] = d_hidden2
    d_feed = d_hidden2.astype(bf16)
    d_feed_ref[...] = d_feed
    sum_ref[...] = column_sums(cot * normal, cot, d_feed.astype(f32))


def branch_kernel(
    core_ref, d_hidden2_ref, own_ref, got_ref, normal_ref, inverse_ref, mine_ref, other_ref, vec_ref,
    d_hidden1_ref, d_branch_ref, near_ref, far_ref, sum_ref,
):
    core, half, near = core_ref[0], mine_ref.shape[1], near_ref.shape[1]
    d_normed = d_hidden2_ref[...] + (own_ref[...] + got_ref[...].astype(f32))
    normal = normal_ref[...]
    d_hidden1 = norm_back(d_normed, normal, inverse_ref[...], vec_ref[2:3, :])
    d_hidden1_ref[...] = d_hidden1
    d_branch = d_hidden1.astype(bf16)
    d_branch_ref[...] = d_branch
    first = d_branch_ref[:, pl.ds(pl.multiple_of(core * half, half), half)]
    second = d_branch_ref[:, pl.ds(pl.multiple_of((1 - core) * half, half), half)]
    for ref, start in ((far_ref, near), (near_ref, 0)):
        span = slice(start, start + ref.shape[1])
        ref[...] = (
            dot(first, mine_ref[span, :], ((1,), (1,)))
            + dot(second, other_ref[span, :], ((1,), (1,)))
        ).astype(bf16)
    sum_ref[...] = column_sums(d_normed * normal, d_normed, d_branch.astype(f32))


def grad_kernel(one_ref, two_ref, left_ref, right_ref, out_ref):
    out_ref[...] = (
        dot(one_ref[...], left_ref[...], ((0,), (0,))) + dot(two_ref[...], right_ref[...], ((0,), (0,)))
    ).astype(bf16)


def grad_split_kernel(shard, odd_ref, keep_ref, got_ref, near_ref, far_ref):
    odd = odd_ref[0]
    for parity, ref in ((1 - odd, far_ref), (odd, near_ref)):
        for j in range(ref.shape[0]):
            rows = pl.ds(pl.multiple_of((2 * j + parity) * shard, shard), shard)
            ref[j] = (keep_ref[rows, :].astype(f32) + got_ref[rows, :].astype(f32)).astype(bf16)


def add_kernel(near_ref, got_ref, out_ref):
    out_ref[...] = (near_ref[...].astype(f32) + got_ref[...].astype(f32)).astype(out_ref.dtype)


def out_grad_kernel(ctx_ref, att_ref, d_branch_ref, keep_ref, send_ref):
    ctx = ctx_ref[0]
    core = ctx_ref[1]
    group, half = ctx_ref_group(att_ref, keep_ref), keep_ref.shape[1]
    for way, ref in ((core, keep_ref), (1 - core, send_ref)):
        columns = d_branch_ref[:, pl.ds(pl.multiple_of(way * half, half), half)]
        grad = dot(att_ref[...], columns, ((0,), (0,)))
        for i in range(grad.shape[0] // group):
            start = pl.multiple_of((ctx ^ i) * group, group)
            ref[pl.ds(start, group), :] = grad[i * group : (i + 1) * group].astype(ref.dtype)


def ctx_ref_group(att_ref, keep_ref):
    return att_ref.shape[1] // lax.axis_size("ctx")


def split_kernel(bit_ref, keep_ref, got_ref, kept_ref, send_ref):
    half = kept_ref.shape[1]
    for way, ref in ((bit_ref[0], kept_ref), (1 - bit_ref[0], send_ref)):
        span = pl.ds(pl.multiple_of(way * half, half), half)
        ref[...] = (keep_ref[:, span] + got_ref[:, span].astype(f32)).astype(ref.dtype)


def pack(values):
    high = values.astype(bf16)
    return jnp.concatenate([high, (values - high.astype(f32)).astype(bf16)])


def unpack(rows):
    return rows[:VEC].astype(f32) + rows[VEC:].astype(f32)


def qkv_send_kernel(shard, r0_ref, dq_ref, dkv_ref, out_ref):
    width = dq_ref.shape[1]
    query = dot(r0_ref[...], dq_ref[...], ((0,), (0,)))
    pair = dot(r0_ref[...], dkv_ref[...], ((0,), (0,)))
    for block in range(out_ref.shape[0]):
        rows = slice(block * shard, (block + 1) * shard)
        out_ref[block, :, :width] = query[rows].astype(bf16)
        out_ref[block, :, width:] = pair[rows].astype(bf16)


def split_by_parity(shard, odd, grad_ref, got_ref, vec_ref, near_ref, far_ref):
    for parity, ref in ((1 - odd, far_ref), (odd, near_ref)):
        for j in range(ref.shape[0]):
            block = 2 * j + parity
            rows = pl.ds(pl.multiple_of(block * shard, shard), shard)
            ref[j, :shard] = (grad_ref[rows, :] + got_ref[block].astype(f32)).astype(ref.dtype)
            vec = vec_ref[block]
            ref[j, shard:] = vec if ref.dtype == f32 else pack(vec)


def qkv_keep_kernel(
    shard, odd_ref, r0_ref, dq_ref, dkv_ref, got_ref, vec_ref, near_ref, far_ref, grad_ref
):
    width = dq_ref.shape[1]
    grad_ref[:, :width] = dot(r0_ref[...], dq_ref[...], ((0,), (0,)))
    grad_ref[:, width:] = dot(r0_ref[...], dkv_ref[...], ((0,), (0,)))
    split_by_parity(shard, odd_ref[0], grad_ref, got_ref, vec_ref, near_ref, far_ref)


def qkv_vec_keep_kernel(
    shard, place_ref, r0_ref, dq_ref, dkv_ref, dq_other_ref, dkv_other_ref, got_ref, sums1_ref, sums2_ref,
    up_own_ref, up_rest_ref, up_own_other_ref, up_rest_other_ref, near_ref, far_ref, grad_ref, flat_ref,
    up_ref, vec_ref,
):
    odd, ctx = place_ref[0], place_ref[1]
    width = dq_ref.shape[1]
    size = vec_ref.shape[0]
    flat_ref[...] = jnp.zeros_like(flat_ref)
    up_ref[...] = jnp.zeros_like(up_ref)
    vec_ref[...] = jnp.zeros_like(vec_ref)
    cut = up_own_ref.shape[1] // size
    pairs = (
        (dq_ref, dkv_ref, up_own_ref, up_rest_ref),
        (dq_other_ref, dkv_other_ref, up_own_other_ref, up_rest_other_ref),
    )
    for i, (query, pair, own, rest) in enumerate(pairs):
        who = ctx ^ i
        span = pl.ds(pl.multiple_of(who * width, width), width)
        flat_ref[0:1, span] = jnp.sum(query[...].astype(f32), axis=0, keepdims=True)
        flat_ref[1:2, span] = jnp.sum(pair[:, width:].astype(f32), axis=0, keepdims=True)
        for f in range(size):
            start = pl.multiple_of((f * (up_ref.shape[1] // cut // size) + who) * cut, cut)
            here = slice(f * cut, (f + 1) * cut)
            up_ref[0:1, pl.ds(start, cut)] = own[0:1, here] + rest[0:1, here]
    full = flat_ref.shape[1]
    model = (flat_ref[0:1], flat_ref[1:2], sums1_ref[2:3], sums2_ref[2:3])
    rows = (model, (up_ref[0:1],), (sums1_ref[0:1], sums2_ref[0:1]), (sums1_ref[1:2], sums2_ref[1:2]))
    for row, sources in enumerate(rows):
        length = sources[0].shape[1]
        part = len(sources) * length // size
        for f in range(size):
            source, start = sources[f * part // length], f * part % length
            vec_ref[f, row : row + 1, :part] = source[:, start : start + part]
    grad_ref[:, :width] = dot(r0_ref[...], dq_ref[...], ((0,), (0,)))
    grad_ref[:, width:] = dot(r0_ref[...], dkv_ref[...], ((0,), (0,)))
    split_by_parity(shard, odd, grad_ref, got_ref, vec_ref, near_ref, far_ref)


def input_kernel(dq_ref, dkv_ref, dq_other_ref, dkv_other_ref, mine_ref, other_ref, own_ref, rest_ref):
    width = dq_ref.shape[1]
    cut = own_ref.shape[0]
    for ref, rows in ((rest_ref, slice(cut, dq_ref.shape[0])), (own_ref, slice(0, cut))):
        total = 0.0
        for query, pair, weights in (
            (dq_ref, dkv_ref, mine_ref), (dq_other_ref, dkv_other_ref, other_ref)
        ):
            total = total + dot(query[rows, :], weights[:, :width], ((1,), (1,)))
            total = total + dot(pair[rows, :], weights[:, width:], ((1,), (1,)))
        ref[...] = total.astype(ref.dtype)


def input_sum_kernel(one_ref, two_ref, got_ref, keep_ref, send_ref):
    total = one_ref[...] + (two_ref[...] + got_ref[...].astype(f32))
    keep_ref[...] = total[: keep_ref.shape[0]]
    send_ref[...] = total[keep_ref.shape[0] :]


def out_keep_kernel(shard, odd_ref, keep_ref, got_ref, near_ref, far_ref):
    odd = odd_ref[0]
    for parity, ref in ((1 - odd, far_ref), (odd, near_ref)):
        for j in range(ref.shape[0]):
            rows = pl.ds(pl.multiple_of((2 * j + parity) * shard, shard), shard)
            ref[j] = (keep_ref[rows, :] + got_ref[rows, :].astype(f32)).astype(ref.dtype)


def z_send_kernel(shard, z_ref, near_ref, got_ref, out_near_ref, out_got_ref, *outs):
    z = z_ref[0]
    columns = near_ref.shape[2]
    for k, ref in enumerate(outs):
        block = z ^ k
        got = got_ref[block]
        near = near_ref[block]
        ref[:shard, :columns] = (near[:shard] + got[:shard].astype(f32)).astype(ref.dtype)
        ref[:shard, columns:] = (
            out_near_ref[block] + out_got_ref[block].astype(f32)
        ).astype(ref.dtype)
        vec = near[shard:] + unpack(got[shard:])
        ref[shard:, :columns] = vec if ref.dtype == f32 else pack(vec)
        ref[shard:, columns:] = jnp.zeros_like(ref[shard:, columns:])


def z_sum_kernel(shard, mine_ref, *refs):
    gots, out_ref = refs[:-1], refs[-1]
    value, vec = mine_ref[:shard], mine_ref[shard:]
    for ref in gots:
        value = value + ref[:shard].astype(f32)
        vec = vec + unpack(ref[shard:])
    out_ref[:shard] = value.astype(bf16)
    out_ref[shard:] = pack(vec)


def tail_kernel(shard, group, ctx_ref, *refs):
    pieces, (qkv_ref, out_ref, vec_ref) = refs[:4], refs[4:]
    ctx = ctx_ref[0]
    width = 4 * group
    for i, piece in enumerate(pieces):
        who = ctx ^ i
        for third in range(3):
            start = pl.multiple_of(third * width + who * group, group)
            qkv_ref[:, pl.ds(start, group)] = piece[
                :shard, third * group : (third + 1) * group
            ].astype(f32)
        start = pl.multiple_of(((who % 2) * 2 + who // 2) * group, group)
        out_ref[:, pl.ds(start, group)] = piece[:shard, 3 * group :].astype(f32)
    vec = [unpack(piece[shard:, : 3 * group]) for piece in pieces]
    vec_ref[...] = (vec[0] + vec[1]) + (vec[2] + vec[3])


def rows_tail_kernel(rows, ctx_ref, *refs):
    pieces, out_ref = refs[:-1], refs[-1]
    for i, piece in enumerate(pieces):
        start = pl.multiple_of((ctx_ref[0] ^ i) * rows, rows)
        out_ref[pl.ds(start, rows), :] = piece[...].astype(f32)


def columns_tail_kernel(cut, ctx_ref, *refs):
    pieces, out_ref = refs[:-1], refs[-1]
    for i, piece in enumerate(pieces):
        for block in range(piece.shape[1] // cut):
            start = pl.multiple_of((block * len(pieces) + (ctx_ref[0] ^ i)) * cut, cut)
            out_ref[:, pl.ds(start, cut)] = piece[:, block * cut : (block + 1) * cut].astype(f32)


def per_device(
    inputs, timestep, doc_ids, w_qkv, w_out, w_up, w_down, bias_model, bias_up,
    norm_gains, norm_shifts, cotangent,
):
    ctx, ctx_size = lax.axis_index("ctx"), lax.axis_size("ctx")
    fsdp, fsdp_size = lax.axis_index("fsdp"), lax.axis_size("fsdp")
    core, ways = ctx % 2, ctx_size // 2
    tokens, width = inputs.shape[2], w_out.shape[1]
    hidden = w_up.shape[1]
    head_size = width // HEADS
    own_rows = 2 * tokens
    rest_rows = (ways - 1) * own_rows
    group = width // ctx_size
    columns = 3 * group
    group_ff = hidden // ctx_size
    shard = w_out.shape[0]
    shard_ff = w_down.shape[0]
    cut_ff = hidden // (fsdp_size * ctx_size)
    fsdp_range = jnp.arange(fsdp_size)
    natural = fsdp_range ^ fsdp

    small = jnp.concatenate([bias_model, bias_up, norm_gains, norm_shifts])
    small_count = small.shape[0]
    qkv_group = lax.dynamic_index_in_dim(
        w_qkv.reshape(shard, 3, ctx_size, group), ctx, 2, False
    ).reshape(shard, columns)
    small_rows = jnp.pad(small, (0, PAD * columns - small_count)).reshape(PAD, columns)
    out_send = lax.dynamic_index_in_dim(w_out.reshape(shard, 2, width // 2), core, 1, False)
    first_send = jnp.concatenate(
        [
            jnp.concatenate([qkv_group, small_rows]),
            jnp.concatenate([out_send, jnp.zeros((PAD, width // 2), bf16)]),
        ],
        axis=1,
    )
    first_pieces = gather_far(gather_near(first_send))
    up_send = lax.dynamic_index_in_dim(
        w_up.reshape(shard, fsdp_size, ctx_size, cut_ff), ctx, 2, False
    ).reshape(shard, group_ff)
    down_send = lax.dynamic_index_in_dim(
        w_down.reshape(ctx_size, shard_ff // ctx_size, width), ctx, 0, False
    )
    merged = up_send.shape == down_send.shape and ctx_size == 4 and cut_ff % 128 == 0
    feed_sends = [jnp.concatenate([up_send, down_send], axis=1)] if merged else [up_send, down_send]
    feed_mine = [lax.all_gather(send, "fsdp", axis=0, tiled=True) for send in feed_sends]

    docs = doc_ids[:, 0].astype(bf16)
    doc_rows = jnp.pad(docs[:, None, :], ((0, 0), (0, PAD - 1), (0, width - tokens)))
    mine, theirs = (
        [lax.dynamic_index_in_dim(a, c, 0, False) for a in (inputs[:, 0], doc_rows, cotangent[:, 0])]
        for c in (core, 1 - core)
    )
    swapped = over_ctx(jnp.concatenate(theirs), 1)
    x_own = jnp.concatenate([mine[0], swapped[:tokens]])
    cot_own = jnp.concatenate([mine[2], swapped[tokens + PAD :]])
    doc_own = jnp.concatenate([mine[1][:1, :tokens], swapped[tokens : tokens + 1, :tokens]], axis=1)
    packed = jnp.concatenate([x_own, jnp.pad(doc_own, ((0, PAD - 1), (0, width - own_rows)))])
    rest = gather_tokens(packed).reshape(ways - 1, own_rows + PAD, width)
    x_rest = rest[:, :own_rows].reshape(rest_rows, width)
    doc_all = jnp.concatenate([doc_own[0], rest[:, own_rows, :own_rows].reshape(-1)]).astype(f32)
    key_docs, query_docs = doc_all[:, None], doc_all[None, :]
    time_row = lax.dynamic_index_in_dim(timestep[:, 0], core, 0, True).astype(f32)
    rounded0 = (jnp.concatenate([x_own, x_rest]).astype(f32) + time_row).astype(bf16)

    ratio = fsdp_size // ctx_size
    orders = [natural] + [
        ((natural // ratio) ^ who) * ratio + natural % ratio for who in (ctx, ctx ^ 1)
    ]
    w_qkv_mine, small_all, out_mine, out_theirs = place(first_pieces, orders, shard, columns)
    w_qkv_pair = (w_qkv_mine, over_ctx(w_qkv_mine, 1))
    small_all = small_all.reshape(fsdp_size, PAD * columns)[:, :small_count].astype(f32)
    starts = [0, bias_model.shape[0]]
    starts.append(starts[1] + bias_up.shape[0])
    starts.append(starts[2] + norm_gains.shape[0])
    starts.append(small_count)
    b_model, b_up, gains, shifts = (
        small_all[:, a:b].reshape(-1) for a, b in zip(starts[:-1], starts[1:])
    )
    vecs = jnp.stack(
        [
            time_row[0], b_model[2 * width : 3 * width], gains[:width], shifts[:width],
            b_model[3 * width :], gains[width:], shifts[width:], jnp.zeros((width,), f32),
        ]
    )
    b_up_groups = b_up.reshape(fsdp_size, ctx_size, cut_ff)

    b_up_pair = [
        lax.dynamic_index_in_dim(b_up_groups, ctx ^ i, 1, False).reshape(1, group_ff)
        for i in range(2)
    ]

    projected, attended, logs = [], [], []
    for i in range(2):
        who = ctx ^ i
        b_query = lax.dynamic_slice_in_dim(b_model, who * group, group)
        b_value = lax.dynamic_slice_in_dim(b_model, width + who * group, group)
        bias = jnp.concatenate([b_query, jnp.zeros_like(b_query), b_value])
        weights = after(w_qkv_pair[i], *attended, *b_up_pair, vecs, cot_own)
        proj = (dot(rounded0, weights) + bias[None]).astype(bf16)
        out, log = attend(proj, key_docs, query_docs, head_size)
        projected.append(proj)
        attended.append(out)
        logs.append(log)
    attended_pair = jnp.concatenate(attended, axis=1)
    attended_cols = [attended_pair[:own_rows]]
    for k in range(1, ways):
        attended_cols.append(over_ctx(attended_pair[k * own_rows : (k + 1) * own_rows], 2 * k))
    attended_own = jnp.concatenate(attended_cols, axis=1)

    out_other = over_ctx(out_theirs, 1)
    normal1, inverse1, normed_own = kernel_call(
        out_kernel,
        [shape((own_rows, width)), shape((own_rows, 1)), shape((own_rows, width), bf16)],
        [attended_own, out_mine, out_other, x_own, vecs],
        scalars=[core],
        scratch=[pltpu.VMEM((own_rows, width), f32)],
    )
    normed_rest = gather_tokens(normed_own)

    feed_mine = [after(w, normed_rest) for w in feed_mine]
    feed_pair = (feed_mine, [over_ctx(w, 1) for w in feed_mine])
    acts, slopes, feeds = {}, {}, {"rest": None, "own": None}
    token = normed_own
    for part, i in (("own", 0), ("rest", 0), ("rest", 1), ("own", 1)):
        rows = normed_own if part == "own" else normed_rest
        acts[part, i], slopes[part, i], feeds[part] = feed_forward(
            after(rows, token), feed_pair[i], b_up_pair[i], feeds[part],
            bf16 if i == 1 and part == "rest" else f32,
        )
        token = acts[part, i]
    feed_own, feed_got = reduce_tokens(feeds["own"], feeds["rest"])

    result_keep, result_send, d_hidden2, d_feed_own, sums2 = kernel_call(
        turn_kernel,
        [
            shape((tokens, width), bf16), shape((tokens, width), bf16), shape((own_rows, width)),
            shape((own_rows, width), bf16), shape((8, width)),
        ],
        [normal1, feed_own, feed_got, cot_own, vecs],
    )
    d_feed_rest = gather_tokens(d_feed_own)

    def gradient(args, flops=50_000_000_000):
        return kernel_call(grad_kernel, [shape((width, width), bf16)], args, flops=flops)[0]

    def split(kept, got):
        return kernel_call(
            functools.partial(grad_split_kernel, shard),
            [shape((fsdp_size // 2, shard, width), bf16)] * 2,
            [kept, got],
            scalars=[fsdp % 2],
        )

    sides = [[2 * k + p for k in range(fsdp_size // 2)] for p in range(2)]

    def finish(near, got):
        mixed = kernel_call(add_kernel, [shape(near.shape, bf16)], [near, got])[0]
        return mixed, lax.psum_scatter(
            mixed.reshape(-1, width), "fsdp", scatter_dimension=0, tiled=True,
            axis_index_groups=sides,
        )

    d_ups, d_up_sums, d_normed = {}, {}, {}
    token = d_feed_own
    for part, rows in (("own", d_feed_own), ("rest", d_feed_rest)):
        total = None
        if merged and part == "rest":
            down_args = [
                [acts["own", i], acts["rest", i], after(d_feed_own, token), d_feed_rest] for i in range(2)
            ]
            down_away = gradient(down_args[1])
            token = down_away
        for i in range(2):
            d_ups[part, i], d_up_sums[part, i], total = feed_backward(
                after(rows, token), feed_pair[i], slopes[part, i], total,
                bf16 if i == 1 and part == "rest" else f32,
            )
            token = d_ups[part, i]
        d_normed[part] = total
    dn_own, dn_got = reduce_tokens(d_normed["own"], d_normed["rest"])

    if merged:
        down_args[0][2] = after(d_feed_own, token)
        down_near, down_far = split(gradient(down_args[0]), over_ctx(down_away, 1))
        up_args = [
            [after(normed_own, down_far), normed_rest, d_ups["own", i], d_ups["rest", i]] for i in range(2)
        ]
        up_away = gradient(up_args[1], 0)
        up_near, up_far = split(gradient(up_args[0], 0), over_ctx(up_away, 1))
        dn_got = after(dn_got, up_far)
        down_got = over_fsdp(down_far, 1)
    else:
        totals = []
        for left, right in ((acts, None), (None, d_ups)):
            grads = []
            for i in range(2):
                one = jnp.concatenate([left["own", i], left["rest", i]]) if left else (
                    jnp.concatenate([normed_own, normed_rest])
                )
                two = jnp.concatenate([right["own", i], right["rest", i]]) if right else (
                    jnp.concatenate([d_feed_own, d_feed_rest])
                )
                grads.append(dot(one, two, ((0,), (0,))))
            mixed = (grads[0] + over_ctx(grads[1].astype(bf16), 1).astype(f32)).astype(bf16)
            totals.append(lax.psum_scatter(mixed, "fsdp", scatter_dimension=0, tiled=True))

    d_hidden1, d_branch, d_att_near, d_att_far, sums1 = kernel_call(
        branch_kernel,
        [
            shape((own_rows, width)), shape((own_rows, width), bf16),
            shape((own_rows, 2 * group), bf16), shape((own_rows, width - 2 * group), bf16),
            shape((8, width)),
        ],
        [d_hidden2, dn_own, dn_got, normal1, inverse1, out_mine, out_other, vecs],
        scalars=[core],
        flops=0,
    )
    if ways == 2:
        d_attended = [d_att_near, over_ctx(d_att_far, 2)]
    else:
        d_attended = [d_att_near] + [
            over_ctx(d_att_far[:, 2 * (k - 1) * group : 2 * k * group], 2 * k)
            for k in range(1, ways)
        ]

    d_projected = [None, None]
    for i in (1, 0):
        d_query, d_pair = attend_back(
            projected[i], d_attended, i * group, key_docs, query_docs, logs[i], head_size,
        )
        d_projected[i] = (d_query, d_pair)
        if i:
            qkv_away = kernel_call(
                functools.partial(qkv_send_kernel, shard),
                [shape((fsdp_size, shard, columns), bf16)],
                [rounded0, *d_projected[1]],
            )[0]
            token = qkv_away
            if merged:
                down_mixed, down_total = finish(down_near, after(down_got, qkv_away))
                up_got = over_fsdp(after(up_far, down_mixed), 1)
                token = down_mixed
            out_keep, out_away = kernel_call(
                out_grad_kernel,
                [shape((width, width // 2)), shape((width, width // 2), bf16)],
                [after(attended_own, token), d_branch],
                scalars=[jnp.stack([ctx, core])],
            )
            out_got = over_ctx(out_away, 1)
            for k in range(int(math.log2(ways))):
                half = out_keep.shape[1] // 2
                bit = (ctx >> (k + 1)) % 2
                if half % 128 == 0:
                    out_keep, out_away = kernel_call(
                        split_kernel, [shape((width, half)), shape((width, half), bf16)],
                        [out_keep, out_got], scalars=[bit],
                    )
                else:
                    both = (out_keep + out_got.astype(f32)).reshape(width, 2, half)
                    out_keep = lax.dynamic_index_in_dim(both, bit, 1, False)
                    out_away = lax.dynamic_index_in_dim(both, 1 - bit, 1, False).astype(bf16)
                out_got = over_ctx(out_away, 2 << k)
            d_attended[0] = after(d_attended[0], out_away)

    qkv_got = over_ctx(qkv_away, 1)
    keep_outs = [
        shape((fsdp_size // 2, shard + VEC, columns)),
        shape((fsdp_size // 2, shard + PAD, columns), bf16),
    ]
    quarter = out_keep.shape[1]
    if merged:
        near, far = kernel_call(
            functools.partial(qkv_vec_keep_kernel, shard),
            keep_outs,
            [
                rounded0, *d_projected[0], *d_projected[1], qkv_got, sums1, sums2,
                *(d_up_sums[part, i] for i in range(2) for part in ("own", "rest")),
            ],
            scalars=[jnp.stack([fsdp % 2, ctx])],
            scratch=[
                pltpu.VMEM((width, columns), f32), pltpu.VMEM((8, width), f32),
                pltpu.VMEM((8, hidden), f32), pltpu.VMEM((fsdp_size, VEC, columns), f32),
            ],
        )
    else:
        def in_groups(pair, size):
            stacked = jnp.stack(pair)
            ordered = jnp.where(core == 0, stacked, stacked[::-1])
            return lax.dynamic_update_slice_in_dim(
                jnp.zeros((ctx_size, size), f32), ordered, ctx - core, 0
            )

        column = lambda value: jnp.sum(value.astype(f32), axis=0)
        vec_query = in_groups([column(d[0]) for d in d_projected], group).reshape(-1)
        vec_value = in_groups([column(d[1][:, group:]) for d in d_projected], group).reshape(-1)
        vec_up = jnp.swapaxes(
            in_groups(
                [d_up_sums["own", i][0] + d_up_sums["rest", i][0] for i in range(2)], group_ff
            ).reshape(ctx_size, fsdp_size, cut_ff), 0, 1,
        ).reshape(fsdp_size, -1)
        vec_model = jnp.concatenate([vec_query, vec_value, sums1[2], sums2[2]]).reshape(fsdp_size, -1)
        vec_gain = jnp.concatenate([sums1[0], sums2[0]]).reshape(fsdp_size, -1)
        vec_shift = jnp.concatenate([sums1[1], sums2[1]]).reshape(fsdp_size, -1)
        vectors = jnp.concatenate([vec_model, vec_up, vec_gain, vec_shift], axis=1)
        vectors = jnp.pad(vectors, ((0, 0), (0, VEC * columns - small_count))).reshape(
            fsdp_size, VEC, columns
        )
        near, far = kernel_call(
            functools.partial(qkv_keep_kernel, shard),
            keep_outs,
            [rounded0, *d_projected[0], qkv_got, vectors],
            scalars=[fsdp % 2],
            scratch=[pltpu.VMEM((width, columns), f32)],
        )
    got = over_fsdp(far, 1)
    if merged:
        up_mixed, up_total = finish(up_near, after(up_got, far))
    out_near, out_far = kernel_call(
        functools.partial(out_keep_kernel, shard),
        [
            shape((fsdp_size // 2, shard, quarter)),
            shape((fsdp_size // 2, shard, quarter), bf16),
        ],
        [after(out_keep, far), out_got],
        scalars=[fsdp % 2],
    )
    out_cross = over_fsdp(out_far, 1)

    dx_own, dx_rest = kernel_call(
        input_kernel,
        [shape((own_rows, width)), shape((rest_rows, width), bf16)],
        [after(d_projected[0][0], out_far, got), d_projected[0][1], *d_projected[1], *w_qkv_pair],
    )
    if merged:
        got = after(got, up_mixed)
    sends = kernel_call(
        functools.partial(z_send_kernel, shard),
        [shape((shard + VEC, columns + quarter))]
        + [shape((shard + PAD, columns + quarter), bf16)] * (fsdp_size // 2 - 1),
        [near, got, out_near, out_cross],
        scalars=[fsdp // 2],
    )
    mine_block = sends[0]
    total = kernel_call(
        functools.partial(z_sum_kernel, shard),
        [shape((shard + PAD, columns + quarter), bf16)],
        [mine_block, *(over_fsdp(value, 2 * k) for k, value in enumerate(sends[1:], 1))],
    )[0]

    dx_own, dx_got = reduce_tokens(dx_own, dx_rest)
    input_keep, input_send = kernel_call(
        input_sum_kernel, [shape((tokens, width))] * 2, [d_hidden1, dx_own, dx_got]
    )

    if merged:
        def quarters(own, direct=False):
            if direct:
                return [own] + [over_ctx(own, i) for i in range(1, 4)]
            far_own = over_ctx(own, 2)
            other = over_ctx(jnp.concatenate([own, far_own]), 1)
            return [own, other[: own.shape[0]], far_own, other[own.shape[0] :]]

        grad_down = kernel_call(
            functools.partial(rows_tail_kernel, shard),
            [shape((shard_ff, width))],
            quarters(after(down_total, up_mixed)),
            scalars=[ctx],
        )[0]
        grad_up = kernel_call(
            functools.partial(columns_tail_kernel, cut_ff),
            [shape((shard, hidden))],
            quarters(up_total),
            scalars=[ctx],
        )[0]
        grad_qkv, grad_out, vec_done = kernel_call(
            functools.partial(tail_kernel, shard, group),
            [shape((shard, 3 * width)), shape((shard, width)), shape((VEC, columns))],
            quarters(total, direct=True),
            scalars=[ctx],
        )
        counts = [b - a for a, b in zip(starts[:-1], starts[1:])]
        vectors = [vec_done[row, :count] for row, count in enumerate(counts)]
    else:
        spread = lambda own: lax.all_gather(own, "ctx", axis=0)
        tail = spread(total)
        grad_qkv = jnp.transpose(
            tail[:, :shard, :columns].reshape(ctx_size, shard, 3, group), (1, 2, 0, 3)
        ).reshape(shard, 3 * width).astype(f32)
        order = []
        levels = int(math.log2(ctx_size))
        for place_index in range(ctx_size):
            order.append(
                sum(((place_index >> (levels - 1 - b)) & 1) << b for b in range(levels))
            )
        grad_out = jnp.concatenate([tail[d, :shard, columns:] for d in order], axis=1).astype(f32)
        vec = tail[:, shard:, :columns].astype(f32)
        vec_done = jnp.sum(vec[:, :VEC] + vec[:, VEC:], axis=0).reshape(-1)
        vectors = [vec_done[a:b] for a, b in zip(starts[:-1], starts[1:])]
        grad_down = spread(totals[0]).reshape(shard_ff, width).astype(f32)
        grad_up = jnp.transpose(
            spread(totals[1]).reshape(ctx_size, shard, fsdp_size, cut_ff), (1, 2, 0, 3)
        ).reshape(shard, hidden).astype(f32)

    def give_back(keep, send):
        got = over_ctx(send, 1)
        return jnp.stack([jnp.where(core == 0, keep, got), jnp.where(core == 0, got, keep)])

    block_output = give_back(result_keep, result_send)[:, None]
    input_grad = give_back(input_keep, input_send)[:, None]
    return (
        block_output, input_grad, grad_qkv, grad_out, grad_up, grad_down,
        *vectors,
    )


def solution(mesh):
    token = P(None, "fsdp", "ctx", None)
    rows = P("fsdp", None)
    flat = P("fsdp")
    return jax.shard_map(
        per_device,
        mesh=mesh,
        in_specs=(
            token, P(None, "fsdp", None), P(None, "fsdp", "ctx"), rows, rows, rows, rows,
            flat, flat, flat, flat, token,
        ),
        out_specs=(token, token, rows, rows, rows, rows, flat, flat, flat, flat),
        check_vma=False,
    )
```

```python
import functools
import math

import jax
import jax.numpy as jnp
from jax import lax
from jax.experimental import pallas as pl
from jax.experimental.pallas import tpu as pltpu
from jax.sharding import PartitionSpec as P

HEADS = 16
EPS = 1e-05
LOG2E = math.log2(math.e)
VEC = 8
PAD = 2 * VEC
f32 = jnp.float32
bf16 = jnp.bfloat16


def dot(left, right, dims=((1,), (0,))):
    return lax.dot_general(left, right, (dims, ((), ())), preferred_element_type=f32)


def over_ctx(value, mask):
    size = lax.axis_size("ctx")
    return lax.ppermute(value, "ctx", [(i, i ^ mask) for i in range(size)])


def over_fsdp(value, mask):
    size = lax.axis_size("fsdp")
    return lax.ppermute(value, "fsdp", [(i, i ^ mask) for i in range(size)])


def after(value, *others):
    return lax.optimization_barrier((value, *others))[0]


def shape(dims, dtype=f32):
    return jax.ShapeDtypeStruct(tuple(dims), dtype)


def kernel_call(body, outs, args, scalars=(), scratch=(), flops=50_000_000_000):
    scalars = [jnp.asarray(s, jnp.int32).reshape(-1) for s in scalars]
    specs = [pl.BlockSpec(memory_space=pltpu.SMEM)] * len(scalars)
    specs += [pl.BlockSpec(memory_space=pltpu.VMEM)] * len(args)
    largest = max(math.prod(a.shape) * 4 for a in [*args, *outs])
    held = sum(math.prod(a.shape) * jnp.dtype(a.dtype).itemsize for a in scratch)
    limit = min(held + max(6 * 2**20, 2 * largest), 56 * 2**20)
    return pl.pallas_call(
        body,
        in_specs=specs,
        out_specs=[pl.BlockSpec(memory_space=pltpu.VMEM)] * len(outs),
        out_shape=list(outs),
        scratch_shapes=list(scratch),
        compiler_params=pltpu.CompilerParams(vmem_limit_bytes=limit),
        cost_estimate=pl.CostEstimate(flops=flops, bytes_accessed=1024, transcendentals=0),
    )(*scalars, *args)


def attend_kernel(head_size, scale, block_ref, whole_ref, key_doc_ref, query_doc_ref, out_ref, log_ref):
    width = out_ref.shape[1]
    same = key_doc_ref[...] == query_doc_ref[...]
    for head in range(width // head_size):
        cut = head * head_size
        query = block_ref[:, cut : cut + head_size]
        key = whole_ref[:, width + cut : width + cut + head_size]
        value = whole_ref[:, 2 * width + cut : 2 * width + cut + head_size]
        scores = jnp.where(same, dot(key, query, ((1,), (1,))), -1e30)
        top = jnp.max(scores, axis=0, keepdims=True)
        expo = jnp.exp2((scores - top) * (scale * LOG2E))
        total = jnp.sum(expo, axis=0, keepdims=True)
        probs = (expo * (1.0 / total)).astype(bf16)
        out_ref[:, cut : cut + head_size] = dot(value, probs, ((0,), (0,))).T.astype(bf16)
        log_ref[head : head + 1, :] = top * (scale * LOG2E) + jnp.log2(total)


def attend(projected, key_docs, query_docs, head_size):
    length, width = projected.shape[0], projected.shape[1] // 3
    heads = width // head_size
    block = min(512, length)
    return pl.pallas_call(
        functools.partial(attend_kernel, head_size, 1.0 / math.sqrt(head_size)),
        grid=(length // block,),
        in_specs=[
            pl.BlockSpec((block, 3 * width), lambda i: (i, 0)),
            pl.BlockSpec((length, 3 * width), lambda i: (0, 0)),
            pl.BlockSpec((length, 1), lambda i: (0, 0)),
            pl.BlockSpec((1, block), lambda i: (0, i)),
        ],
        out_specs=[
            pl.BlockSpec((block, width), lambda i: (i, 0)),
            pl.BlockSpec((heads, block), lambda i: (0, i)),
        ],
        out_shape=[shape((length, width), bf16), shape((heads, length))],
        compiler_params=pltpu.CompilerParams(vmem_limit_bytes=(24 if length <= 512 else 48) * 2**20),
        cost_estimate=pl.CostEstimate(
            flops=0, bytes_accessed=1024, transcendentals=0,
        ),
    )(projected, projected, key_docs, query_docs)


def attend_back_kernel(head_size, scale, steps, first, pieces, *refs):
    block_ref, whole_ref, key_doc_ref, query_doc_ref, log_ref = refs[:5]
    grad_refs, (query_out, pair_out, pair_sum) = refs[5 : 5 + pieces], refs[5 + pieces :]
    width = query_out.shape[1]
    step = pl.program_id(0)
    same = key_doc_ref[...] == query_doc_ref[...]

    if steps > 1:
        @pl.when(step == 0)
        def _():
            pair_sum[...] = jnp.zeros_like(pair_sum)

    def add(place, value):
        if steps > 1:
            pair_sum[:, place : place + head_size] += value
        else:
            pair_out[:, place : place + head_size] = value.astype(bf16)

    for head in range(width // head_size):
        cut = head * head_size
        query = block_ref[:, cut : cut + head_size]
        key = whole_ref[:, width + cut : width + cut + head_size]
        value = whole_ref[:, 2 * width + cut : 2 * width + cut + head_size]
        span = slice(first + cut, first + cut + head_size)
        grad = jnp.concatenate([ref[:, span] for ref in grad_refs]) if pieces > 1 else grad_refs[0][:, span]
        scores = dot(key, query, ((1,), (1,)))
        probs = jnp.where(
            same, jnp.exp2(scores * (scale * LOG2E) - log_ref[head : head + 1, :]), 0.0
        )
        d_probs = dot(value, grad, ((1,), (1,)))
        inner = jnp.sum(probs * d_probs, axis=0, keepdims=True)
        d_scores = (probs * (d_probs - inner)).astype(bf16)
        query_out[:, cut : cut + head_size] = (
            dot(key, d_scores, ((0,), (0,))).T * scale
        ).astype(bf16)
        add(cut, dot(d_scores, query) * scale)
        add(width + cut, dot(probs.astype(bf16), grad))

    if steps > 1:
        @pl.when(step == steps - 1)
        def _():
            pair_out[...] = pair_sum[...].astype(bf16)


def attend_back(projected, grads, first, key_docs, query_docs, logs, head_size):
    length, width = projected.shape[0], projected.shape[1] // 3
    heads = width // head_size
    block = min(512, length)
    steps = length // block
    if steps > 1:
        grads = [jnp.concatenate(grads)]
    grad_rows = [grad.shape[0] // steps for grad in grads]
    return pl.pallas_call(
        functools.partial(
            attend_back_kernel, head_size, 1.0 / math.sqrt(head_size), steps, first, len(grads)
        ),
        grid=(steps,),
        in_specs=[
            pl.BlockSpec((block, 3 * width), lambda i: (i, 0)),
            pl.BlockSpec((length, 3 * width), lambda i: (0, 0)),
            pl.BlockSpec((length, 1), lambda i: (0, 0)),
            pl.BlockSpec((1, block), lambda i: (0, i)),
            pl.BlockSpec((heads, block), lambda i: (0, i)),
        ]
        + [pl.BlockSpec((rows, grads[0].shape[1]), lambda i: (i, 0)) for rows in grad_rows],
        out_specs=[
            pl.BlockSpec((block, width), lambda i: (i, 0)),
            pl.BlockSpec((length, 2 * width), lambda i: (0, 0)),
        ],
        out_shape=[shape((length, width), bf16), shape((length, 2 * width), bf16)],
        scratch_shapes=[pltpu.VMEM((length if steps > 1 else 8, 2 * width), f32)],
        compiler_params=pltpu.CompilerParams(vmem_limit_bytes=(24 if length <= 512 else 56) * 2**20),
        cost_estimate=pl.CostEstimate(flops=0, bytes_accessed=1024, transcendentals=0),
    )(projected, projected, key_docs, query_docs, logs, *grads)


def place_kernel(count, rows, columns, where_ref, *refs):
    pieces, (qkv_ref, small_ref, mine_ref, theirs_ref) = refs[:count], refs[count:]
    for j, piece in enumerate(pieces):
        spare = piece.shape[0] - rows
        start = pl.multiple_of(where_ref[j] * rows, rows)
        qkv_ref[pl.ds(start, rows), :] = piece[:rows, :columns]
        start = pl.multiple_of(where_ref[j] * spare, spare)
        small_ref[pl.ds(start, spare), :] = piece[rows:, :columns]
        for way, ref in enumerate((mine_ref, theirs_ref), 1):
            start = pl.multiple_of(where_ref[way * count + j] * rows, rows)
            ref[pl.ds(start, rows), :] = piece[:rows, columns:]


def place(pieces, orders, rows, columns):
    count, spare = len(pieces), pieces[0].shape[0] - rows
    rest = pieces[0].shape[1] - columns
    return kernel_call(
        functools.partial(place_kernel, count, rows, columns),
        [
            shape((count * rows, columns), bf16), shape((count * spare, columns), bf16),
            shape((count * rows, rest), bf16), shape((count * rows, rest), bf16),
        ],
        pieces,
        scalars=[jnp.concatenate(orders)],
    )


def gather_near(shard):
    size = lax.axis_size("fsdp")
    return [shard] + [over_fsdp(shard, 2 * k) for k in range(1, size // 2)]


def gather_far(near):
    pieces = []
    for value in near:
        pieces += [value, over_fsdp(value, 1)]
    return pieces


def gather_tokens(own):
    have, mask = own, 1
    while 2 * mask < lax.axis_size("ctx"):
        got = over_ctx(have, 2 * mask)
        if lax.axis_size("ctx") == 4:
            return got
        have = jnp.concatenate([have, got])
        mask *= 2
    return have[own.shape[0] :]


def reduce_tokens(own, rest):
    ways = lax.axis_size("ctx") // 2
    if ways == 2:
        return own, over_ctx(rest, 2)
    have, mask = jnp.concatenate([own, rest.astype(f32)]), ways // 2
    while mask > 1:
        half = have.shape[0] // 2
        have = have[:half] + over_ctx(have[half:].astype(bf16), 2 * mask).astype(f32)
        mask //= 2
    half = have.shape[0] // 2
    return have[:half], over_ctx(have[half:].astype(bf16), 2)


def norm_parts(value):
    centred = value - jnp.mean(value, axis=-1, keepdims=True)
    inverse = lax.rsqrt(jnp.mean(centred * centred, axis=-1, keepdims=True) + EPS)
    return centred * inverse, inverse


def norm_back(grad, normal, inverse, gain):
    inner = grad * gain
    return inverse * (
        inner
        - jnp.mean(inner, axis=-1, keepdims=True)
        - normal * jnp.mean(inner * normal, axis=-1, keepdims=True)
    )


def column_sums(*values):
    rows = [jnp.sum(value, axis=0, keepdims=True) for value in values]
    return jnp.concatenate(rows + [jnp.zeros_like(rows[0])] * (8 - len(rows)))


def out_kernel(
    core_ref, att_ref, mine_ref, other_ref, x_ref, vec_ref, normal_ref, inverse_ref, normed_ref, hidden_ref
):
    half = mine_ref.shape[1]
    core = core_ref[0]
    for way, ref in ((core, mine_ref), (1 - core, other_ref)):
        hidden_ref[:, pl.ds(pl.multiple_of(way * half, half), half)] = dot(att_ref[...], ref[...])
    hidden1 = hidden_ref[...] + (x_ref[...].astype(f32) + vec_ref[0:1, :]) + vec_ref[1:2, :]
    normal, inverse = norm_parts(hidden1)
    normal_ref[...] = normal
    inverse_ref[...] = inverse
    normed_ref[...] = (normal * vec_ref[2:3, :] + vec_ref[3:4, :]).astype(bf16)


def views(refs, width):
    if len(refs) == 2:
        return refs
    return refs[0].at[:, : refs[0].shape[1] - width], refs[0].at[:, refs[0].shape[1] - width :]


def forward_kernel(count, first, rows_ref, bias_ref, *refs):
    up_ref, down_ref = views(refs[:count], rows_ref.shape[1])
    act_ref, slope_ref, feed_ref = refs[-3:]
    upward = dot(rows_ref[...], up_ref[...]) + bias_ref[...]
    lower = 0.5 + 0.5 * lax.erf(upward * math.sqrt(0.5))
    density = jnp.exp2(upward * upward * (-0.5 * LOG2E)) * (1.0 / math.sqrt(2.0 * math.pi))
    act = (upward * lower).astype(bf16)
    act_ref[...] = act
    slope_ref[...] = lower + upward * density
    feed = dot(act, down_ref[...])
    if not first:
        feed = feed + refs[count][...]
    feed_ref[...] = feed.astype(feed_ref.dtype)


def feed_forward(rows, weights, bias, feed, dtype):
    count, group_ff = rows.shape[0], bias.shape[1]
    return kernel_call(
        functools.partial(forward_kernel, len(weights), feed is None),
        [shape((count, group_ff), bf16), shape((count, group_ff)), shape(rows.shape, dtype)],
        [rows, bias, *weights] + ([] if feed is None else [feed]),
    )


def backward_kernel(count, first, rows_ref, slope_ref, *refs):
    up_ref, down_ref = views(refs[:count], rows_ref.shape[1])
    d_up_ref, sum_ref, total_ref = refs[-3:]
    d_up = (dot(rows_ref[...], down_ref[...], ((1,), (1,))) * slope_ref[...]).astype(bf16)
    d_up_ref[...] = d_up
    sum_ref[...] = column_sums(d_up.astype(f32))
    total = dot(d_up, up_ref[...], ((1,), (1,)))
    if not first:
        total = total + refs[count][...]
    total_ref[...] = total.astype(total_ref.dtype)


def feed_backward(rows, weights, slope, total, dtype):
    count, group_ff = slope.shape
    return kernel_call(
        functools.partial(backward_kernel, len(weights), total is None),
        [shape((count, group_ff), bf16), shape((8, group_ff)), shape(rows.shape, dtype)],
        [rows, slope, *weights] + ([] if total is None else [total]),
    )


def turn_kernel(
    normal_ref, feed_ref, got_ref, cot_ref, vec_ref, keep_ref, send_ref, d_hidden_ref, d_feed_ref, sum_ref
):
    normed1 = normal_ref[...] * vec_ref[2:3, :] + vec_ref[3:4, :]
    hidden2 = normed1 + (feed_ref[...] + got_ref[...].astype(f32) + vec_ref[4:5, :])
    normal, inverse = norm_parts(hidden2)
    gain = vec_ref[5:6, :]
    result = (normal * gain + vec_ref[6:7, :]).astype(bf16)
    keep_ref[...] = result[: keep_ref.shape[0]]
    send_ref[...] = result[keep_ref.shape[0] :]
    cot = cot_ref[...].astype(f32)
    d_hidden2 = norm_back(cot, normal, inverse, gain)
    d_hidden_ref[...] = d_hidden2
    d_feed = d_hidden2.astype(bf16)
    d_feed_ref[...] = d_feed
    sum_ref[...] = column_sums(cot * normal, cot, d_feed.astype(f32))


def branch_kernel(
    core_ref, d_hidden2_ref, own_ref, got_ref, normal_ref, inverse_ref, mine_ref, other_ref, vec_ref,
    d_hidden1_ref, d_branch_ref, near_ref, far_ref, sum_ref,
):
    core, half, near = core_ref[0], mine_ref.shape[1], near_ref.shape[1]
    d_normed = d_hidden2_ref[...] + (own_ref[...] + got_ref[...].astype(f32))
    normal = normal_ref[...]
    d_hidden1 = norm_back(d_normed, normal, inverse_ref[...], vec_ref[2:3, :])
    d_hidden1_ref[...] = d_hidden1
    d_branch = d_hidden1.astype(bf16)
    d_branch_ref[...] = d_branch
    first = d_branch_ref[:, pl.ds(pl.multiple_of(core * half, half), half)]
    second = d_branch_ref[:, pl.ds(pl.multiple_of((1 - core) * half, half), half)]
    for ref, start in ((far_ref, near), (near_ref, 0)):
        span = slice(start, start + ref.shape[1])
        ref[...] = (
            dot(first, mine_ref[span, :], ((1,), (1,)))
            + dot(second, other_ref[span, :], ((1,), (1,)))
        ).astype(bf16)
    sum_ref[...] = column_sums(d_normed * normal, d_normed, d_branch.astype(f32))


def grad_kernel(one_ref, two_ref, left_ref, right_ref, out_ref):
    out_ref[...] = (
        dot(one_ref[...], left_ref[...], ((0,), (0,))) + dot(two_ref[...], right_ref[...], ((0,), (0,)))
    ).astype(bf16)


def grad_split_kernel(shard, odd_ref, keep_ref, got_ref, near_ref, far_ref):
    odd = odd_ref[0]
    for parity, ref in ((1 - odd, far_ref), (odd, near_ref)):
        for j in range(ref.shape[0]):
            rows = pl.ds(pl.multiple_of((2 * j + parity) * shard, shard), shard)
            ref[j] = (keep_ref[rows, :].astype(f32) + got_ref[rows, :].astype(f32)).astype(bf16)


def add_kernel(near_ref, got_ref, out_ref):
    out_ref[...] = (near_ref[...].astype(f32) + got_ref[...].astype(f32)).astype(out_ref.dtype)


def out_grad_kernel(ctx_ref, att_ref, d_branch_ref, keep_ref, send_ref):
    ctx = ctx_ref[0]
    core = ctx_ref[1]
    group, half = ctx_ref_group(att_ref, keep_ref), keep_ref.shape[1]
    for way, ref in ((core, keep_ref), (1 - core, send_ref)):
        columns = d_branch_ref[:, pl.ds(pl.multiple_of(way * half, half), half)]
        grad = dot(att_ref[...], columns, ((0,), (0,)))
        for i in range(grad.shape[0] // group):
            start = pl.multiple_of((ctx ^ i) * group, group)
            ref[pl.ds(start, group), :] = grad[i * group : (i + 1) * group].astype(ref.dtype)


def ctx_ref_group(att_ref, keep_ref):
    return att_ref.shape[1] // lax.axis_size("ctx")


def split_kernel(bit_ref, keep_ref, got_ref, kept_ref, send_ref):
    half = kept_ref.shape[1]
    for way, ref in ((bit_ref[0], kept_ref), (1 - bit_ref[0], send_ref)):
        span = pl.ds(pl.multiple_of(way * half, half), half)
        ref[...] = (keep_ref[:, span] + got_ref[:, span].astype(f32)).astype(ref.dtype)


def pack(values):
    high = values.astype(bf16)
    return jnp.concatenate([high, (values - high.astype(f32)).astype(bf16)])


def unpack(rows):
    return rows[:VEC].astype(f32) + rows[VEC:].astype(f32)


def qkv_send_kernel(shard, r0_ref, dq_ref, dkv_ref, out_ref):
    width = dq_ref.shape[1]
    query = dot(r0_ref[...], dq_ref[...], ((0,), (0,)))
    pair = dot(r0_ref[...], dkv_ref[...], ((0,), (0,)))
    for block in range(out_ref.shape[0]):
        rows = slice(block * shard, (block + 1) * shard)
        out_ref[block, :, :width] = query[rows].astype(bf16)
        out_ref[block, :, width:] = pair[rows].astype(bf16)


def split_by_parity(shard, odd, grad_ref, got_ref, vec_ref, near_ref, far_ref):
    for parity, ref in ((1 - odd, far_ref), (odd, near_ref)):
        for j in range(ref.shape[0]):
            block = 2 * j + parity
            rows = pl.ds(pl.multiple_of(block * shard, shard), shard)
            ref[j, :shard] = (grad_ref[rows, :] + got_ref[block].astype(f32)).astype(ref.dtype)
            vec = vec_ref[block]
            ref[j, shard:] = vec if ref.dtype == f32 else pack(vec)


def qkv_keep_kernel(
    shard, odd_ref, r0_ref, dq_ref, dkv_ref, got_ref, vec_ref, near_ref, far_ref, grad_ref
):
    width = dq_ref.shape[1]
    grad_ref[:, :width] = dot(r0_ref[...], dq_ref[...], ((0,), (0,)))
    grad_ref[:, width:] = dot(r0_ref[...], dkv_ref[...], ((0,), (0,)))
    split_by_parity(shard, odd_ref[0], grad_ref, got_ref, vec_ref, near_ref, far_ref)


def qkv_vec_keep_kernel(
    shard, place_ref, r0_ref, dq_ref, dkv_ref, dq_other_ref, dkv_other_ref, got_ref, sums1_ref, sums2_ref,
    up_own_ref, up_rest_ref, up_own_other_ref, up_rest_other_ref, near_ref, far_ref, grad_ref, flat_ref,
    up_ref, vec_ref,
):
    odd, ctx = place_ref[0], place_ref[1]
    width = dq_ref.shape[1]
    size = vec_ref.shape[0]
    flat_ref[...] = jnp.zeros_like(flat_ref)
    up_ref[...] = jnp.zeros_like(up_ref)
    vec_ref[...] = jnp.zeros_like(vec_ref)
    cut = up_own_ref.shape[1] // size
    pairs = (
        (dq_ref, dkv_ref, up_own_ref, up_rest_ref),
        (dq_other_ref, dkv_other_ref, up_own_other_ref, up_rest_other_ref),
    )
    for i, (query, pair, own, rest) in enumerate(pairs):
        who = ctx ^ i
        span = pl.ds(pl.multiple_of(who * width, width), width)
        flat_ref[0:1, span] = jnp.sum(query[...].astype(f32), axis=0, keepdims=True)
        flat_ref[1:2, span] = jnp.sum(pair[:, width:].astype(f32), axis=0, keepdims=True)
        for f in range(size):
            start = pl.multiple_of((f * (up_ref.shape[1] // cut // size) + who) * cut, cut)
            here = slice(f * cut, (f + 1) * cut)
            up_ref[0:1, pl.ds(start, cut)] = own[0:1, here] + rest[0:1, here]
    full = flat_ref.shape[1]
    model = (flat_ref[0:1], flat_ref[1:2], sums1_ref[2:3], sums2_ref[2:3])
    rows = (model, (up_ref[0:1],), (sums1_ref[0:1], sums2_ref[0:1]), (sums1_ref[1:2], sums2_ref[1:2]))
    for row, sources in enumerate(rows):
        length = sources[0].shape[1]
        part = len(sources) * length // size
        for f in range(size):
            source, start = sources[f * part // length], f * part % length
            vec_ref[f, row : row + 1, :part] = source[:, start : start + part]
    grad_ref[:, :width] = dot(r0_ref[...], dq_ref[...], ((0,), (0,)))
    grad_ref[:, width:] = dot(r0_ref[...], dkv_ref[...], ((0,), (0,)))
    split_by_parity(shard, odd, grad_ref, got_ref, vec_ref, near_ref, far_ref)


def input_kernel(dq_ref, dkv_ref, dq_other_ref, dkv_other_ref, mine_ref, other_ref, own_ref, rest_ref):
    width = dq_ref.shape[1]
    cut = own_ref.shape[0]
    for ref, rows in ((rest_ref, slice(cut, dq_ref.shape[0])), (own_ref, slice(0, cut))):
        total = 0.0
        for query, pair, weights in (
            (dq_ref, dkv_ref, mine_ref), (dq_other_ref, dkv_other_ref, other_ref)
        ):
            total = total + dot(query[rows, :], weights[:, :width], ((1,), (1,)))
            total = total + dot(pair[rows, :], weights[:, width:], ((1,), (1,)))
        ref[...] = total.astype(ref.dtype)


def input_sum_kernel(one_ref, two_ref, got_ref, keep_ref, send_ref):
    total = one_ref[...] + (two_ref[...] + got_ref[...].astype(f32))
    keep_ref[...] = total[: keep_ref.shape[0]]
    send_ref[...] = total[keep_ref.shape[0] :]


def out_keep_kernel(shard, odd_ref, keep_ref, got_ref, near_ref, far_ref):
    odd = odd_ref[0]
    for parity, ref in ((1 - odd, far_ref), (odd, near_ref)):
        for j in range(ref.shape[0]):
            rows = pl.ds(pl.multiple_of((2 * j + parity) * shard, shard), shard)
            ref[j] = (keep_ref[rows, :] + got_ref[rows, :].astype(f32)).astype(ref.dtype)


def z_send_kernel(shard, z_ref, near_ref, got_ref, out_near_ref, out_got_ref, *outs):
    z = z_ref[0]
    columns = near_ref.shape[2]
    for k, ref in enumerate(outs):
        block = z ^ k
        got = got_ref[block]
        near = near_ref[block]
        ref[:shard, :columns] = (near[:shard] + got[:shard].astype(f32)).astype(ref.dtype)
        ref[:shard, columns:] = (
            out_near_ref[block] + out_got_ref[block].astype(f32)
        ).astype(ref.dtype)
        vec = near[shard:] + unpack(got[shard:])
        ref[shard:, :columns] = vec if ref.dtype == f32 else pack(vec)
        ref[shard:, columns:] = jnp.zeros_like(ref[shard:, columns:])


def z_sum_kernel(shard, mine_ref, *refs):
    gots, out_ref = refs[:-1], refs[-1]
    value, vec = mine_ref[:shard], mine_ref[shard:]
    for ref in gots:
        value = value + ref[:shard].astype(f32)
        vec = vec + unpack(ref[shard:])
    out_ref[:shard] = value.astype(bf16)
    out_ref[shard:] = pack(vec)


def tail_kernel(shard, group, ctx_ref, *refs):
    pieces, (qkv_ref, out_ref, vec_ref) = refs[:4], refs[4:]
    ctx = ctx_ref[0]
    width = 4 * group
    for i, piece in enumerate(pieces):
        who = ctx ^ i
        for third in range(3):
            start = pl.multiple_of(third * width + who * group, group)
            qkv_ref[:, pl.ds(start, group)] = piece[
                :shard, third * group : (third + 1) * group
            ].astype(f32)
        start = pl.multiple_of(((who % 2) * 2 + who // 2) * group, group)
        out_ref[:, pl.ds(start, group)] = piece[:shard, 3 * group :].astype(f32)
    vec = [unpack(piece[shard:, : 3 * group]) for piece in pieces]
    vec_ref[...] = (vec[0] + vec[1]) + (vec[2] + vec[3])


def rows_tail_kernel(rows, ctx_ref, *refs):
    pieces, out_ref = refs[:-1], refs[-1]
    for i, piece in enumerate(pieces):
        start = pl.multiple_of((ctx_ref[0] ^ i) * rows, rows)
        out_ref[pl.ds(start, rows), :] = piece[...].astype(f32)


def columns_tail_kernel(cut, ctx_ref, *refs):
    pieces, out_ref = refs[:-1], refs[-1]
    for i, piece in enumerate(pieces):
        for block in range(piece.shape[1] // cut):
            start = pl.multiple_of((block * len(pieces) + (ctx_ref[0] ^ i)) * cut, cut)
            out_ref[:, pl.ds(start, cut)] = piece[:, block * cut : (block + 1) * cut].astype(f32)


def per_device(
    inputs, timestep, doc_ids, w_qkv, w_out, w_up, w_down, bias_model, bias_up,
    norm_gains, norm_shifts, cotangent,
):
    ctx, ctx_size = lax.axis_index("ctx"), lax.axis_size("ctx")
    fsdp, fsdp_size = lax.axis_index("fsdp"), lax.axis_size("fsdp")
    core, ways = ctx % 2, ctx_size // 2
    tokens, width = inputs.shape[2], w_out.shape[1]
    hidden = w_up.shape[1]
    head_size = width // HEADS
    own_rows = 2 * tokens
    rest_rows = (ways - 1) * own_rows
    group = width // ctx_size
    columns = 3 * group
    group_ff = hidden // ctx_size
    shard = w_out.shape[0]
    shard_ff = w_down.shape[0]
    cut_ff = hidden // (fsdp_size * ctx_size)
    fsdp_range = jnp.arange(fsdp_size)
    natural = fsdp_range ^ fsdp

    small = jnp.concatenate([bias_model, bias_up, norm_gains, norm_shifts])
    small_count = small.shape[0]
    qkv_group = lax.dynamic_index_in_dim(
        w_qkv.reshape(shard, 3, ctx_size, group), ctx, 2, False
    ).reshape(shard, columns)
    small_rows = jnp.pad(small, (0, PAD * columns - small_count)).reshape(PAD, columns)
    out_send = lax.dynamic_index_in_dim(w_out.reshape(shard, 2, width // 2), core, 1, False)
    first_send = jnp.concatenate(
        [
            jnp.concatenate([qkv_group, small_rows]),
            jnp.concatenate([out_send, jnp.zeros((PAD, width // 2), bf16)]),
        ],
        axis=1,
    )
    first_pieces = gather_far(gather_near(first_send))
    up_send = lax.dynamic_index_in_dim(
        w_up.reshape(shard, fsdp_size, ctx_size, cut_ff), ctx, 2, False
    ).reshape(shard, group_ff)
    down_send = lax.dynamic_index_in_dim(
        w_down.reshape(ctx_size, shard_ff // ctx_size, width), ctx, 0, False
    )
    merged = up_send.shape == down_send.shape and ctx_size == 4 and cut_ff % 128 == 0
    feed_sends = [jnp.concatenate([up_send, down_send], axis=1)] if merged else [up_send, down_send]
    feed_mine = [lax.all_gather(send, "fsdp", axis=0, tiled=True) for send in feed_sends]

    docs = doc_ids[:, 0].astype(bf16)
    doc_rows = jnp.pad(docs[:, None, :], ((0, 0), (0, PAD - 1), (0, width - tokens)))
    mine, theirs = (
        [lax.dynamic_index_in_dim(a, c, 0, False) for a in (inputs[:, 0], doc_rows, cotangent[:, 0])]
        for c in (core, 1 - core)
    )
    swapped = over_ctx(jnp.concatenate(theirs), 1)
    x_own = jnp.concatenate([mine[0], swapped[:tokens]])
    cot_own = jnp.concatenate([mine[2], swapped[tokens + PAD :]])
    doc_own = jnp.concatenate([mine[1][:1, :tokens], swapped[tokens : tokens + 1, :tokens]], axis=1)
    packed = jnp.concatenate([x_own, jnp.pad(doc_own, ((0, PAD - 1), (0, width - own_rows)))])
    rest = gather_tokens(packed).reshape(ways - 1, own_rows + PAD, width)
    x_rest = rest[:, :own_rows].reshape(rest_rows, width)
    doc_all = jnp.concatenate([doc_own[0], rest[:, own_rows, :own_rows].reshape(-1)]).astype(f32)
    key_docs, query_docs = doc_all[:, None], doc_all[None, :]
    time_row = lax.dynamic_index_in_dim(timestep[:, 0], core, 0, True).astype(f32)
    rounded0 = (jnp.concatenate([x_own, x_rest]).astype(f32) + time_row).astype(bf16)

    ratio = fsdp_size // ctx_size
    orders = [natural] + [
        ((natural // ratio) ^ who) * ratio + natural % ratio for who in (ctx, ctx ^ 1)
    ]
    w_qkv_mine, small_all, out_mine, out_theirs = place(first_pieces, orders, shard, columns)
    w_qkv_pair = (w_qkv_mine, over_ctx(w_qkv_mine, 1))
    small_all = small_all.reshape(fsdp_size, PAD * columns)[:, :small_count].astype(f32)
    starts = [0, bias_model.shape[0]]
    starts.append(starts[1] + bias_up.shape[0])
    starts.append(starts[2] + norm_gains.shape[0])
    starts.append(small_count)
    b_model, b_up, gains, shifts = (
        small_all[:, a:b].reshape(-1) for a, b in zip(starts[:-1], starts[1:])
    )
    vecs = jnp.stack(
        [
            time_row[0], b_model[2 * width : 3 * width], gains[:width], shifts[:width],
            b_model[3 * width :], gains[width:], shifts[width:], jnp.zeros((width,), f32),
        ]
    )
    b_up_groups = b_up.reshape(fsdp_size, ctx_size, cut_ff)

    b_up_pair = [
        lax.dynamic_index_in_dim(b_up_groups, ctx ^ i, 1, False).reshape(1, group_ff)
        for i in range(2)
    ]

    projected, attended, logs = [], [], []
    for i in range(2):
        who = ctx ^ i
        b_query = lax.dynamic_slice_in_dim(b_model, who * group, group)
        b_value = lax.dynamic_slice_in_dim(b_model, width + who * group, group)
        bias = jnp.concatenate([b_query, jnp.zeros_like(b_query), b_value])
        weights = after(w_qkv_pair[i], *attended, *b_up_pair, vecs, cot_own)
        proj = (dot(rounded0, weights) + bias[None]).astype(bf16)
        out, log = attend(proj, key_docs, query_docs, head_size)
        projected.append(proj)
        attended.append(out)
        logs.append(log)
    attended_pair = jnp.concatenate(attended, axis=1)
    attended_cols = [attended_pair[:own_rows]]
    for k in range(1, ways):
        attended_cols.append(over_ctx(attended_pair[k * own_rows : (k + 1) * own_rows], 2 * k))
    attended_own = jnp.concatenate(attended_cols, axis=1)

    out_other = over_ctx(out_theirs, 1)
    normal1, inverse1, normed_own = kernel_call(
        out_kernel,
        [shape((own_rows, width)), shape((own_rows, 1)), shape((own_rows, width), bf16)],
        [attended_own, out_mine, out_other, x_own, vecs],
        scalars=[core],
        scratch=[pltpu.VMEM((own_rows, width), f32)],
    )
    normed_rest = gather_tokens(normed_own)

    feed_mine = [after(w, normed_rest) for w in feed_mine]
    feed_pair = (feed_mine, [over_ctx(w, 1) for w in feed_mine])
    acts, slopes, feeds = {}, {}, {"rest": None, "own": None}
    token = normed_own
    for part, i in (("own", 0), ("rest", 0), ("rest", 1), ("own", 1)):
        rows = normed_own if part == "own" else normed_rest
        acts[part, i], slopes[part, i], feeds[part] = feed_forward(
            after(rows, token), feed_pair[i], b_up_pair[i], feeds[part],
            bf16 if i == 1 and part == "rest" else f32,
        )
        token = acts[part, i]
    feed_own, feed_got = reduce_tokens(feeds["own"], feeds["rest"])

    result_keep, result_send, d_hidden2, d_feed_own, sums2 = kernel_call(
        turn_kernel,
        [
            shape((tokens, width), bf16), shape((tokens, width), bf16), shape((own_rows, width)),
            shape((own_rows, width), bf16), shape((8, width)),
        ],
        [normal1, feed_own, feed_got, cot_own, vecs],
    )
    d_feed_rest = gather_tokens(d_feed_own)

    def gradient(args, flops=50_000_000_000):
        return kernel_call(grad_kernel, [shape((width, width), bf16)], args, flops=flops)[0]

    def split(kept, got):
        return kernel_call(
            functools.partial(grad_split_kernel, shard),
            [shape((fsdp_size // 2, shard, width), bf16)] * 2,
            [kept, got],
            scalars=[fsdp % 2],
        )

    sides = [[2 * k + p for k in range(fsdp_size // 2)] for p in range(2)]

    def finish(near, got):
        mixed = kernel_call(add_kernel, [shape(near.shape, bf16)], [near, got])[0]
        return mixed, lax.psum_scatter(
            mixed.reshape(-1, width), "fsdp", scatter_dimension=0, tiled=True,
            axis_index_groups=sides,
        )

    d_ups, d_up_sums, d_normed = {}, {}, {}
    token = d_feed_own
    for part, rows in (("own", d_feed_own), ("rest", d_feed_rest)):
        total = None
        if merged and part == "rest":
            down_args = [
                [acts["own", i], acts["rest", i], after(d_feed_own, token), d_feed_rest] for i in range(2)
            ]
            down_away = gradient(down_args[1])
            token = down_away
        for i in range(2):
            d_ups[part, i], d_up_sums[part, i], total = feed_backward(
                after(rows, token), feed_pair[i], slopes[part, i], total,
                bf16 if i == 1 and part == "rest" else f32,
            )
            token = d_ups[part, i]
        d_normed[part] = total
    dn_own, dn_got = reduce_tokens(d_normed["own"], d_normed["rest"])

    if merged:
        down_args[0][2] = after(d_feed_own, token)
        down_near, down_far = split(gradient(down_args[0]), over_ctx(down_away, 1))
        up_args = [
            [after(normed_own, down_far), normed_rest, d_ups["own", i], d_ups["rest", i]] for i in range(2)
        ]
        up_away = gradient(up_args[1], 0)
        up_near, up_far = split(gradient(up_args[0], 0), over_ctx(up_away, 1))
        dn_got = after(dn_got, up_far)
        down_got = over_fsdp(down_far, 1)
    else:
        totals = []
        for left, right in ((acts, None), (None, d_ups)):
            grads = []
            for i in range(2):
                one = jnp.concatenate([left["own", i], left["rest", i]]) if left else (
                    jnp.concatenate([normed_own, normed_rest])
                )
                two = jnp.concatenate([right["own", i], right["rest", i]]) if right else (
                    jnp.concatenate([d_feed_own, d_feed_rest])
                )
                grads.append(dot(one, two, ((0,), (0,))))
            mixed = (grads[0] + over_ctx(grads[1].astype(bf16), 1).astype(f32)).astype(bf16)
            totals.append(lax.psum_scatter(mixed, "fsdp", scatter_dimension=0, tiled=True))

    d_hidden1, d_branch, d_att_near, d_att_far, sums1 = kernel_call(
        branch_kernel,
        [
            shape((own_rows, width)), shape((own_rows, width), bf16),
            shape((own_rows, 2 * group), bf16), shape((own_rows, width - 2 * group), bf16),
            shape((8, width)),
        ],
        [d_hidden2, dn_own, dn_got, normal1, inverse1, out_mine, out_other, vecs],
        scalars=[core],
        flops=0,
    )
    if ways == 2:
        d_attended = [d_att_near, over_ctx(d_att_far, 2)]
    else:
        d_attended = [d_att_near] + [
            over_ctx(d_att_far[:, 2 * (k - 1) * group : 2 * k * group], 2 * k)
            for k in range(1, ways)
        ]

    d_projected = [None, None]
    for i in (1, 0):
        d_query, d_pair = attend_back(
            projected[i], d_attended, i * group, key_docs, query_docs, logs[i], head_size,
        )
        d_projected[i] = (d_query, d_pair)
        if i:
            if merged:
                down_mixed, down_total = finish(down_near, after(down_got, d_query))
                up_got = over_fsdp(after(up_far, down_mixed), 1)
                d_query = after(d_query, down_mixed)
            qkv_away = kernel_call(
                functools.partial(qkv_send_kernel, shard),
                [shape((fsdp_size, shard, columns), bf16)],
                [rounded0, d_query, d_pair],
            )[0]
            out_keep, out_away = kernel_call(
                out_grad_kernel,
                [shape((width, width // 2)), shape((width, width // 2), bf16)],
                [after(attended_own, qkv_away), d_branch],
                scalars=[jnp.stack([ctx, core])],
            )
            out_got = over_ctx(out_away, 1)
            for k in range(int(math.log2(ways))):
                half = out_keep.shape[1] // 2
                bit = (ctx >> (k + 1)) % 2
                if half % 128 == 0:
                    out_keep, out_away = kernel_call(
                        split_kernel, [shape((width, half)), shape((width, half), bf16)],
                        [out_keep, out_got], scalars=[bit],
                    )
                else:
                    both = (out_keep + out_got.astype(f32)).reshape(width, 2, half)
                    out_keep = lax.dynamic_index_in_dim(both, bit, 1, False)
                    out_away = lax.dynamic_index_in_dim(both, 1 - bit, 1, False).astype(bf16)
                out_got = over_ctx(out_away, 2 << k)
            d_attended[0] = after(d_attended[0], out_away)

    qkv_got = over_ctx(qkv_away, 1)
    keep_outs = [
        shape((fsdp_size // 2, shard + VEC, columns)),
        shape((fsdp_size // 2, shard + PAD, columns), bf16),
    ]
    quarter = out_keep.shape[1]
    if merged:
        near, far = kernel_call(
            functools.partial(qkv_vec_keep_kernel, shard),
            keep_outs,
            [
                rounded0, *d_projected[0], *d_projected[1], qkv_got, sums1, sums2,
                *(d_up_sums[part, i] for i in range(2) for part in ("own", "rest")),
            ],
            scalars=[jnp.stack([fsdp % 2, ctx])],
            scratch=[
                pltpu.VMEM((width, columns), f32), pltpu.VMEM((8, width), f32),
                pltpu.VMEM((8, hidden), f32), pltpu.VMEM((fsdp_size, VEC, columns), f32),
            ],
        )
    else:
        def in_groups(pair, size):
            stacked = jnp.stack(pair)
            ordered = jnp.where(core == 0, stacked, stacked[::-1])
            return lax.dynamic_update_slice_in_dim(
                jnp.zeros((ctx_size, size), f32), ordered, ctx - core, 0
            )

        column = lambda value: jnp.sum(value.astype(f32), axis=0)
        vec_query = in_groups([column(d[0]) for d in d_projected], group).reshape(-1)
        vec_value = in_groups([column(d[1][:, group:]) for d in d_projected], group).reshape(-1)
        vec_up = jnp.swapaxes(
            in_groups(
                [d_up_sums["own", i][0] + d_up_sums["rest", i][0] for i in range(2)], group_ff
            ).reshape(ctx_size, fsdp_size, cut_ff), 0, 1,
        ).reshape(fsdp_size, -1)
        vec_model = jnp.concatenate([vec_query, vec_value, sums1[2], sums2[2]]).reshape(fsdp_size, -1)
        vec_gain = jnp.concatenate([sums1[0], sums2[0]]).reshape(fsdp_size, -1)
        vec_shift = jnp.concatenate([sums1[1], sums2[1]]).reshape(fsdp_size, -1)
        vectors = jnp.concatenate([vec_model, vec_up, vec_gain, vec_shift], axis=1)
        vectors = jnp.pad(vectors, ((0, 0), (0, VEC * columns - small_count))).reshape(
            fsdp_size, VEC, columns
        )
        near, far = kernel_call(
            functools.partial(qkv_keep_kernel, shard),
            keep_outs,
            [rounded0, *d_projected[0], qkv_got, vectors],
            scalars=[fsdp % 2],
            scratch=[pltpu.VMEM((width, columns), f32)],
        )
    got = over_fsdp(far, 1)
    if merged:
        up_mixed, up_total = finish(up_near, after(up_got, far))
    out_near, out_far = kernel_call(
        functools.partial(out_keep_kernel, shard),
        [
            shape((fsdp_size // 2, shard, quarter)),
            shape((fsdp_size // 2, shard, quarter), bf16),
        ],
        [after(out_keep, far), out_got],
        scalars=[fsdp % 2],
    )
    out_cross = over_fsdp(out_far, 1)

    dx_own, dx_rest = kernel_call(
        input_kernel,
        [shape((own_rows, width)), shape((rest_rows, width), bf16)],
        [after(d_projected[0][0], out_far, got), d_projected[0][1], *d_projected[1], *w_qkv_pair],
    )
    if merged:
        got = after(got, up_mixed)
    sends = kernel_call(
        functools.partial(z_send_kernel, shard),
        [shape((shard + VEC, columns + quarter))]
        + [shape((shard + PAD, columns + quarter), bf16)] * (fsdp_size // 2 - 1),
        [near, got, out_near, out_cross],
        scalars=[fsdp // 2],
    )
    mine_block = sends[0]
    total = kernel_call(
        functools.partial(z_sum_kernel, shard),
        [shape((shard + PAD, columns + quarter), bf16)],
        [mine_block, *(over_fsdp(value, 2 * k) for k, value in enumerate(sends[1:], 1))],
    )[0]

    dx_own, dx_got = reduce_tokens(dx_own, dx_rest)
    input_keep, input_send = kernel_call(
        input_sum_kernel, [shape((tokens, width))] * 2, [d_hidden1, dx_own, dx_got]
    )

    if merged:
        def quarters(own, direct=False):
            if direct:
                return [own] + [over_ctx(own, i) for i in range(1, 4)]
            far_own = over_ctx(own, 2)
            other = over_ctx(jnp.concatenate([own, far_own]), 1)
            return [own, other[: own.shape[0]], far_own, other[own.shape[0] :]]

        grad_down = kernel_call(
            functools.partial(rows_tail_kernel, shard),
            [shape((shard_ff, width))],
            quarters(after(down_total, up_mixed)),
            scalars=[ctx],
        )[0]
        grad_up = kernel_call(
            functools.partial(columns_tail_kernel, cut_ff),
            [shape((shard, hidden))],
            quarters(up_total),
            scalars=[ctx],
        )[0]
        grad_qkv, grad_out, vec_done = kernel_call(
            functools.partial(tail_kernel, shard, group),
            [shape((shard, 3 * width)), shape((shard, width)), shape((VEC, columns))],
            quarters(total, direct=True),
            scalars=[ctx],
        )
        counts = [b - a for a, b in zip(starts[:-1], starts[1:])]
        vectors = [vec_done[row, :count] for row, count in enumerate(counts)]
    else:
        spread = lambda own: lax.all_gather(own, "ctx", axis=0)
        tail = spread(total)
        grad_qkv = jnp.transpose(
            tail[:, :shard, :columns].reshape(ctx_size, shard, 3, group), (1, 2, 0, 3)
        ).reshape(shard, 3 * width).astype(f32)
        order = []
        levels = int(math.log2(ctx_size))
        for place_index in range(ctx_size):
            order.append(
                sum(((place_index >> (levels - 1 - b)) & 1) << b for b in range(levels))
            )
        grad_out = jnp.concatenate([tail[d, :shard, columns:] for d in order], axis=1).astype(f32)
        vec = tail[:, shard:, :columns].astype(f32)
        vec_done = jnp.sum(vec[:, :VEC] + vec[:, VEC:], axis=0).reshape(-1)
        vectors = [vec_done[a:b] for a, b in zip(starts[:-1], starts[1:])]
        grad_down = spread(totals[0]).reshape(shard_ff, width).astype(f32)
        grad_up = jnp.transpose(
            spread(totals[1]).reshape(ctx_size, shard, fsdp_size, cut_ff), (1, 2, 0, 3)
        ).reshape(shard, hidden).astype(f32)

    def give_back(keep, send):
        got = over_ctx(send, 1)
        return jnp.stack([jnp.where(core == 0, keep, got), jnp.where(core == 0, got, keep)])

    block_output = give_back(result_keep, result_send)[:, None]
    input_grad = give_back(input_keep, input_send)[:, None]
    return (
        block_output, input_grad, grad_qkv, grad_out, grad_up, grad_down,
        *vectors,
    )


def solution(mesh):
    token = P(None, "fsdp", "ctx", None)
    rows = P("fsdp", None)
    flat = P("fsdp")
    return jax.shard_map(
        per_device,
        mesh=mesh,
        in_specs=(
            token, P(None, "fsdp", None), P(None, "fsdp", "ctx"), rows, rows, rows, rows,
            flat, flat, flat, flat, token,
        ),
        out_specs=(token, token, rows, rows, rows, rows, flat, flat, flat, flat),
        check_vma=False,
    )
```

```python
import functools
import math

import jax
import jax.numpy as jnp
from jax import lax
from jax.experimental import pallas as pl
from jax.experimental.pallas import tpu as pltpu
from jax.sharding import PartitionSpec as P

HEADS = 16
EPS = 1e-05
LOG2E = math.log2(math.e)
VEC = 8
PAD = 2 * VEC
f32 = jnp.float32
bf16 = jnp.bfloat16


def dot(left, right, dims=((1,), (0,))):
    return lax.dot_general(left, right, (dims, ((), ())), preferred_element_type=f32)


def over_ctx(value, mask):
    size = lax.axis_size("ctx")
    return lax.ppermute(value, "ctx", [(i, i ^ mask) for i in range(size)])


def over_fsdp(value, mask):
    size = lax.axis_size("fsdp")
    return lax.ppermute(value, "fsdp", [(i, i ^ mask) for i in range(size)])


def after(value, *others):
    return lax.optimization_barrier((value, *others))[0]


def shape(dims, dtype=f32):
    return jax.ShapeDtypeStruct(tuple(dims), dtype)


def kernel_call(body, outs, args, scalars=(), scratch=(), flops=50_000_000_000):
    scalars = [jnp.asarray(s, jnp.int32).reshape(-1) for s in scalars]
    specs = [pl.BlockSpec(memory_space=pltpu.SMEM)] * len(scalars)
    specs += [pl.BlockSpec(memory_space=pltpu.VMEM)] * len(args)
    largest = max(math.prod(a.shape) * 4 for a in [*args, *outs])
    held = sum(math.prod(a.shape) * jnp.dtype(a.dtype).itemsize for a in scratch)
    limit = min(held + max(6 * 2**20, 2 * largest), 56 * 2**20)
    return pl.pallas_call(
        body,
        in_specs=specs,
        out_specs=[pl.BlockSpec(memory_space=pltpu.VMEM)] * len(outs),
        out_shape=list(outs),
        scratch_shapes=list(scratch),
        compiler_params=pltpu.CompilerParams(vmem_limit_bytes=limit),
        cost_estimate=pl.CostEstimate(flops=flops, bytes_accessed=1024, transcendentals=0),
    )(*scalars, *args)


def attend_kernel(head_size, scale, block_ref, whole_ref, key_doc_ref, query_doc_ref, out_ref, log_ref):
    width = out_ref.shape[1]
    same = key_doc_ref[...] == query_doc_ref[...]
    for head in range(width // head_size):
        cut = head * head_size
        query = block_ref[:, cut : cut + head_size]
        key = whole_ref[:, width + cut : width + cut + head_size]
        value = whole_ref[:, 2 * width + cut : 2 * width + cut + head_size]
        scores = jnp.where(same, dot(key, query, ((1,), (1,))), -1e30)
        top = jnp.max(scores, axis=0, keepdims=True)
        expo = jnp.exp2((scores - top) * (scale * LOG2E))
        total = jnp.sum(expo, axis=0, keepdims=True)
        probs = (expo * (1.0 / total)).astype(bf16)
        out_ref[:, cut : cut + head_size] = dot(value, probs, ((0,), (0,))).T.astype(bf16)
        log_ref[head : head + 1, :] = top * (scale * LOG2E) + jnp.log2(total)


def attend(projected, key_docs, query_docs, head_size):
    length, width = projected.shape[0], projected.shape[1] // 3
    heads = width // head_size
    block = min(512, length)
    return pl.pallas_call(
        functools.partial(attend_kernel, head_size, 1.0 / math.sqrt(head_size)),
        grid=(length // block,),
        in_specs=[
            pl.BlockSpec((block, 3 * width), lambda i: (i, 0)),
            pl.BlockSpec((length, 3 * width), lambda i: (0, 0)),
            pl.BlockSpec((length, 1), lambda i: (0, 0)),
            pl.BlockSpec((1, block), lambda i: (0, i)),
        ],
        out_specs=[
            pl.BlockSpec((block, width), lambda i: (i, 0)),
            pl.BlockSpec((heads, block), lambda i: (0, i)),
        ],
        out_shape=[shape((length, width), bf16), shape((heads, length))],
        compiler_params=pltpu.CompilerParams(vmem_limit_bytes=(24 if length <= 512 else 48) * 2**20),
        cost_estimate=pl.CostEstimate(
            flops=0, bytes_accessed=1024, transcendentals=0,
        ),
    )(projected, projected, key_docs, query_docs)


def attend_back_kernel(head_size, scale, steps, first, pieces, *refs):
    block_ref, whole_ref, key_doc_ref, query_doc_ref, log_ref = refs[:5]
    grad_refs, (query_out, pair_out, pair_sum) = refs[5 : 5 + pieces], refs[5 + pieces :]
    width = query_out.shape[1]
    step = pl.program_id(0)
    same = key_doc_ref[...] == query_doc_ref[...]

    if steps > 1:
        @pl.when(step == 0)
        def _():
            pair_sum[...] = jnp.zeros_like(pair_sum)

    def add(place, value):
        if steps > 1:
            pair_sum[:, place : place + head_size] += value
        else:
            pair_out[:, place : place + head_size] = value.astype(bf16)

    for head in range(width // head_size):
        cut = head * head_size
        query = block_ref[:, cut : cut + head_size]
        key = whole_ref[:, width + cut : width + cut + head_size]
        value = whole_ref[:, 2 * width + cut : 2 * width + cut + head_size]
        span = slice(first + cut, first + cut + head_size)
        grad = jnp.concatenate([ref[:, span] for ref in grad_refs]) if pieces > 1 else grad_refs[0][:, span]
        scores = dot(key, query, ((1,), (1,)))
        probs = jnp.where(
            same, jnp.exp2(scores * (scale * LOG2E) - log_ref[head : head + 1, :]), 0.0
        )
        d_probs = dot(value, grad, ((1,), (1,)))
        inner = jnp.sum(probs * d_probs, axis=0, keepdims=True)
        d_scores = (probs * (d_probs - inner)).astype(bf16)
        query_out[:, cut : cut + head_size] = (
            dot(key, d_scores, ((0,), (0,))).T * scale
        ).astype(bf16)
        add(cut, dot(d_scores, query) * scale)
        add(width + cut, dot(probs.astype(bf16), grad))

    if steps > 1:
        @pl.when(step == steps - 1)
        def _():
            pair_out[...] = pair_sum[...].astype(bf16)


def attend_back(projected, grads, first, key_docs, query_docs, logs, head_size):
    length, width = projected.shape[0], projected.shape[1] // 3
    heads = width // head_size
    block = min(512, length)
    steps = length // block
    if steps > 1:
        grads = [jnp.concatenate(grads)]
    grad_rows = [grad.shape[0] // steps for grad in grads]
    return pl.pallas_call(
        functools.partial(
            attend_back_kernel, head_size, 1.0 / math.sqrt(head_size), steps, first, len(grads)
        ),
        grid=(steps,),
        in_specs=[
            pl.BlockSpec((block, 3 * width), lambda i: (i, 0)),
            pl.BlockSpec((length, 3 * width), lambda i: (0, 0)),
            pl.BlockSpec((length, 1), lambda i: (0, 0)),
            pl.BlockSpec((1, block), lambda i: (0, i)),
            pl.BlockSpec((heads, block), lambda i: (0, i)),
        ]
        + [pl.BlockSpec((rows, grads[0].shape[1]), lambda i: (i, 0)) for rows in grad_rows],
        out_specs=[
            pl.BlockSpec((block, width), lambda i: (i, 0)),
            pl.BlockSpec((length, 2 * width), lambda i: (0, 0)),
        ],
        out_shape=[shape((length, width), bf16), shape((length, 2 * width), bf16)],
        scratch_shapes=[pltpu.VMEM((length if steps > 1 else 8, 2 * width), f32)],
        compiler_params=pltpu.CompilerParams(vmem_limit_bytes=(24 if length <= 512 else 56) * 2**20),
        cost_estimate=pl.CostEstimate(flops=0, bytes_accessed=1024, transcendentals=0),
    )(projected, projected, key_docs, query_docs, logs, *grads)


def place_kernel(count, rows, columns, where_ref, *refs):
    pieces, (qkv_ref, small_ref, mine_ref, theirs_ref) = refs[:count], refs[count:]
    for j, piece in enumerate(pieces):
        spare = piece.shape[0] - rows
        start = pl.multiple_of(where_ref[j] * rows, rows)
        qkv_ref[pl.ds(start, rows), :] = piece[:rows, :columns]
        start = pl.multiple_of(where_ref[j] * spare, spare)
        small_ref[pl.ds(start, spare), :] = piece[rows:, :columns]
        for way, ref in enumerate((mine_ref, theirs_ref), 1):
            start = pl.multiple_of(where_ref[way * count + j] * rows, rows)
            ref[pl.ds(start, rows), :] = piece[:rows, columns:]


def place(pieces, orders, rows, columns):
    count, spare = len(pieces), pieces[0].shape[0] - rows
    rest = pieces[0].shape[1] - columns
    return kernel_call(
        functools.partial(place_kernel, count, rows, columns),
        [
            shape((count * rows, columns), bf16), shape((count * spare, columns), bf16),
            shape((count * rows, rest), bf16), shape((count * rows, rest), bf16),
        ],
        pieces,
        scalars=[jnp.concatenate(orders)],
    )


def gather_near(shard):
    size = lax.axis_size("fsdp")
    return [shard] + [over_fsdp(shard, 2 * k) for k in range(1, size // 2)]


def gather_far(near):
    pieces = []
    for value in near:
        pieces += [value, over_fsdp(value, 1)]
    return pieces


def gather_tokens(own):
    have, mask = own, 1
    while 2 * mask < lax.axis_size("ctx"):
        got = over_ctx(have, 2 * mask)
        if lax.axis_size("ctx") == 4:
            return got
        have = jnp.concatenate([have, got])
        mask *= 2
    return have[own.shape[0] :]


def reduce_tokens(own, rest):
    ways = lax.axis_size("ctx") // 2
    if ways == 2:
        return own, over_ctx(rest, 2)
    have, mask = jnp.concatenate([own, rest.astype(f32)]), ways // 2
    while mask > 1:
        half = have.shape[0] // 2
        have = have[:half] + over_ctx(have[half:].astype(bf16), 2 * mask).astype(f32)
        mask //= 2
    half = have.shape[0] // 2
    return have[:half], over_ctx(have[half:].astype(bf16), 2)


def norm_parts(value):
    centred = value - jnp.mean(value, axis=-1, keepdims=True)
    inverse = lax.rsqrt(jnp.mean(centred * centred, axis=-1, keepdims=True) + EPS)
    return centred * inverse, inverse


def norm_back(grad, normal, inverse, gain):
    inner = grad * gain
    return inverse * (
        inner
        - jnp.mean(inner, axis=-1, keepdims=True)
        - normal * jnp.mean(inner * normal, axis=-1, keepdims=True)
    )


def column_sums(*values):
    rows = [jnp.sum(value, axis=0, keepdims=True) for value in values]
    return jnp.concatenate(rows + [jnp.zeros_like(rows[0])] * (8 - len(rows)))


def out_kernel(
    core_ref, att_ref, mine_ref, other_ref, x_ref, vec_ref, normal_ref, inverse_ref, normed_ref, hidden_ref
):
    half = mine_ref.shape[1]
    core = core_ref[0]
    for way, ref in ((core, mine_ref), (1 - core, other_ref)):
        hidden_ref[:, pl.ds(pl.multiple_of(way * half, half), half)] = dot(att_ref[...], ref[...])
    hidden1 = hidden_ref[...] + (x_ref[...].astype(f32) + vec_ref[0:1, :]) + vec_ref[1:2, :]
    normal, inverse = norm_parts(hidden1)
    normal_ref[...] = normal
    inverse_ref[...] = inverse
    normed_ref[...] = (normal * vec_ref[2:3, :] + vec_ref[3:4, :]).astype(bf16)


def views(refs, width):
    if len(refs) == 2:
        return refs
    return refs[0].at[:, : refs[0].shape[1] - width], refs[0].at[:, refs[0].shape[1] - width :]


def forward_kernel(count, first, rows_ref, bias_ref, *refs):
    up_ref, down_ref = views(refs[:count], rows_ref.shape[1])
    act_ref, slope_ref, feed_ref = refs[-3:]
    upward = dot(rows_ref[...], up_ref[...]) + bias_ref[...]
    lower = 0.5 + 0.5 * lax.erf(upward * math.sqrt(0.5))
    density = jnp.exp2(upward * upward * (-0.5 * LOG2E)) * (1.0 / math.sqrt(2.0 * math.pi))
    act = (upward * lower).astype(bf16)
    act_ref[...] = act
    slope_ref[...] = lower + upward * density
    feed = dot(act, down_ref[...])
    if not first:
        feed = feed + refs[count][...]
    feed_ref[...] = feed.astype(feed_ref.dtype)


def feed_forward(rows, weights, bias, feed, dtype):
    count, group_ff = rows.shape[0], bias.shape[1]
    return kernel_call(
        functools.partial(forward_kernel, len(weights), feed is None),
        [shape((count, group_ff), bf16), shape((count, group_ff)), shape(rows.shape, dtype)],
        [rows, bias, *weights] + ([] if feed is None else [feed]),
    )


def backward_kernel(count, first, rows_ref, slope_ref, *refs):
    up_ref, down_ref = views(refs[:count], rows_ref.shape[1])
    d_up_ref, sum_ref, total_ref = refs[-3:]
    d_up = (dot(rows_ref[...], down_ref[...], ((1,), (1,))) * slope_ref[...]).astype(bf16)
    d_up_ref[...] = d_up
    sum_ref[...] = column_sums(d_up.astype(f32))
    total = dot(d_up, up_ref[...], ((1,), (1,)))
    if not first:
        total = total + refs[count][...]
    total_ref[...] = total.astype(total_ref.dtype)


def feed_backward(rows, weights, slope, total, dtype):
    count, group_ff = slope.shape
    return kernel_call(
        functools.partial(backward_kernel, len(weights), total is None),
        [shape((count, group_ff), bf16), shape((8, group_ff)), shape(rows.shape, dtype)],
        [rows, slope, *weights] + ([] if total is None else [total]),
    )


def turn_kernel(
    normal_ref, feed_ref, got_ref, cot_ref, vec_ref, keep_ref, send_ref, d_hidden_ref, d_feed_ref, sum_ref
):
    normed1 = normal_ref[...] * vec_ref[2:3, :] + vec_ref[3:4, :]
    hidden2 = normed1 + (feed_ref[...] + got_ref[...].astype(f32) + vec_ref[4:5, :])
    normal, inverse = norm_parts(hidden2)
    gain = vec_ref[5:6, :]
    result = (normal * gain + vec_ref[6:7, :]).astype(bf16)
    keep_ref[...] = result[: keep_ref.shape[0]]
    send_ref[...] = result[keep_ref.shape[0] :]
    cot = cot_ref[...].astype(f32)
    d_hidden2 = norm_back(cot, normal, inverse, gain)
    d_hidden_ref[...] = d_hidden2
    d_feed = d_hidden2.astype(bf16)
    d_feed_ref[...] = d_feed
    sum_ref[...] = column_sums(cot * normal, cot, d_feed.astype(f32))


def branch_kernel(
    core_ref, d_hidden2_ref, own_ref, got_ref, normal_ref, inverse_ref, mine_ref, other_ref, vec_ref,
    d_hidden1_ref, d_branch_ref, near_ref, far_ref, sum_ref,
):
    core, half, near = core_ref[0], mine_ref.shape[1], near_ref.shape[1]
    d_normed = d_hidden2_ref[...] + (own_ref[...] + got_ref[...].astype(f32))
    normal = normal_ref[...]
    d_hidden1 = norm_back(d_normed, normal, inverse_ref[...], vec_ref[2:3, :])
    d_hidden1_ref[...] = d_hidden1
    d_branch = d_hidden1.astype(bf16)
    d_branch_ref[...] = d_branch
    first = d_branch_ref[:, pl.ds(pl.multiple_of(core * half, half), half)]
    second = d_branch_ref[:, pl.ds(pl.multiple_of((1 - core) * half, half), half)]
    for ref, start in ((far_ref, near), (near_ref, 0)):
        span = slice(start, start + ref.shape[1])
        ref[...] = (
            dot(first, mine_ref[span, :], ((1,), (1,)))
            + dot(second, other_ref[span, :], ((1,), (1,)))
        ).astype(bf16)
    sum_ref[...] = column_sums(d_normed * normal, d_normed, d_branch.astype(f32))


def grad_kernel(one_ref, two_ref, left_ref, right_ref, out_ref):
    out_ref[...] = (
        dot(one_ref[...], left_ref[...], ((0,), (0,))) + dot(two_ref[...], right_ref[...], ((0,), (0,)))
    ).astype(bf16)


def grad_split_kernel(shard, odd_ref, keep_ref, got_ref, near_ref, far_ref):
    odd = odd_ref[0]
    for parity, ref in ((1 - odd, far_ref), (odd, near_ref)):
        for j in range(ref.shape[0]):
            rows = pl.ds(pl.multiple_of((2 * j + parity) * shard, shard), shard)
            ref[j] = (keep_ref[rows, :].astype(f32) + got_ref[rows, :].astype(f32)).astype(bf16)


def add_kernel(near_ref, got_ref, out_ref):
    out_ref[...] = (near_ref[...].astype(f32) + got_ref[...].astype(f32)).astype(out_ref.dtype)


def out_grad_kernel(ctx_ref, att_ref, d_branch_ref, keep_ref, send_ref):
    ctx = ctx_ref[0]
    core = ctx_ref[1]
    group, half = ctx_ref_group(att_ref, keep_ref), keep_ref.shape[1]
    for way, ref in ((core, keep_ref), (1 - core, send_ref)):
        columns = d_branch_ref[:, pl.ds(pl.multiple_of(way * half, half), half)]
        grad = dot(att_ref[...], columns, ((0,), (0,)))
        for i in range(grad.shape[0] // group):
            start = pl.multiple_of((ctx ^ i) * group, group)
            ref[pl.ds(start, group), :] = grad[i * group : (i + 1) * group].astype(ref.dtype)


def ctx_ref_group(att_ref, keep_ref):
    return att_ref.shape[1] // lax.axis_size("ctx")


def split_kernel(bit_ref, keep_ref, got_ref, kept_ref, send_ref):
    half = kept_ref.shape[1]
    for way, ref in ((bit_ref[0], kept_ref), (1 - bit_ref[0], send_ref)):
        span = pl.ds(pl.multiple_of(way * half, half), half)
        ref[...] = (keep_ref[:, span] + got_ref[:, span].astype(f32)).astype(ref.dtype)


def pack(values):
    high = values.astype(bf16)
    return jnp.concatenate([high, (values - high.astype(f32)).astype(bf16)])


def unpack(rows):
    return rows[:VEC].astype(f32) + rows[VEC:].astype(f32)


def qkv_send_kernel(shard, r0_ref, dq_ref, dkv_ref, out_ref):
    width = dq_ref.shape[1]
    query = dot(r0_ref[...], dq_ref[...], ((0,), (0,)))
    pair = dot(r0_ref[...], dkv_ref[...], ((0,), (0,)))
    for block in range(out_ref.shape[0]):
        rows = slice(block * shard, (block + 1) * shard)
        out_ref[block, :, :width] = query[rows].astype(bf16)
        out_ref[block, :, width:] = pair[rows].astype(bf16)


def split_by_parity(shard, odd, grad_ref, got_ref, vec_ref, near_ref, far_ref):
    for parity, ref in ((1 - odd, far_ref), (odd, near_ref)):
        for j in range(ref.shape[0]):
            block = 2 * j + parity
            rows = pl.ds(pl.multiple_of(block * shard, shard), shard)
            ref[j, :shard] = (grad_ref[rows, :] + got_ref[block].astype(f32)).astype(ref.dtype)
            vec = vec_ref[block]
            ref[j, shard:] = vec if ref.dtype == f32 else pack(vec)


def qkv_keep_kernel(
    shard, odd_ref, r0_ref, dq_ref, dkv_ref, got_ref, vec_ref, near_ref, far_ref, grad_ref
):
    width = dq_ref.shape[1]
    grad_ref[:, :width] = dot(r0_ref[...], dq_ref[...], ((0,), (0,)))
    grad_ref[:, width:] = dot(r0_ref[...], dkv_ref[...], ((0,), (0,)))
    split_by_parity(shard, odd_ref[0], grad_ref, got_ref, vec_ref, near_ref, far_ref)


def qkv_vec_keep_kernel(
    shard, place_ref, r0_ref, dq_ref, dkv_ref, dq_other_ref, dkv_other_ref, got_ref, sums1_ref, sums2_ref,
    up_own_ref, up_rest_ref, up_own_other_ref, up_rest_other_ref, near_ref, far_ref, grad_ref, flat_ref,
    up_ref, vec_ref,
):
    odd, ctx = place_ref[0], place_ref[1]
    width = dq_ref.shape[1]
    size = vec_ref.shape[0]
    flat_ref[...] = jnp.zeros_like(flat_ref)
    up_ref[...] = jnp.zeros_like(up_ref)
    vec_ref[...] = jnp.zeros_like(vec_ref)
    cut = up_own_ref.shape[1] // size
    pairs = (
        (dq_ref, dkv_ref, up_own_ref, up_rest_ref),
        (dq_other_ref, dkv_other_ref, up_own_other_ref, up_rest_other_ref),
    )
    for i, (query, pair, own, rest) in enumerate(pairs):
        who = ctx ^ i
        span = pl.ds(pl.multiple_of(who * width, width), width)
        flat_ref[0:1, span] = jnp.sum(query[...].astype(f32), axis=0, keepdims=True)
        flat_ref[1:2, span] = jnp.sum(pair[:, width:].astype(f32), axis=0, keepdims=True)
        for f in range(size):
            start = pl.multiple_of((f * (up_ref.shape[1] // cut // size) + who) * cut, cut)
            here = slice(f * cut, (f + 1) * cut)
            up_ref[0:1, pl.ds(start, cut)] = own[0:1, here] + rest[0:1, here]
    full = flat_ref.shape[1]
    model = (flat_ref[0:1], flat_ref[1:2], sums1_ref[2:3], sums2_ref[2:3])
    rows = (model, (up_ref[0:1],), (sums1_ref[0:1], sums2_ref[0:1]), (sums1_ref[1:2], sums2_ref[1:2]))
    for row, sources in enumerate(rows):
        length = sources[0].shape[1]
        part = len(sources) * length // size
        for f in range(size):
            source, start = sources[f * part // length], f * part % length
            vec_ref[f, row : row + 1, :part] = source[:, start : start + part]
    grad_ref[:, :width] = dot(r0_ref[...], dq_ref[...], ((0,), (0,)))
    grad_ref[:, width:] = dot(r0_ref[...], dkv_ref[...], ((0,), (0,)))
    split_by_parity(shard, odd, grad_ref, got_ref, vec_ref, near_ref, far_ref)


def input_kernel(dq_ref, dkv_ref, dq_other_ref, dkv_other_ref, mine_ref, other_ref, own_ref, rest_ref):
    width = dq_ref.shape[1]
    cut = own_ref.shape[0]
    for ref, rows in ((rest_ref, slice(cut, dq_ref.shape[0])), (own_ref, slice(0, cut))):
        total = 0.0
        for query, pair, weights in (
            (dq_ref, dkv_ref, mine_ref), (dq_other_ref, dkv_other_ref, other_ref)
        ):
            total = total + dot(query[rows, :], weights[:, :width], ((1,), (1,)))
            total = total + dot(pair[rows, :], weights[:, width:], ((1,), (1,)))
        ref[...] = total.astype(ref.dtype)


def input_sum_kernel(one_ref, two_ref, got_ref, keep_ref, send_ref):
    total = one_ref[...] + (two_ref[...] + got_ref[...].astype(f32))
    keep_ref[...] = total[: keep_ref.shape[0]]
    send_ref[...] = total[keep_ref.shape[0] :]


def out_keep_kernel(shard, odd_ref, keep_ref, got_ref, near_ref, far_ref):
    odd = odd_ref[0]
    for parity, ref in ((1 - odd, far_ref), (odd, near_ref)):
        for j in range(ref.shape[0]):
            rows = pl.ds(pl.multiple_of((2 * j + parity) * shard, shard), shard)
            ref[j] = (keep_ref[rows, :] + got_ref[rows, :].astype(f32)).astype(ref.dtype)


def z_send_kernel(shard, z_ref, near_ref, got_ref, out_near_ref, out_got_ref, *outs):
    z = z_ref[0]
    columns = near_ref.shape[2]
    for k, ref in enumerate(outs):
        block = z ^ k
        got = got_ref[block]
        near = near_ref[block]
        ref[:shard, :columns] = (near[:shard] + got[:shard].astype(f32)).astype(ref.dtype)
        ref[:shard, columns:] = (
            out_near_ref[block] + out_got_ref[block].astype(f32)
        ).astype(ref.dtype)
        vec = near[shard:] + unpack(got[shard:])
        ref[shard:, :columns] = vec if ref.dtype == f32 else pack(vec)
        ref[shard:, columns:] = jnp.zeros_like(ref[shard:, columns:])


def z_sum_kernel(shard, mine_ref, *refs):
    gots, out_ref = refs[:-1], refs[-1]
    value, vec = mine_ref[:shard], mine_ref[shard:]
    for ref in gots:
        value = value + ref[:shard].astype(f32)
        vec = vec + unpack(ref[shard:])
    out_ref[:shard] = value.astype(bf16)
    out_ref[shard:] = pack(vec)


def tail_kernel(shard, group, ctx_ref, *refs):
    pieces, (qkv_ref, out_ref, vec_ref) = refs[:4], refs[4:]
    ctx = ctx_ref[0]
    width = 4 * group
    for i, piece in enumerate(pieces):
        who = ctx ^ i
        for third in range(3):
            start = pl.multiple_of(third * width + who * group, group)
            qkv_ref[:, pl.ds(start, group)] = piece[
                :shard, third * group : (third + 1) * group
            ].astype(f32)
        start = pl.multiple_of(((who % 2) * 2 + who // 2) * group, group)
        out_ref[:, pl.ds(start, group)] = piece[:shard, 3 * group :].astype(f32)
    vec = [unpack(piece[shard:, : 3 * group]) for piece in pieces]
    vec_ref[...] = (vec[0] + vec[1]) + (vec[2] + vec[3])


def rows_tail_kernel(rows, ctx_ref, *refs):
    pieces, out_ref = refs[:-1], refs[-1]
    for i, piece in enumerate(pieces):
        start = pl.multiple_of((ctx_ref[0] ^ i) * rows, rows)
        out_ref[pl.ds(start, rows), :] = piece[...].astype(f32)


def columns_tail_kernel(cut, ctx_ref, *refs):
    pieces, out_ref = refs[:-1], refs[-1]
    for i, piece in enumerate(pieces):
        for block in range(piece.shape[1] // cut):
            start = pl.multiple_of((block * len(pieces) + (ctx_ref[0] ^ i)) * cut, cut)
            out_ref[:, pl.ds(start, cut)] = piece[:, block * cut : (block + 1) * cut].astype(f32)


def per_device(
    inputs, timestep, doc_ids, w_qkv, w_out, w_up, w_down, bias_model, bias_up,
    norm_gains, norm_shifts, cotangent,
):
    ctx, ctx_size = lax.axis_index("ctx"), lax.axis_size("ctx")
    fsdp, fsdp_size = lax.axis_index("fsdp"), lax.axis_size("fsdp")
    core, ways = ctx % 2, ctx_size // 2
    tokens, width = inputs.shape[2], w_out.shape[1]
    hidden = w_up.shape[1]
    head_size = width // HEADS
    own_rows = 2 * tokens
    rest_rows = (ways - 1) * own_rows
    group = width // ctx_size
    columns = 3 * group
    group_ff = hidden // ctx_size
    shard = w_out.shape[0]
    shard_ff = w_down.shape[0]
    cut_ff = hidden // (fsdp_size * ctx_size)
    fsdp_range = jnp.arange(fsdp_size)
    natural = fsdp_range ^ fsdp

    small = jnp.concatenate([bias_model, bias_up, norm_gains, norm_shifts])
    small_count = small.shape[0]
    qkv_group = lax.dynamic_index_in_dim(
        w_qkv.reshape(shard, 3, ctx_size, group), ctx, 2, False
    ).reshape(shard, columns)
    small_rows = jnp.pad(small, (0, PAD * columns - small_count)).reshape(PAD, columns)
    out_send = lax.dynamic_index_in_dim(w_out.reshape(shard, 2, width // 2), core, 1, False)
    first_send = jnp.concatenate(
        [
            jnp.concatenate([qkv_group, small_rows]),
            jnp.concatenate([out_send, jnp.zeros((PAD, width // 2), bf16)]),
        ],
        axis=1,
    )
    first_pieces = gather_far(gather_near(first_send))
    up_send = lax.dynamic_index_in_dim(
        w_up.reshape(shard, fsdp_size, ctx_size, cut_ff), ctx, 2, False
    ).reshape(shard, group_ff)
    down_send = lax.dynamic_index_in_dim(
        w_down.reshape(ctx_size, shard_ff // ctx_size, width), ctx, 0, False
    )
    merged = up_send.shape == down_send.shape and ctx_size == 4 and cut_ff % 128 == 0
    feed_sends = [jnp.concatenate([up_send, down_send], axis=1)] if merged else [up_send, down_send]
    feed_mine = [lax.all_gather(send, "fsdp", axis=0, tiled=True) for send in feed_sends]

    docs = doc_ids[:, 0].astype(bf16)
    doc_rows = jnp.pad(docs[:, None, :], ((0, 0), (0, PAD - 1), (0, width - tokens)))
    mine, theirs = (
        [lax.dynamic_index_in_dim(a, c, 0, False) for a in (inputs[:, 0], doc_rows, cotangent[:, 0])]
        for c in (core, 1 - core)
    )
    swapped = over_ctx(jnp.concatenate(theirs), 1)
    x_own = jnp.concatenate([mine[0], swapped[:tokens]])
    cot_own = jnp.concatenate([mine[2], swapped[tokens + PAD :]])
    doc_own = jnp.concatenate([mine[1][:1, :tokens], swapped[tokens : tokens + 1, :tokens]], axis=1)
    packed = jnp.concatenate([x_own, jnp.pad(doc_own, ((0, PAD - 1), (0, width - own_rows)))])
    rest = gather_tokens(packed).reshape(ways - 1, own_rows + PAD, width)
    x_rest = rest[:, :own_rows].reshape(rest_rows, width)
    doc_all = jnp.concatenate([doc_own[0], rest[:, own_rows, :own_rows].reshape(-1)]).astype(f32)
    key_docs, query_docs = doc_all[:, None], doc_all[None, :]
    time_row = lax.dynamic_index_in_dim(timestep[:, 0], core, 0, True).astype(f32)
    rounded0 = (jnp.concatenate([x_own, x_rest]).astype(f32) + time_row).astype(bf16)

    ratio = fsdp_size // ctx_size
    orders = [natural] + [
        ((natural // ratio) ^ who) * ratio + natural % ratio for who in (ctx, ctx ^ 1)
    ]
    w_qkv_mine, small_all, out_mine, out_theirs = place(first_pieces, orders, shard, columns)
    w_qkv_pair = (w_qkv_mine, over_ctx(w_qkv_mine, 1))
    small_all = small_all.reshape(fsdp_size, PAD * columns)[:, :small_count].astype(f32)
    starts = [0, bias_model.shape[0]]
    starts.append(starts[1] + bias_up.shape[0])
    starts.append(starts[2] + norm_gains.shape[0])
    starts.append(small_count)
    b_model, b_up, gains, shifts = (
        small_all[:, a:b].reshape(-1) for a, b in zip(starts[:-1], starts[1:])
    )
    vecs = jnp.stack(
        [
            time_row[0], b_model[2 * width : 3 * width], gains[:width], shifts[:width],
            b_model[3 * width :], gains[width:], shifts[width:], jnp.zeros((width,), f32),
        ]
    )
    b_up_groups = b_up.reshape(fsdp_size, ctx_size, cut_ff)

    b_up_pair = [
        lax.dynamic_index_in_dim(b_up_groups, ctx ^ i, 1, False).reshape(1, group_ff)
        for i in range(2)
    ]

    projected, attended, logs = [], [], []
    for i in range(2):
        who = ctx ^ i
        b_query = lax.dynamic_slice_in_dim(b_model, who * group, group)
        b_value = lax.dynamic_slice_in_dim(b_model, width + who * group, group)
        bias = jnp.concatenate([b_query, jnp.zeros_like(b_query), b_value])
        weights = after(w_qkv_pair[i], *attended, *b_up_pair, vecs, cot_own)
        proj = (dot(rounded0, weights) + bias[None]).astype(bf16)
        out, log = attend(proj, key_docs, query_docs, head_size)
        projected.append(proj)
        attended.append(out)
        logs.append(log)
    attended_pair = jnp.concatenate(attended, axis=1)
    attended_cols = [attended_pair[:own_rows]]
    for k in range(1, ways):
        attended_cols.append(over_ctx(attended_pair[k * own_rows : (k + 1) * own_rows], 2 * k))
    attended_own = jnp.concatenate(attended_cols, axis=1)

    out_other = over_ctx(out_theirs, 1)
    normal1, inverse1, normed_own = kernel_call(
        out_kernel,
        [shape((own_rows, width)), shape((own_rows, 1)), shape((own_rows, width), bf16)],
        [attended_own, out_mine, out_other, x_own, vecs],
        scalars=[core],
        scratch=[pltpu.VMEM((own_rows, width), f32)],
    )
    normed_rest = gather_tokens(normed_own)

    feed_mine = [after(w, normed_rest) for w in feed_mine]
    feed_pair = (feed_mine, [over_ctx(w, 1) for w in feed_mine])
    acts, slopes, feeds = {}, {}, {"rest": None, "own": None}
    token = normed_own
    for part, i in (("own", 0), ("rest", 0), ("rest", 1), ("own", 1)):
        rows = normed_own if part == "own" else normed_rest
        acts[part, i], slopes[part, i], feeds[part] = feed_forward(
            after(rows, token), feed_pair[i], b_up_pair[i], feeds[part],
            bf16 if i == 1 and part == "rest" else f32,
        )
        token = acts[part, i]
    feed_own, feed_got = reduce_tokens(feeds["own"], feeds["rest"])

    result_keep, result_send, d_hidden2, d_feed_own, sums2 = kernel_call(
        turn_kernel,
        [
            shape((tokens, width), bf16), shape((tokens, width), bf16), shape((own_rows, width)),
            shape((own_rows, width), bf16), shape((8, width)),
        ],
        [normal1, feed_own, feed_got, cot_own, vecs],
    )
    d_feed_rest = gather_tokens(d_feed_own)

    def gradient(args, flops=50_000_000_000):
        return kernel_call(grad_kernel, [shape((width, width), bf16)], args, flops=flops)[0]

    def split(kept, got):
        return kernel_call(
            functools.partial(grad_split_kernel, shard),
            [shape((fsdp_size // 2, shard, width), bf16)] * 2,
            [kept, got],
            scalars=[fsdp % 2],
        )

    sides = [[2 * k + p for k in range(fsdp_size // 2)] for p in range(2)]

    def finish(near, got):
        mixed = kernel_call(add_kernel, [shape(near.shape, bf16)], [near, got])[0]
        return mixed, lax.psum_scatter(
            mixed.reshape(-1, width), "fsdp", scatter_dimension=0, tiled=True,
            axis_index_groups=sides,
        )

    d_ups, d_up_sums, d_normed = {}, {}, {}
    token = d_feed_own
    for part, rows in (("own", d_feed_own), ("rest", d_feed_rest)):
        total = None
        if merged and part == "rest":
            down_args = [
                [acts["own", i], acts["rest", i], after(d_feed_own, token), d_feed_rest] for i in range(2)
            ]
            down_away = gradient(down_args[1])
            token = down_away
        for i in range(2):
            d_ups[part, i], d_up_sums[part, i], total = feed_backward(
                after(rows, token), feed_pair[i], slopes[part, i], total,
                bf16 if i == 1 and part == "rest" else f32,
            )
            token = d_ups[part, i]
        d_normed[part] = total
    dn_own, dn_got = reduce_tokens(d_normed["own"], d_normed["rest"])

    if merged:
        down_args[0][2] = after(d_feed_own, token)
        down_near, down_far = split(gradient(down_args[0]), over_ctx(down_away, 1))
        up_args = [
            [after(normed_own, down_far), normed_rest, d_ups["own", i], d_ups["rest", i]] for i in range(2)
        ]
        up_away = gradient(up_args[1], 0)
        up_near, up_far = split(gradient(up_args[0], 0), over_ctx(up_away, 1))
        dn_got = after(dn_got, up_far)
        down_got = over_fsdp(down_far, 1)
    else:
        totals = []
        for left, right in ((acts, None), (None, d_ups)):
            grads = []
            for i in range(2):
                one = jnp.concatenate([left["own", i], left["rest", i]]) if left else (
                    jnp.concatenate([normed_own, normed_rest])
                )
                two = jnp.concatenate([right["own", i], right["rest", i]]) if right else (
                    jnp.concatenate([d_feed_own, d_feed_rest])
                )
                grads.append(dot(one, two, ((0,), (0,))))
            mixed = (grads[0] + over_ctx(grads[1].astype(bf16), 1).astype(f32)).astype(bf16)
            totals.append(lax.psum_scatter(mixed, "fsdp", scatter_dimension=0, tiled=True))

    d_hidden1, d_branch, d_att_near, d_att_far, sums1 = kernel_call(
        branch_kernel,
        [
            shape((own_rows, width)), shape((own_rows, width), bf16),
            shape((own_rows, 2 * group), bf16), shape((own_rows, width - 2 * group), bf16),
            shape((8, width)),
        ],
        [d_hidden2, dn_own, dn_got, normal1, inverse1, out_mine, out_other, vecs],
        scalars=[core],
        flops=0,
    )
    if ways == 2:
        d_attended = [d_att_near, over_ctx(d_att_far, 2)]
    else:
        d_attended = [d_att_near] + [
            over_ctx(d_att_far[:, 2 * (k - 1) * group : 2 * k * group], 2 * k)
            for k in range(1, ways)
        ]

    d_projected = [None, None]
    for i in (1, 0):
        d_query, d_pair = attend_back(
            projected[i], d_attended, i * group, key_docs, query_docs, logs[i], head_size,
        )
        d_projected[i] = (d_query, d_pair)
        if i:
            if merged:
                down_mixed, down_total = finish(down_near, after(down_got, d_query))
                up_got = over_fsdp(after(up_far, down_mixed), 1)
                d_query = after(d_query, down_mixed)
            qkv_away = kernel_call(
                functools.partial(qkv_send_kernel, shard),
                [shape((fsdp_size, shard, columns), bf16)],
                [rounded0, d_query, d_pair],
            )[0]
            out_keep, out_away = kernel_call(
                out_grad_kernel,
                [shape((width, width // 2)), shape((width, width // 2), bf16)],
                [after(attended_own, qkv_away), d_branch],
                scalars=[jnp.stack([ctx, core])],
            )
            out_got = over_ctx(out_away, 1)
            for k in range(int(math.log2(ways))):
                half = out_keep.shape[1] // 2
                bit = (ctx >> (k + 1)) % 2
                if half % 128 == 0:
                    out_keep, out_away = kernel_call(
                        split_kernel, [shape((width, half)), shape((width, half), bf16)],
                        [out_keep, out_got], scalars=[bit],
                    )
                else:
                    both = (out_keep + out_got.astype(f32)).reshape(width, 2, half)
                    out_keep = lax.dynamic_index_in_dim(both, bit, 1, False)
                    out_away = lax.dynamic_index_in_dim(both, 1 - bit, 1, False).astype(bf16)
                out_got = over_ctx(out_away, 2 << k)
            d_attended[0] = after(d_attended[0], out_away)

    qkv_got = over_ctx(qkv_away, 1)
    keep_outs = [
        shape((fsdp_size // 2, shard + VEC, columns)),
        shape((fsdp_size // 2, shard + PAD, columns), bf16),
    ]
    quarter = out_keep.shape[1]
    if merged:
        near, far = kernel_call(
            functools.partial(qkv_vec_keep_kernel, shard),
            keep_outs,
            [
                rounded0, *d_projected[0], *d_projected[1], qkv_got, sums1, sums2,
                *(d_up_sums[part, i] for i in range(2) for part in ("own", "rest")),
            ],
            scalars=[jnp.stack([fsdp % 2, ctx])],
            scratch=[
                pltpu.VMEM((width, columns), f32), pltpu.VMEM((8, width), f32),
                pltpu.VMEM((8, hidden), f32), pltpu.VMEM((fsdp_size, VEC, columns), f32),
            ],
        )
    else:
        def in_groups(pair, size):
            stacked = jnp.stack(pair)
            ordered = jnp.where(core == 0, stacked, stacked[::-1])
            return lax.dynamic_update_slice_in_dim(
                jnp.zeros((ctx_size, size), f32), ordered, ctx - core, 0
            )

        column = lambda value: jnp.sum(value.astype(f32), axis=0)
        vec_query = in_groups([column(d[0]) for d in d_projected], group).reshape(-1)
        vec_value = in_groups([column(d[1][:, group:]) for d in d_projected], group).reshape(-1)
        vec_up = jnp.swapaxes(
            in_groups(
                [d_up_sums["own", i][0] + d_up_sums["rest", i][0] for i in range(2)], group_ff
            ).reshape(ctx_size, fsdp_size, cut_ff), 0, 1,
        ).reshape(fsdp_size, -1)
        vec_model = jnp.concatenate([vec_query, vec_value, sums1[2], sums2[2]]).reshape(fsdp_size, -1)
        vec_gain = jnp.concatenate([sums1[0], sums2[0]]).reshape(fsdp_size, -1)
        vec_shift = jnp.concatenate([sums1[1], sums2[1]]).reshape(fsdp_size, -1)
        vectors = jnp.concatenate([vec_model, vec_up, vec_gain, vec_shift], axis=1)
        vectors = jnp.pad(vectors, ((0, 0), (0, VEC * columns - small_count))).reshape(
            fsdp_size, VEC, columns
        )
        near, far = kernel_call(
            functools.partial(qkv_keep_kernel, shard),
            keep_outs,
            [rounded0, *d_projected[0], qkv_got, vectors],
            scalars=[fsdp % 2],
            scratch=[pltpu.VMEM((width, columns), f32)],
        )
    got = over_fsdp(far, 1)
    if merged:
        up_mixed, up_total = finish(up_near, after(up_got, far))
    out_near, out_far = kernel_call(
        functools.partial(out_keep_kernel, shard),
        [
            shape((fsdp_size // 2, shard, quarter)),
            shape((fsdp_size // 2, shard, quarter), bf16),
        ],
        [after(out_keep, far), out_got],
        scalars=[fsdp % 2],
    )
    out_cross = over_fsdp(out_far, 1)

    dx_own, dx_rest = kernel_call(
        input_kernel,
        [shape((own_rows, width)), shape((rest_rows, width), bf16)],
        [after(d_projected[0][0], out_far, got), d_projected[0][1], *d_projected[1], *w_qkv_pair],
    )
    if merged:
        got = after(got, up_mixed)
    sends = kernel_call(
        functools.partial(z_send_kernel, shard),
        [shape((shard + VEC, columns + quarter))]
        + [shape((shard + PAD, columns + quarter), bf16)] * (fsdp_size // 2 - 1),
        [near, got, out_near, out_cross],
        scalars=[fsdp // 2],
    )
    mine_block = sends[0]
    if merged:
        up_spread = over_ctx(up_total, 2)
        mine_block = after(mine_block, up_spread)
    total = kernel_call(
        functools.partial(z_sum_kernel, shard),
        [shape((shard + PAD, columns + quarter), bf16)],
        [mine_block, *(over_fsdp(value, 2 * k) for k, value in enumerate(sends[1:], 1))],
    )[0]

    dx_own, dx_got = reduce_tokens(dx_own, dx_rest)
    input_keep, input_send = kernel_call(
        input_sum_kernel, [shape((tokens, width))] * 2, [d_hidden1, dx_own, dx_got]
    )

    if merged:
        def quarters(own, far_own):
            return [own, over_ctx(own, 1), far_own, over_ctx(far_own, 1)]

        grad_down = kernel_call(
            functools.partial(rows_tail_kernel, shard),
            [shape((shard_ff, width))],
            quarters(down_total, over_ctx(after(down_total, up_mixed), 2)),
            scalars=[ctx],
        )[0]
        grad_up = kernel_call(
            functools.partial(columns_tail_kernel, cut_ff),
            [shape((shard, hidden))],
            quarters(up_total, up_spread),
            scalars=[ctx],
        )[0]
        grad_qkv, grad_out, vec_done = kernel_call(
            functools.partial(tail_kernel, shard, group),
            [shape((shard, 3 * width)), shape((shard, width)), shape((VEC, columns))],
            quarters(total, over_ctx(total, 2)),
            scalars=[ctx],
        )
        counts = [b - a for a, b in zip(starts[:-1], starts[1:])]
        vectors = [vec_done[row, :count] for row, count in enumerate(counts)]
    else:
        spread = lambda own: lax.all_gather(own, "ctx", axis=0)
        tail = spread(total)
        grad_qkv = jnp.transpose(
            tail[:, :shard, :columns].reshape(ctx_size, shard, 3, group), (1, 2, 0, 3)
        ).reshape(shard, 3 * width).astype(f32)
        order = []
        levels = int(math.log2(ctx_size))
        for place_index in range(ctx_size):
            order.append(
                sum(((place_index >> (levels - 1 - b)) & 1) << b for b in range(levels))
            )
        grad_out = jnp.concatenate([tail[d, :shard, columns:] for d in order], axis=1).astype(f32)
        vec = tail[:, shard:, :columns].astype(f32)
        vec_done = jnp.sum(vec[:, :VEC] + vec[:, VEC:], axis=0).reshape(-1)
        vectors = [vec_done[a:b] for a, b in zip(starts[:-1], starts[1:])]
        grad_down = spread(totals[0]).reshape(shard_ff, width).astype(f32)
        grad_up = jnp.transpose(
            spread(totals[1]).reshape(ctx_size, shard, fsdp_size, cut_ff), (1, 2, 0, 3)
        ).reshape(shard, hidden).astype(f32)

    def give_back(keep, send):
        got = over_ctx(send, 1)
        return jnp.stack([jnp.where(core == 0, keep, got), jnp.where(core == 0, got, keep)])

    block_output = give_back(result_keep, result_send)[:, None]
    input_grad = give_back(input_keep, input_send)[:, None]
    return (
        block_output, input_grad, grad_qkv, grad_out, grad_up, grad_down,
        *vectors,
    )


def solution(mesh):
    token = P(None, "fsdp", "ctx", None)
    rows = P("fsdp", None)
    flat = P("fsdp")
    return jax.shard_map(
        per_device,
        mesh=mesh,
        in_specs=(
            token, P(None, "fsdp", None), P(None, "fsdp", "ctx"), rows, rows, rows, rows,
            flat, flat, flat, flat, token,
        ),
        out_specs=(token, token, rows, rows, rows, rows, flat, flat, flat, flat),
        check_vma=False,
    )
```

```python
import functools
import math

import jax
import jax.numpy as jnp
from jax import lax
from jax.experimental import pallas as pl
from jax.experimental.pallas import tpu as pltpu
from jax.sharding import PartitionSpec as P

HEADS = 16
EPS = 1e-05
LOG2E = math.log2(math.e)
VEC = 8
PAD = 2 * VEC
f32 = jnp.float32
bf16 = jnp.bfloat16


def dot(left, right, dims=((1,), (0,))):
    return lax.dot_general(left, right, (dims, ((), ())), preferred_element_type=f32)


def over_ctx(value, mask):
    size = lax.axis_size("ctx")
    return lax.ppermute(value, "ctx", [(i, i ^ mask) for i in range(size)])


def over_fsdp(value, mask):
    size = lax.axis_size("fsdp")
    return lax.ppermute(value, "fsdp", [(i, i ^ mask) for i in range(size)])


def after(value, *others):
    return lax.optimization_barrier((value, *others))[0]


def shape(dims, dtype=f32):
    return jax.ShapeDtypeStruct(tuple(dims), dtype)


def kernel_call(body, outs, args, scalars=(), scratch=(), flops=30_000_000_000):
    scalars = [jnp.asarray(s, jnp.int32).reshape(-1) for s in scalars]
    specs = [pl.BlockSpec(memory_space=pltpu.SMEM)] * len(scalars)
    specs += [pl.BlockSpec(memory_space=pltpu.VMEM)] * len(args)
    largest = max(math.prod(a.shape) * 4 for a in [*args, *outs])
    held = sum(math.prod(a.shape) * jnp.dtype(a.dtype).itemsize for a in scratch)
    limit = min(held + max(6 * 2**20, 2 * largest), 56 * 2**20)
    return pl.pallas_call(
        body,
        in_specs=specs,
        out_specs=[pl.BlockSpec(memory_space=pltpu.VMEM)] * len(outs),
        out_shape=list(outs),
        scratch_shapes=list(scratch),
        compiler_params=pltpu.CompilerParams(vmem_limit_bytes=limit),
        cost_estimate=pl.CostEstimate(flops=flops, bytes_accessed=1024, transcendentals=0),
    )(*scalars, *args)


def attend_kernel(head_size, scale, block_ref, whole_ref, key_doc_ref, query_doc_ref, out_ref, log_ref):
    width = out_ref.shape[1]
    same = key_doc_ref[...] == query_doc_ref[...]
    for head in range(width // head_size):
        cut = head * head_size
        query = block_ref[:, cut : cut + head_size]
        key = whole_ref[:, width + cut : width + cut + head_size]
        value = whole_ref[:, 2 * width + cut : 2 * width + cut + head_size]
        scores = jnp.where(same, dot(key, query, ((1,), (1,))), -1e30)
        top = jnp.max(scores, axis=0, keepdims=True)
        expo = jnp.exp2((scores - top) * (scale * LOG2E))
        total = jnp.sum(expo, axis=0, keepdims=True)
        probs = (expo * (1.0 / total)).astype(bf16)
        out_ref[:, cut : cut + head_size] = dot(value, probs, ((0,), (0,))).T.astype(bf16)
        log_ref[head : head + 1, :] = top * (scale * LOG2E) + jnp.log2(total)


def attend(projected, key_docs, query_docs, head_size):
    length, width = projected.shape[0], projected.shape[1] // 3
    heads = width // head_size
    block = min(512, length)
    return pl.pallas_call(
        functools.partial(attend_kernel, head_size, 1.0 / math.sqrt(head_size)),
        grid=(length // block,),
        in_specs=[
            pl.BlockSpec((block, 3 * width), lambda i: (i, 0)),
            pl.BlockSpec((length, 3 * width), lambda i: (0, 0)),
            pl.BlockSpec((length, 1), lambda i: (0, 0)),
            pl.BlockSpec((1, block), lambda i: (0, i)),
        ],
        out_specs=[
            pl.BlockSpec((block, width), lambda i: (i, 0)),
            pl.BlockSpec((heads, block), lambda i: (0, i)),
        ],
        out_shape=[shape((length, width), bf16), shape((heads, length))],
        compiler_params=pltpu.CompilerParams(vmem_limit_bytes=(24 if length <= 512 else 48) * 2**20),
        cost_estimate=pl.CostEstimate(
            flops=0, bytes_accessed=1024, transcendentals=0,
        ),
    )(projected, projected, key_docs, query_docs)


def attend_back_kernel(head_size, scale, steps, first, pieces, *refs):
    block_ref, whole_ref, key_doc_ref, query_doc_ref, log_ref = refs[:5]
    grad_refs, (query_out, pair_out, pair_sum) = refs[5 : 5 + pieces], refs[5 + pieces :]
    width = query_out.shape[1]
    step = pl.program_id(0)
    same = key_doc_ref[...] == query_doc_ref[...]

    if steps > 1:
        @pl.when(step == 0)
        def _():
            pair_sum[...] = jnp.zeros_like(pair_sum)

    def add(place, value):
        if steps > 1:
            pair_sum[:, place : place + head_size] += value
        else:
            pair_out[:, place : place + head_size] = value.astype(bf16)

    for head in range(width // head_size):
        cut = head * head_size
        query = block_ref[:, cut : cut + head_size]
        key = whole_ref[:, width + cut : width + cut + head_size]
        value = whole_ref[:, 2 * width + cut : 2 * width + cut + head_size]
        span = slice(first + cut, first + cut + head_size)
        grad = jnp.concatenate([ref[:, span] for ref in grad_refs]) if pieces > 1 else grad_refs[0][:, span]
        scores = dot(key, query, ((1,), (1,)))
        probs = jnp.where(
            same, jnp.exp2(scores * (scale * LOG2E) - log_ref[head : head + 1, :]), 0.0
        )
        d_probs = dot(value, grad, ((1,), (1,)))
        inner = jnp.sum(probs * d_probs, axis=0, keepdims=True)
        d_scores = (probs * (d_probs - inner)).astype(bf16)
        query_out[:, cut : cut + head_size] = (
            dot(key, d_scores, ((0,), (0,))).T * scale
        ).astype(bf16)
        add(cut, dot(d_scores, query) * scale)
        add(width + cut, dot(probs.astype(bf16), grad))

    if steps > 1:
        @pl.when(step == steps - 1)
        def _():
            pair_out[...] = pair_sum[...].astype(bf16)


def attend_back(projected, grads, first, key_docs, query_docs, logs, head_size):
    length, width = projected.shape[0], projected.shape[1] // 3
    heads = width // head_size
    block = min(512, length)
    steps = length // block
    if steps > 1:
        grads = [jnp.concatenate(grads)]
    grad_rows = [grad.shape[0] // steps for grad in grads]
    return pl.pallas_call(
        functools.partial(
            attend_back_kernel, head_size, 1.0 / math.sqrt(head_size), steps, first, len(grads)
        ),
        grid=(steps,),
        in_specs=[
            pl.BlockSpec((block, 3 * width), lambda i: (i, 0)),
            pl.BlockSpec((length, 3 * width), lambda i: (0, 0)),
            pl.BlockSpec((length, 1), lambda i: (0, 0)),
            pl.BlockSpec((1, block), lambda i: (0, i)),
            pl.BlockSpec((heads, block), lambda i: (0, i)),
        ]
        + [pl.BlockSpec((rows, grads[0].shape[1]), lambda i: (i, 0)) for rows in grad_rows],
        out_specs=[
            pl.BlockSpec((block, width), lambda i: (i, 0)),
            pl.BlockSpec((length, 2 * width), lambda i: (0, 0)),
        ],
        out_shape=[shape((length, width), bf16), shape((length, 2 * width), bf16)],
        scratch_shapes=[pltpu.VMEM((length if steps > 1 else 8, 2 * width), f32)],
        compiler_params=pltpu.CompilerParams(vmem_limit_bytes=(24 if length <= 512 else 56) * 2**20),
        cost_estimate=pl.CostEstimate(flops=0, bytes_accessed=1024, transcendentals=0),
    )(projected, projected, key_docs, query_docs, logs, *grads)


def place_kernel(count, rows, columns, where_ref, *refs):
    pieces, (qkv_ref, small_ref, mine_ref, theirs_ref) = refs[:count], refs[count:]
    for j, piece in enumerate(pieces):
        spare = piece.shape[0] - rows
        start = pl.multiple_of(where_ref[j] * rows, rows)
        qkv_ref[pl.ds(start, rows), :] = piece[:rows, :columns]
        start = pl.multiple_of(where_ref[j] * spare, spare)
        small_ref[pl.ds(start, spare), :] = piece[rows:, :columns]
        for way, ref in enumerate((mine_ref, theirs_ref), 1):
            start = pl.multiple_of(where_ref[way * count + j] * rows, rows)
            ref[pl.ds(start, rows), :] = piece[:rows, columns:]


def place(pieces, orders, rows, columns):
    count, spare = len(pieces), pieces[0].shape[0] - rows
    rest = pieces[0].shape[1] - columns
    return kernel_call(
        functools.partial(place_kernel, count, rows, columns),
        [
            shape((count * rows, columns), bf16), shape((count * spare, columns), bf16),
            shape((count * rows, rest), bf16), shape((count * rows, rest), bf16),
        ],
        pieces,
        scalars=[jnp.concatenate(orders)],
    )


def gather_near(shard):
    size = lax.axis_size("fsdp")
    return [shard] + [over_fsdp(shard, 2 * k) for k in range(1, size // 2)]


def gather_far(near):
    pieces = []
    for value in near:
        pieces += [value, over_fsdp(value, 1)]
    return pieces


def gather_tokens(own):
    have, mask = own, 1
    while 2 * mask < lax.axis_size("ctx"):
        got = over_ctx(have, 2 * mask)
        if lax.axis_size("ctx") == 4:
            return got
        have = jnp.concatenate([have, got])
        mask *= 2
    return have[own.shape[0] :]


def reduce_tokens(own, rest):
    ways = lax.axis_size("ctx") // 2
    if ways == 2:
        return own, over_ctx(rest, 2)
    have, mask = jnp.concatenate([own, rest.astype(f32)]), ways // 2
    while mask > 1:
        half = have.shape[0] // 2
        have = have[:half] + over_ctx(have[half:].astype(bf16), 2 * mask).astype(f32)
        mask //= 2
    half = have.shape[0] // 2
    return have[:half], over_ctx(have[half:].astype(bf16), 2)


def norm_parts(value):
    centred = value - jnp.mean(value, axis=-1, keepdims=True)
    inverse = lax.rsqrt(jnp.mean(centred * centred, axis=-1, keepdims=True) + EPS)
    return centred * inverse, inverse


def norm_back(grad, normal, inverse, gain):
    inner = grad * gain
    return inverse * (
        inner
        - jnp.mean(inner, axis=-1, keepdims=True)
        - normal * jnp.mean(inner * normal, axis=-1, keepdims=True)
    )


def column_sums(*values):
    rows = [jnp.sum(value, axis=0, keepdims=True) for value in values]
    return jnp.concatenate(rows + [jnp.zeros_like(rows[0])] * (8 - len(rows)))


def out_kernel(
    core_ref, att_ref, mine_ref, other_ref, x_ref, vec_ref, normal_ref, inverse_ref, normed_ref, hidden_ref
):
    half = mine_ref.shape[1]
    core = core_ref[0]
    for way, ref in ((core, mine_ref), (1 - core, other_ref)):
        hidden_ref[:, pl.ds(pl.multiple_of(way * half, half), half)] = dot(att_ref[...], ref[...])
    hidden1 = hidden_ref[...] + (x_ref[...].astype(f32) + vec_ref[0:1, :]) + vec_ref[1:2, :]
    normal, inverse = norm_parts(hidden1)
    normal_ref[...] = normal
    inverse_ref[...] = inverse
    normed_ref[...] = (normal * vec_ref[2:3, :] + vec_ref[3:4, :]).astype(bf16)


def views(refs, width):
    if len(refs) == 2:
        return refs
    return refs[0].at[:, : refs[0].shape[1] - width], refs[0].at[:, refs[0].shape[1] - width :]


def forward_kernel(count, first, rows_ref, bias_ref, *refs):
    up_ref, down_ref = views(refs[:count], rows_ref.shape[1])
    act_ref, slope_ref, feed_ref = refs[-3:]
    upward = dot(rows_ref[...], up_ref[...]) + bias_ref[...]
    lower = 0.5 + 0.5 * lax.erf(upward * math.sqrt(0.5))
    density = jnp.exp2(upward * upward * (-0.5 * LOG2E)) * (1.0 / math.sqrt(2.0 * math.pi))
    act = (upward * lower).astype(bf16)
    act_ref[...] = act
    slope_ref[...] = lower + upward * density
    feed = dot(act, down_ref[...])
    if not first:
        feed = feed + refs[count][...]
    feed_ref[...] = feed.astype(feed_ref.dtype)


def feed_forward(rows, weights, bias, feed, dtype):
    count, group_ff = rows.shape[0], bias.shape[1]
    return kernel_call(
        functools.partial(forward_kernel, len(weights), feed is None),
        [shape((count, group_ff), bf16), shape((count, group_ff)), shape(rows.shape, dtype)],
        [rows, bias, *weights] + ([] if feed is None else [feed]),
    )


def backward_kernel(count, first, rows_ref, slope_ref, *refs):
    up_ref, down_ref = views(refs[:count], rows_ref.shape[1])
    d_up_ref, sum_ref, total_ref = refs[-3:]
    d_up = (dot(rows_ref[...], down_ref[...], ((1,), (1,))) * slope_ref[...]).astype(bf16)
    d_up_ref[...] = d_up
    sum_ref[...] = column_sums(d_up.astype(f32))
    total = dot(d_up, up_ref[...], ((1,), (1,)))
    if not first:
        total = total + refs[count][...]
    total_ref[...] = total.astype(total_ref.dtype)


def feed_backward(rows, weights, slope, total, dtype):
    count, group_ff = slope.shape
    return kernel_call(
        functools.partial(backward_kernel, len(weights), total is None),
        [shape((count, group_ff), bf16), shape((8, group_ff)), shape(rows.shape, dtype)],
        [rows, slope, *weights] + ([] if total is None else [total]),
    )


def turn_kernel(
    normal_ref, feed_ref, got_ref, cot_ref, vec_ref, keep_ref, send_ref, d_hidden_ref, d_feed_ref, sum_ref
):
    normed1 = normal_ref[...] * vec_ref[2:3, :] + vec_ref[3:4, :]
    hidden2 = normed1 + (feed_ref[...] + got_ref[...].astype(f32) + vec_ref[4:5, :])
    normal, inverse = norm_parts(hidden2)
    gain = vec_ref[5:6, :]
    result = (normal * gain + vec_ref[6:7, :]).astype(bf16)
    keep_ref[...] = result[: keep_ref.shape[0]]
    send_ref[...] = result[keep_ref.shape[0] :]
    cot = cot_ref[...].astype(f32)
    d_hidden2 = norm_back(cot, normal, inverse, gain)
    d_hidden_ref[...] = d_hidden2
    d_feed = d_hidden2.astype(bf16)
    d_feed_ref[...] = d_feed
    sum_ref[...] = column_sums(cot * normal, cot, d_feed.astype(f32))


def branch_kernel(
    core_ref, d_hidden2_ref, own_ref, got_ref, normal_ref, inverse_ref, mine_ref, other_ref, vec_ref,
    d_hidden1_ref, d_branch_ref, near_ref, far_ref, sum_ref,
):
    core, half, near = core_ref[0], mine_ref.shape[1], near_ref.shape[1]
    d_normed = d_hidden2_ref[...] + (own_ref[...] + got_ref[...].astype(f32))
    normal = normal_ref[...]
    d_hidden1 = norm_back(d_normed, normal, inverse_ref[...], vec_ref[2:3, :])
    d_hidden1_ref[...] = d_hidden1
    d_branch = d_hidden1.astype(bf16)
    d_branch_ref[...] = d_branch
    first = d_branch_ref[:, pl.ds(pl.multiple_of(core * half, half), half)]
    second = d_branch_ref[:, pl.ds(pl.multiple_of((1 - core) * half, half), half)]
    for ref, start in ((far_ref, near), (near_ref, 0)):
        span = slice(start, start + ref.shape[1])
        ref[...] = (
            dot(first, mine_ref[span, :], ((1,), (1,)))
            + dot(second, other_ref[span, :], ((1,), (1,)))
        ).astype(bf16)
    sum_ref[...] = column_sums(d_normed * normal, d_normed, d_branch.astype(f32))


def grad_kernel(one_ref, two_ref, left_ref, right_ref, out_ref):
    out_ref[...] = (
        dot(one_ref[...], left_ref[...], ((0,), (0,))) + dot(two_ref[...], right_ref[...], ((0,), (0,)))
    ).astype(bf16)


def grad_split_kernel(shard, odd_ref, keep_ref, got_ref, near_ref, far_ref):
    odd = odd_ref[0]
    for parity, ref in ((1 - odd, far_ref), (odd, near_ref)):
        for j in range(ref.shape[0]):
            rows = pl.ds(pl.multiple_of((2 * j + parity) * shard, shard), shard)
            ref[j] = (keep_ref[rows, :].astype(f32) + got_ref[rows, :].astype(f32)).astype(bf16)


def add_kernel(near_ref, got_ref, out_ref):
    out_ref[...] = (near_ref[...].astype(f32) + got_ref[...].astype(f32)).astype(out_ref.dtype)


def out_grad_kernel(ctx_ref, att_ref, d_branch_ref, keep_ref, send_ref):
    ctx = ctx_ref[0]
    core = ctx_ref[1]
    group, half = ctx_ref_group(att_ref, keep_ref), keep_ref.shape[1]
    for way, ref in ((core, keep_ref), (1 - core, send_ref)):
        columns = d_branch_ref[:, pl.ds(pl.multiple_of(way * half, half), half)]
        grad = dot(att_ref[...], columns, ((0,), (0,)))
        for i in range(grad.shape[0] // group):
            start = pl.multiple_of((ctx ^ i) * group, group)
            ref[pl.ds(start, group), :] = grad[i * group : (i + 1) * group].astype(ref.dtype)


def ctx_ref_group(att_ref, keep_ref):
    return att_ref.shape[1] // lax.axis_size("ctx")


def split_kernel(bit_ref, keep_ref, got_ref, kept_ref, send_ref):
    half = kept_ref.shape[1]
    for way, ref in ((bit_ref[0], kept_ref), (1 - bit_ref[0], send_ref)):
        span = pl.ds(pl.multiple_of(way * half, half), half)
        ref[...] = (keep_ref[:, span] + got_ref[:, span].astype(f32)).astype(ref.dtype)


def pack(values):
    high = values.astype(bf16)
    return jnp.concatenate([high, (values - high.astype(f32)).astype(bf16)])


def unpack(rows):
    return rows[:VEC].astype(f32) + rows[VEC:].astype(f32)


def qkv_send_kernel(shard, r0_ref, dq_ref, dkv_ref, out_ref):
    width = dq_ref.shape[1]
    query = dot(r0_ref[...], dq_ref[...], ((0,), (0,)))
    pair = dot(r0_ref[...], dkv_ref[...], ((0,), (0,)))
    for block in range(out_ref.shape[0]):
        rows = slice(block * shard, (block + 1) * shard)
        out_ref[block, :, :width] = query[rows].astype(bf16)
        out_ref[block, :, width:] = pair[rows].astype(bf16)


def split_by_parity(shard, odd, grad_ref, got_ref, vec_ref, near_ref, far_ref):
    for parity, ref in ((1 - odd, far_ref), (odd, near_ref)):
        for j in range(ref.shape[0]):
            block = 2 * j + parity
            rows = pl.ds(pl.multiple_of(block * shard, shard), shard)
            ref[j, :shard] = (grad_ref[rows, :] + got_ref[block].astype(f32)).astype(ref.dtype)
            vec = vec_ref[block]
            ref[j, shard:] = vec if ref.dtype == f32 else pack(vec)


def qkv_keep_kernel(
    shard, odd_ref, r0_ref, dq_ref, dkv_ref, got_ref, vec_ref, near_ref, far_ref, grad_ref
):
    width = dq_ref.shape[1]
    grad_ref[:, :width] = dot(r0_ref[...], dq_ref[...], ((0,), (0,)))
    grad_ref[:, width:] = dot(r0_ref[...], dkv_ref[...], ((0,), (0,)))
    split_by_parity(shard, odd_ref[0], grad_ref, got_ref, vec_ref, near_ref, far_ref)


def qkv_vec_keep_kernel(
    shard, place_ref, r0_ref, dq_ref, dkv_ref, dq_other_ref, dkv_other_ref, got_ref, sums1_ref, sums2_ref,
    up_own_ref, up_rest_ref, up_own_other_ref, up_rest_other_ref, near_ref, far_ref, grad_ref, flat_ref,
    up_ref, vec_ref,
):
    odd, ctx = place_ref[0], place_ref[1]
    width = dq_ref.shape[1]
    size = vec_ref.shape[0]
    flat_ref[...] = jnp.zeros_like(flat_ref)
    up_ref[...] = jnp.zeros_like(up_ref)
    vec_ref[...] = jnp.zeros_like(vec_ref)
    cut = up_own_ref.shape[1] // size
    pairs = (
        (dq_ref, dkv_ref, up_own_ref, up_rest_ref),
        (dq_other_ref, dkv_other_ref, up_own_other_ref, up_rest_other_ref),
    )
    for i, (query, pair, own, rest) in enumerate(pairs):
        who = ctx ^ i
        span = pl.ds(pl.multiple_of(who * width, width), width)
        flat_ref[0:1, span] = jnp.sum(query[...].astype(f32), axis=0, keepdims=True)
        flat_ref[1:2, span] = jnp.sum(pair[:, width:].astype(f32), axis=0, keepdims=True)
        for f in range(size):
            start = pl.multiple_of((f * (up_ref.shape[1] // cut // size) + who) * cut, cut)
            here = slice(f * cut, (f + 1) * cut)
            up_ref[0:1, pl.ds(start, cut)] = own[0:1, here] + rest[0:1, here]
    full = flat_ref.shape[1]
    model = (flat_ref[0:1], flat_ref[1:2], sums1_ref[2:3], sums2_ref[2:3])
    rows = (model, (up_ref[0:1],), (sums1_ref[0:1], sums2_ref[0:1]), (sums1_ref[1:2], sums2_ref[1:2]))
    for row, sources in enumerate(rows):
        length = sources[0].shape[1]
        part = len(sources) * length // size
        for f in range(size):
            source, start = sources[f * part // length], f * part % length
            vec_ref[f, row : row + 1, :part] = source[:, start : start + part]
    grad_ref[:, :width] = dot(r0_ref[...], dq_ref[...], ((0,), (0,)))
    grad_ref[:, width:] = dot(r0_ref[...], dkv_ref[...], ((0,), (0,)))
    split_by_parity(shard, odd, grad_ref, got_ref, vec_ref, near_ref, far_ref)


def input_kernel(dq_ref, dkv_ref, dq_other_ref, dkv_other_ref, mine_ref, other_ref, own_ref, rest_ref):
    width = dq_ref.shape[1]
    cut = own_ref.shape[0]
    for ref, rows in ((rest_ref, slice(cut, dq_ref.shape[0])), (own_ref, slice(0, cut))):
        total = 0.0
        for query, pair, weights in (
            (dq_ref, dkv_ref, mine_ref), (dq_other_ref, dkv_other_ref, other_ref)
        ):
            total = total + dot(query[rows, :], weights[:, :width], ((1,), (1,)))
            total = total + dot(pair[rows, :], weights[:, width:], ((1,), (1,)))
        ref[...] = total.astype(ref.dtype)


def input_sum_kernel(one_ref, two_ref, got_ref, keep_ref, send_ref):
    total = one_ref[...] + (two_ref[...] + got_ref[...].astype(f32))
    keep_ref[...] = total[: keep_ref.shape[0]]
    send_ref[...] = total[keep_ref.shape[0] :]


def out_keep_kernel(shard, odd_ref, keep_ref, got_ref, near_ref, far_ref):
    odd = odd_ref[0]
    for parity, ref in ((1 - odd, far_ref), (odd, near_ref)):
        for j in range(ref.shape[0]):
            rows = pl.ds(pl.multiple_of((2 * j + parity) * shard, shard), shard)
            ref[j] = (keep_ref[rows, :] + got_ref[rows, :].astype(f32)).astype(ref.dtype)


def z_send_kernel(shard, z_ref, near_ref, got_ref, out_near_ref, out_got_ref, *outs):
    z = z_ref[0]
    columns = near_ref.shape[2]
    for k, ref in enumerate(outs):
        block = z ^ k
        got = got_ref[block]
        near = near_ref[block]
        ref[:shard, :columns] = (near[:shard] + got[:shard].astype(f32)).astype(ref.dtype)
        ref[:shard, columns:] = (
            out_near_ref[block] + out_got_ref[block].astype(f32)
        ).astype(ref.dtype)
        vec = near[shard:] + unpack(got[shard:])
        ref[shard:, :columns] = vec if ref.dtype == f32 else pack(vec)
        ref[shard:, columns:] = jnp.zeros_like(ref[shard:, columns:])


def z_sum_kernel(shard, mine_ref, *refs):
    gots, out_ref = refs[:-1], refs[-1]
    value, vec = mine_ref[:shard], mine_ref[shard:]
    for ref in gots:
        value = value + ref[:shard].astype(f32)
        vec = vec + unpack(ref[shard:])
    out_ref[:shard] = value.astype(bf16)
    out_ref[shard:] = pack(vec)


def tail_kernel(shard, group, ctx_ref, *refs):
    pieces, (qkv_ref, out_ref, vec_ref) = refs[:4], refs[4:]
    ctx = ctx_ref[0]
    width = 4 * group
    for i, piece in enumerate(pieces):
        who = ctx ^ i
        for third in range(3):
            start = pl.multiple_of(third * width + who * group, group)
            qkv_ref[:, pl.ds(start, group)] = piece[
                :shard, third * group : (third + 1) * group
            ].astype(f32)
        start = pl.multiple_of(((who % 2) * 2 + who // 2) * group, group)
        out_ref[:, pl.ds(start, group)] = piece[:shard, 3 * group :].astype(f32)
    vec = [unpack(piece[shard:, : 3 * group]) for piece in pieces]
    vec_ref[...] = (vec[0] + vec[1]) + (vec[2] + vec[3])


def rows_tail_kernel(rows, ctx_ref, *refs):
    pieces, out_ref = refs[:-1], refs[-1]
    for i, piece in enumerate(pieces):
        start = pl.multiple_of((ctx_ref[0] ^ i) * rows, rows)
        out_ref[pl.ds(start, rows), :] = piece[...].astype(f32)


def columns_tail_kernel(cut, ctx_ref, *refs):
    pieces, out_ref = refs[:-1], refs[-1]
    for i, piece in enumerate(pieces):
        for block in range(piece.shape[1] // cut):
            start = pl.multiple_of((block * len(pieces) + (ctx_ref[0] ^ i)) * cut, cut)
            out_ref[:, pl.ds(start, cut)] = piece[:, block * cut : (block + 1) * cut].astype(f32)


def per_device(
    inputs, timestep, doc_ids, w_qkv, w_out, w_up, w_down, bias_model, bias_up,
    norm_gains, norm_shifts, cotangent,
):
    ctx, ctx_size = lax.axis_index("ctx"), lax.axis_size("ctx")
    fsdp, fsdp_size = lax.axis_index("fsdp"), lax.axis_size("fsdp")
    core, ways = ctx % 2, ctx_size // 2
    tokens, width = inputs.shape[2], w_out.shape[1]
    hidden = w_up.shape[1]
    head_size = width // HEADS
    own_rows = 2 * tokens
    rest_rows = (ways - 1) * own_rows
    group = width // ctx_size
    columns = 3 * group
    group_ff = hidden // ctx_size
    shard = w_out.shape[0]
    shard_ff = w_down.shape[0]
    cut_ff = hidden // (fsdp_size * ctx_size)
    fsdp_range = jnp.arange(fsdp_size)
    natural = fsdp_range ^ fsdp

    small = jnp.concatenate([bias_model, bias_up, norm_gains, norm_shifts])
    small_count = small.shape[0]
    qkv_group = lax.dynamic_index_in_dim(
        w_qkv.reshape(shard, 3, ctx_size, group), ctx, 2, False
    ).reshape(shard, columns)
    small_rows = jnp.pad(small, (0, PAD * columns - small_count)).reshape(PAD, columns)
    out_send = lax.dynamic_index_in_dim(w_out.reshape(shard, 2, width // 2), core, 1, False)
    first_send = jnp.concatenate(
        [
            jnp.concatenate([qkv_group, small_rows]),
            jnp.concatenate([out_send, jnp.zeros((PAD, width // 2), bf16)]),
        ],
        axis=1,
    )
    first_pieces = gather_far(gather_near(first_send))
    up_send = lax.dynamic_index_in_dim(
        w_up.reshape(shard, fsdp_size, ctx_size, cut_ff), ctx, 2, False
    ).reshape(shard, group_ff)
    down_send = lax.dynamic_index_in_dim(
        w_down.reshape(ctx_size, shard_ff // ctx_size, width), ctx, 0, False
    )
    merged = up_send.shape == down_send.shape and ctx_size == 4 and cut_ff % 128 == 0
    feed_sends = [jnp.concatenate([up_send, down_send], axis=1)] if merged else [up_send, down_send]
    feed_mine = [lax.all_gather(send, "fsdp", axis=0, tiled=True) for send in feed_sends]

    docs = doc_ids[:, 0].astype(bf16)
    doc_rows = jnp.pad(docs[:, None, :], ((0, 0), (0, PAD - 1), (0, width - tokens)))
    mine, theirs = (
        [lax.dynamic_index_in_dim(a, c, 0, False) for a in (inputs[:, 0], doc_rows, cotangent[:, 0])]
        for c in (core, 1 - core)
    )
    swapped = over_ctx(jnp.concatenate(theirs), 1)
    x_own = jnp.concatenate([mine[0], swapped[:tokens]])
    cot_own = jnp.concatenate([mine[2], swapped[tokens + PAD :]])
    doc_own = jnp.concatenate([mine[1][:1, :tokens], swapped[tokens : tokens + 1, :tokens]], axis=1)
    packed = jnp.concatenate([x_own, jnp.pad(doc_own, ((0, PAD - 1), (0, width - own_rows)))])
    rest = gather_tokens(packed).reshape(ways - 1, own_rows + PAD, width)
    x_rest = rest[:, :own_rows].reshape(rest_rows, width)
    doc_all = jnp.concatenate([doc_own[0], rest[:, own_rows, :own_rows].reshape(-1)]).astype(f32)
    key_docs, query_docs = doc_all[:, None], doc_all[None, :]
    time_row = lax.dynamic_index_in_dim(timestep[:, 0], core, 0, True).astype(f32)
    rounded0 = (jnp.concatenate([x_own, x_rest]).astype(f32) + time_row).astype(bf16)

    ratio = fsdp_size // ctx_size
    orders = [natural] + [
        ((natural // ratio) ^ who) * ratio + natural % ratio for who in (ctx, ctx ^ 1)
    ]
    w_qkv_mine, small_all, out_mine, out_theirs = place(first_pieces, orders, shard, columns)
    w_qkv_pair = (w_qkv_mine, over_ctx(w_qkv_mine, 1))
    small_all = small_all.reshape(fsdp_size, PAD * columns)[:, :small_count].astype(f32)
    starts = [0, bias_model.shape[0]]
    starts.append(starts[1] + bias_up.shape[0])
    starts.append(starts[2] + norm_gains.shape[0])
    starts.append(small_count)
    b_model, b_up, gains, shifts = (
        small_all[:, a:b].reshape(-1) for a, b in zip(starts[:-1], starts[1:])
    )
    vecs = jnp.stack(
        [
            time_row[0], b_model[2 * width : 3 * width], gains[:width], shifts[:width],
            b_model[3 * width :], gains[width:], shifts[width:], jnp.zeros((width,), f32),
        ]
    )
    b_up_groups = b_up.reshape(fsdp_size, ctx_size, cut_ff)

    b_up_pair = [
        lax.dynamic_index_in_dim(b_up_groups, ctx ^ i, 1, False).reshape(1, group_ff)
        for i in range(2)
    ]

    projected, attended, logs = [], [], []
    for i in range(2):
        who = ctx ^ i
        b_query = lax.dynamic_slice_in_dim(b_model, who * group, group)
        b_value = lax.dynamic_slice_in_dim(b_model, width + who * group, group)
        bias = jnp.concatenate([b_query, jnp.zeros_like(b_query), b_value])
        weights = after(w_qkv_pair[i], *attended, *b_up_pair, vecs, cot_own)
        proj = (dot(rounded0, weights) + bias[None]).astype(bf16)
        out, log = attend(proj, key_docs, query_docs, head_size)
        projected.append(proj)
        attended.append(out)
        logs.append(log)
    attended_pair = jnp.concatenate(attended, axis=1)
    attended_cols = [attended_pair[:own_rows]]
    for k in range(1, ways):
        attended_cols.append(over_ctx(attended_pair[k * own_rows : (k + 1) * own_rows], 2 * k))
    attended_own = jnp.concatenate(attended_cols, axis=1)

    out_other = over_ctx(out_theirs, 1)
    normal1, inverse1, normed_own = kernel_call(
        out_kernel,
        [shape((own_rows, width)), shape((own_rows, 1)), shape((own_rows, width), bf16)],
        [attended_own, out_mine, out_other, x_own, vecs],
        scalars=[core],
        scratch=[pltpu.VMEM((own_rows, width), f32)],
    )
    normed_rest = gather_tokens(normed_own)

    feed_mine = [after(w, normed_rest) for w in feed_mine]
    feed_pair = (feed_mine, [over_ctx(w, 1) for w in feed_mine])
    acts, slopes, feeds = {}, {}, {"rest": None, "own": None}
    token = normed_own
    for part, i in (("own", 0), ("rest", 0), ("rest", 1), ("own", 1)):
        rows = normed_own if part == "own" else normed_rest
        acts[part, i], slopes[part, i], feeds[part] = feed_forward(
            after(rows, token), feed_pair[i], b_up_pair[i], feeds[part],
            bf16 if i == 1 and part == "rest" else f32,
        )
        token = acts[part, i]
    feed_own, feed_got = reduce_tokens(feeds["own"], feeds["rest"])

    result_keep, result_send, d_hidden2, d_feed_own, sums2 = kernel_call(
        turn_kernel,
        [
            shape((tokens, width), bf16), shape((tokens, width), bf16), shape((own_rows, width)),
            shape((own_rows, width), bf16), shape((8, width)),
        ],
        [normal1, feed_own, feed_got, cot_own, vecs],
    )
    d_feed_rest = gather_tokens(d_feed_own)

    def gradient(args, flops=30_000_000_000):
        return kernel_call(grad_kernel, [shape((width, width), bf16)], args, flops=flops)[0]

    def split(kept, got):
        return kernel_call(
            functools.partial(grad_split_kernel, shard),
            [shape((fsdp_size // 2, shard, width), bf16)] * 2,
            [kept, got],
            scalars=[fsdp % 2],
        )

    sides = [[2 * k + p for k in range(fsdp_size // 2)] for p in range(2)]

    def finish(near, got):
        mixed = kernel_call(add_kernel, [shape(near.shape, bf16)], [near, got])[0]
        return mixed, lax.psum_scatter(
            mixed.reshape(-1, width), "fsdp", scatter_dimension=0, tiled=True,
            axis_index_groups=sides,
        )

    d_ups, d_up_sums, d_normed = {}, {}, {}
    token = d_feed_own
    for part, rows in (("own", d_feed_own), ("rest", d_feed_rest)):
        total = None
        if merged and part == "rest":
            down_args = [
                [acts["own", i], acts["rest", i], after(d_feed_own, token), d_feed_rest] for i in range(2)
            ]
            down_away = gradient(down_args[1])
            token = down_away
        for i in range(2):
            d_ups[part, i], d_up_sums[part, i], total = feed_backward(
                after(rows, token), feed_pair[i], slopes[part, i], total,
                bf16 if i == 1 and part == "rest" else f32,
            )
            token = d_ups[part, i]
        d_normed[part] = total
    dn_own, dn_got = reduce_tokens(d_normed["own"], d_normed["rest"])

    if merged:
        down_args[0][2] = after(d_feed_own, token)
        down_near, down_far = split(gradient(down_args[0]), over_ctx(down_away, 1))
        up_args = [
            [after(normed_own, down_far), normed_rest, d_ups["own", i], d_ups["rest", i]] for i in range(2)
        ]
        up_away = gradient(up_args[1], 0)
        up_near, up_far = split(gradient(up_args[0], 0), over_ctx(up_away, 1))
        dn_got = after(dn_got, up_far)
        down_got = over_fsdp(down_far, 1)
    else:
        totals = []
        for left, right in ((acts, None), (None, d_ups)):
            grads = []
            for i in range(2):
                one = jnp.concatenate([left["own", i], left["rest", i]]) if left else (
                    jnp.concatenate([normed_own, normed_rest])
                )
                two = jnp.concatenate([right["own", i], right["rest", i]]) if right else (
                    jnp.concatenate([d_feed_own, d_feed_rest])
                )
                grads.append(dot(one, two, ((0,), (0,))))
            mixed = (grads[0] + over_ctx(grads[1].astype(bf16), 1).astype(f32)).astype(bf16)
            totals.append(lax.psum_scatter(mixed, "fsdp", scatter_dimension=0, tiled=True))

    d_hidden1, d_branch, d_att_near, d_att_far, sums1 = kernel_call(
        branch_kernel,
        [
            shape((own_rows, width)), shape((own_rows, width), bf16),
            shape((own_rows, 2 * group), bf16), shape((own_rows, width - 2 * group), bf16),
            shape((8, width)),
        ],
        [d_hidden2, dn_own, dn_got, normal1, inverse1, out_mine, out_other, vecs],
        scalars=[core],
        flops=0,
    )
    if ways == 2:
        d_attended = [d_att_near, over_ctx(d_att_far, 2)]
    else:
        d_attended = [d_att_near] + [
            over_ctx(d_att_far[:, 2 * (k - 1) * group : 2 * k * group], 2 * k)
            for k in range(1, ways)
        ]

    d_projected = [None, None]
    for i in (1, 0):
        d_query, d_pair = attend_back(
            projected[i], d_attended, i * group, key_docs, query_docs, logs[i], head_size,
        )
        d_projected[i] = (d_query, d_pair)
        if i:
            if merged:
                down_mixed, down_total = finish(down_near, after(down_got, d_query))
                up_got = over_fsdp(after(up_far, down_mixed), 1)
                d_query = after(d_query, down_mixed)
            qkv_away = kernel_call(
                functools.partial(qkv_send_kernel, shard),
                [shape((fsdp_size, shard, columns), bf16)],
                [rounded0, d_query, d_pair],
            )[0]
            out_keep, out_away = kernel_call(
                out_grad_kernel,
                [shape((width, width // 2)), shape((width, width // 2), bf16)],
                [after(attended_own, qkv_away), d_branch],
                scalars=[jnp.stack([ctx, core])],
            )
            out_got = over_ctx(out_away, 1)
            for k in range(int(math.log2(ways))):
                half = out_keep.shape[1] // 2
                bit = (ctx >> (k + 1)) % 2
                if half % 128 == 0:
                    out_keep, out_away = kernel_call(
                        split_kernel, [shape((width, half)), shape((width, half), bf16)],
                        [out_keep, out_got], scalars=[bit],
                    )
                else:
                    both = (out_keep + out_got.astype(f32)).reshape(width, 2, half)
                    out_keep = lax.dynamic_index_in_dim(both, bit, 1, False)
                    out_away = lax.dynamic_index_in_dim(both, 1 - bit, 1, False).astype(bf16)
                out_got = over_ctx(out_away, 2 << k)
            d_attended[0] = after(d_attended[0], out_away)

    qkv_got = over_ctx(qkv_away, 1)
    keep_outs = [
        shape((fsdp_size // 2, shard + VEC, columns)),
        shape((fsdp_size // 2, shard + PAD, columns), bf16),
    ]
    quarter = out_keep.shape[1]
    if merged:
        near, far = kernel_call(
            functools.partial(qkv_vec_keep_kernel, shard),
            keep_outs,
            [
                rounded0, *d_projected[0], *d_projected[1], qkv_got, sums1, sums2,
                *(d_up_sums[part, i] for i in range(2) for part in ("own", "rest")),
            ],
            scalars=[jnp.stack([fsdp % 2, ctx])],
            scratch=[
                pltpu.VMEM((width, columns), f32), pltpu.VMEM((8, width), f32),
                pltpu.VMEM((8, hidden), f32), pltpu.VMEM((fsdp_size, VEC, columns), f32),
            ],
        )
    else:
        def in_groups(pair, size):
            stacked = jnp.stack(pair)
            ordered = jnp.where(core == 0, stacked, stacked[::-1])
            return lax.dynamic_update_slice_in_dim(
                jnp.zeros((ctx_size, size), f32), ordered, ctx - core, 0
            )

        column = lambda value: jnp.sum(value.astype(f32), axis=0)
        vec_query = in_groups([column(d[0]) for d in d_projected], group).reshape(-1)
        vec_value = in_groups([column(d[1][:, group:]) for d in d_projected], group).reshape(-1)
        vec_up = jnp.swapaxes(
            in_groups(
                [d_up_sums["own", i][0] + d_up_sums["rest", i][0] for i in range(2)], group_ff
            ).reshape(ctx_size, fsdp_size, cut_ff), 0, 1,
        ).reshape(fsdp_size, -1)
        vec_model = jnp.concatenate([vec_query, vec_value, sums1[2], sums2[2]]).reshape(fsdp_size, -1)
        vec_gain = jnp.concatenate([sums1[0], sums2[0]]).reshape(fsdp_size, -1)
        vec_shift = jnp.concatenate([sums1[1], sums2[1]]).reshape(fsdp_size, -1)
        vectors = jnp.concatenate([vec_model, vec_up, vec_gain, vec_shift], axis=1)
        vectors = jnp.pad(vectors, ((0, 0), (0, VEC * columns - small_count))).reshape(
            fsdp_size, VEC, columns
        )
        near, far = kernel_call(
            functools.partial(qkv_keep_kernel, shard),
            keep_outs,
            [rounded0, *d_projected[0], qkv_got, vectors],
            scalars=[fsdp % 2],
            scratch=[pltpu.VMEM((width, columns), f32)],
        )
    got = over_fsdp(far, 1)
    if merged:
        up_mixed, up_total = finish(up_near, after(up_got, far))
    out_near, out_far = kernel_call(
        functools.partial(out_keep_kernel, shard),
        [
            shape((fsdp_size // 2, shard, quarter)),
            shape((fsdp_size // 2, shard, quarter), bf16),
        ],
        [after(out_keep, far), out_got],
        scalars=[fsdp % 2],
    )
    out_cross = over_fsdp(out_far, 1)

    dx_own, dx_rest = kernel_call(
        input_kernel,
        [shape((own_rows, width)), shape((rest_rows, width), bf16)],
        [after(d_projected[0][0], out_far, got), d_projected[0][1], *d_projected[1], *w_qkv_pair],
    )
    sends = kernel_call(
        functools.partial(z_send_kernel, shard),
        [shape((shard + VEC, columns + quarter))]
        + [shape((shard + PAD, columns + quarter), bf16)] * (fsdp_size // 2 - 1),
        [near, got, out_near, out_cross],
        scalars=[fsdp // 2],
    )
    mine_block = sends[0]
    if merged:
        up_spread = over_ctx(up_total, 2)
        mine_block = after(mine_block, up_spread)
    total = kernel_call(
        functools.partial(z_sum_kernel, shard),
        [shape((shard + PAD, columns + quarter), bf16)],
        [mine_block, *(over_fsdp(value, 2 * k) for k, value in enumerate(sends[1:], 1))],
    )[0]

    dx_own, dx_got = reduce_tokens(dx_own, dx_rest)
    input_keep, input_send = kernel_call(
        input_sum_kernel, [shape((tokens, width))] * 2, [d_hidden1, dx_own, dx_got]
    )

    if merged:
        def quarters(own, far_own):
            return [own, over_ctx(own, 1), far_own, over_ctx(far_own, 1)]

        grad_down = kernel_call(
            functools.partial(rows_tail_kernel, shard),
            [shape((shard_ff, width))],
            quarters(down_total, over_ctx(after(down_total, up_mixed), 2)),
            scalars=[ctx],
        )[0]
        grad_up = kernel_call(
            functools.partial(columns_tail_kernel, cut_ff),
            [shape((shard, hidden))],
            quarters(up_total, up_spread),
            scalars=[ctx],
        )[0]
        grad_qkv, grad_out, vec_done = kernel_call(
            functools.partial(tail_kernel, shard, group),
            [shape((shard, 3 * width)), shape((shard, width)), shape((VEC, columns))],
            quarters(total, over_ctx(total, 2)),
            scalars=[ctx],
        )
        counts = [b - a for a, b in zip(starts[:-1], starts[1:])]
        vectors = [vec_done[row, :count] for row, count in enumerate(counts)]
    else:
        spread = lambda own: lax.all_gather(own, "ctx", axis=0)
        tail = spread(total)
        grad_qkv = jnp.transpose(
            tail[:, :shard, :columns].reshape(ctx_size, shard, 3, group), (1, 2, 0, 3)
        ).reshape(shard, 3 * width).astype(f32)
        order = []
        levels = int(math.log2(ctx_size))
        for place_index in range(ctx_size):
            order.append(
                sum(((place_index >> (levels - 1 - b)) & 1) << b for b in range(levels))
            )
        grad_out = jnp.concatenate([tail[d, :shard, columns:] for d in order], axis=1).astype(f32)
        vec = tail[:, shard:, :columns].astype(f32)
        vec_done = jnp.sum(vec[:, :VEC] + vec[:, VEC:], axis=0).reshape(-1)
        vectors = [vec_done[a:b] for a, b in zip(starts[:-1], starts[1:])]
        grad_down = spread(totals[0]).reshape(shard_ff, width).astype(f32)
        grad_up = jnp.transpose(
            spread(totals[1]).reshape(ctx_size, shard, fsdp_size, cut_ff), (1, 2, 0, 3)
        ).reshape(shard, hidden).astype(f32)

    def give_back(keep, send):
        got = over_ctx(send, 1)
        return jnp.stack([jnp.where(core == 0, keep, got), jnp.where(core == 0, got, keep)])

    block_output = give_back(result_keep, result_send)[:, None]
    input_grad = give_back(input_keep, input_send)[:, None]
    return (
        block_output, input_grad, grad_qkv, grad_out, grad_up, grad_down,
        *vectors,
    )


def solution(mesh):
    token = P(None, "fsdp", "ctx", None)
    rows = P("fsdp", None)
    flat = P("fsdp")
    return jax.shard_map(
        per_device,
        mesh=mesh,
        in_specs=(
            token, P(None, "fsdp", None), P(None, "fsdp", "ctx"), rows, rows, rows, rows,
            flat, flat, flat, flat, token,
        ),
        out_specs=(token, token, rows, rows, rows, rows, flat, flat, flat, flat),
        check_vma=False,
    )
```

```python
import functools
import math

import jax
import jax.numpy as jnp
from jax import lax
from jax.experimental import pallas as pl
from jax.experimental.pallas import tpu as pltpu
from jax.sharding import PartitionSpec as P

HEADS = 16
EPS = 1e-05
LOG2E = math.log2(math.e)
VEC = 8
PAD = 2 * VEC
f32 = jnp.float32
bf16 = jnp.bfloat16


def dot(left, right, dims=((1,), (0,))):
    return lax.dot_general(left, right, (dims, ((), ())), preferred_element_type=f32)


def over_ctx(value, mask):
    size = lax.axis_size("ctx")
    return lax.ppermute(value, "ctx", [(i, i ^ mask) for i in range(size)])


def over_fsdp(value, mask):
    size = lax.axis_size("fsdp")
    return lax.ppermute(value, "fsdp", [(i, i ^ mask) for i in range(size)])


def after(value, *others):
    return lax.optimization_barrier((value, *others))[0]


def shape(dims, dtype=f32):
    return jax.ShapeDtypeStruct(tuple(dims), dtype)


def kernel_call(body, outs, args, scalars=(), scratch=(), flops=30_000_000_000):
    scalars = [jnp.asarray(s, jnp.int32).reshape(-1) for s in scalars]
    specs = [pl.BlockSpec(memory_space=pltpu.SMEM)] * len(scalars)
    specs += [pl.BlockSpec(memory_space=pltpu.VMEM)] * len(args)
    largest = max(math.prod(a.shape) * 4 for a in [*args, *outs])
    held = sum(math.prod(a.shape) * jnp.dtype(a.dtype).itemsize for a in scratch)
    limit = min(held + max(6 * 2**20, 2 * largest), 56 * 2**20)
    return pl.pallas_call(
        body,
        in_specs=specs,
        out_specs=[pl.BlockSpec(memory_space=pltpu.VMEM)] * len(outs),
        out_shape=list(outs),
        scratch_shapes=list(scratch),
        compiler_params=pltpu.CompilerParams(vmem_limit_bytes=limit),
        cost_estimate=pl.CostEstimate(flops=flops, bytes_accessed=1024, transcendentals=0),
    )(*scalars, *args)


def attend_kernel(head_size, scale, block_ref, whole_ref, key_doc_ref, query_doc_ref, out_ref, log_ref):
    width = out_ref.shape[1]
    same = key_doc_ref[...] == query_doc_ref[...]
    for head in range(width // head_size):
        cut = head * head_size
        query = block_ref[:, cut : cut + head_size]
        key = whole_ref[:, width + cut : width + cut + head_size]
        value = whole_ref[:, 2 * width + cut : 2 * width + cut + head_size]
        scores = jnp.where(same, dot(key, query, ((1,), (1,))), -1e30)
        top = jnp.max(scores, axis=0, keepdims=True)
        expo = jnp.exp2((scores - top) * (scale * LOG2E))
        total = jnp.sum(expo, axis=0, keepdims=True)
        probs = (expo * (1.0 / total)).astype(bf16)
        out_ref[:, cut : cut + head_size] = dot(value, probs, ((0,), (0,))).T.astype(bf16)
        log_ref[head : head + 1, :] = top * (scale * LOG2E) + jnp.log2(total)


def attend(projected, key_docs, query_docs, head_size):
    length, width = projected.shape[0], projected.shape[1] // 3
    heads = width // head_size
    block = min(512, length)
    return pl.pallas_call(
        functools.partial(attend_kernel, head_size, 1.0 / math.sqrt(head_size)),
        grid=(length // block,),
        in_specs=[
            pl.BlockSpec((block, 3 * width), lambda i: (i, 0)),
            pl.BlockSpec((length, 3 * width), lambda i: (0, 0)),
            pl.BlockSpec((length, 1), lambda i: (0, 0)),
            pl.BlockSpec((1, block), lambda i: (0, i)),
        ],
        out_specs=[
            pl.BlockSpec((block, width), lambda i: (i, 0)),
            pl.BlockSpec((heads, block), lambda i: (0, i)),
        ],
        out_shape=[shape((length, width), bf16), shape((heads, length))],
        compiler_params=pltpu.CompilerParams(vmem_limit_bytes=(24 if length <= 512 else 48) * 2**20),
        cost_estimate=pl.CostEstimate(
            flops=0, bytes_accessed=1024, transcendentals=0,
        ),
    )(projected, projected, key_docs, query_docs)


def attend_back_kernel(head_size, scale, steps, first, pieces, *refs):
    block_ref, whole_ref, key_doc_ref, query_doc_ref, log_ref = refs[:5]
    grad_refs, (query_out, pair_out, pair_sum) = refs[5 : 5 + pieces], refs[5 + pieces :]
    width = query_out.shape[1]
    step = pl.program_id(0)
    same = key_doc_ref[...] == query_doc_ref[...]

    if steps > 1:
        @pl.when(step == 0)
        def _():
            pair_sum[...] = jnp.zeros_like(pair_sum)

    def add(place, value):
        if steps > 1:
            pair_sum[:, place : place + head_size] += value
        else:
            pair_out[:, place : place + head_size] = value.astype(bf16)

    for head in range(width // head_size):
        cut = head * head_size
        query = block_ref[:, cut : cut + head_size]
        key = whole_ref[:, width + cut : width + cut + head_size]
        value = whole_ref[:, 2 * width + cut : 2 * width + cut + head_size]
        span = slice(first + cut, first + cut + head_size)
        grad = jnp.concatenate([ref[:, span] for ref in grad_refs]) if pieces > 1 else grad_refs[0][:, span]
        scores = dot(key, query, ((1,), (1,)))
        probs = jnp.where(
            same, jnp.exp2(scores * (scale * LOG2E) - log_ref[head : head + 1, :]), 0.0
        )
        d_probs = dot(value, grad, ((1,), (1,)))
        inner = jnp.sum(probs * d_probs, axis=0, keepdims=True)
        d_scores = (probs * (d_probs - inner)).astype(bf16)
        query_out[:, cut : cut + head_size] = (
            dot(key, d_scores, ((0,), (0,))).T * scale
        ).astype(bf16)
        add(cut, dot(d_scores, query) * scale)
        add(width + cut, dot(probs.astype(bf16), grad))

    if steps > 1:
        @pl.when(step == steps - 1)
        def _():
            pair_out[...] = pair_sum[...].astype(bf16)


def attend_back(projected, grads, first, key_docs, query_docs, logs, head_size):
    length, width = projected.shape[0], projected.shape[1] // 3
    heads = width // head_size
    block = min(512, length)
    steps = length // block
    if steps > 1:
        grads = [jnp.concatenate(grads)]
    grad_rows = [grad.shape[0] // steps for grad in grads]
    return pl.pallas_call(
        functools.partial(
            attend_back_kernel, head_size, 1.0 / math.sqrt(head_size), steps, first, len(grads)
        ),
        grid=(steps,),
        in_specs=[
            pl.BlockSpec((block, 3 * width), lambda i: (i, 0)),
            pl.BlockSpec((length, 3 * width), lambda i: (0, 0)),
            pl.BlockSpec((length, 1), lambda i: (0, 0)),
            pl.BlockSpec((1, block), lambda i: (0, i)),
            pl.BlockSpec((heads, block), lambda i: (0, i)),
        ]
        + [pl.BlockSpec((rows, grads[0].shape[1]), lambda i: (i, 0)) for rows in grad_rows],
        out_specs=[
            pl.BlockSpec((block, width), lambda i: (i, 0)),
            pl.BlockSpec((length, 2 * width), lambda i: (0, 0)),
        ],
        out_shape=[shape((length, width), bf16), shape((length, 2 * width), bf16)],
        scratch_shapes=[pltpu.VMEM((length if steps > 1 else 8, 2 * width), f32)],
        compiler_params=pltpu.CompilerParams(vmem_limit_bytes=(24 if length <= 512 else 56) * 2**20),
        cost_estimate=pl.CostEstimate(flops=0, bytes_accessed=1024, transcendentals=0),
    )(projected, projected, key_docs, query_docs, logs, *grads)


def place_kernel(count, rows, columns, where_ref, *refs):
    pieces, (qkv_ref, small_ref, mine_ref, theirs_ref) = refs[:count], refs[count:]
    for j, piece in enumerate(pieces):
        spare = piece.shape[0] - rows
        start = pl.multiple_of(where_ref[j] * rows, rows)
        qkv_ref[pl.ds(start, rows), :] = piece[:rows, :columns]
        start = pl.multiple_of(where_ref[j] * spare, spare)
        small_ref[pl.ds(start, spare), :] = piece[rows:, :columns]
        for way, ref in enumerate((mine_ref, theirs_ref), 1):
            start = pl.multiple_of(where_ref[way * count + j] * rows, rows)
            ref[pl.ds(start, rows), :] = piece[:rows, columns:]


def place(pieces, orders, rows, columns):
    count, spare = len(pieces), pieces[0].shape[0] - rows
    rest = pieces[0].shape[1] - columns
    return kernel_call(
        functools.partial(place_kernel, count, rows, columns),
        [
            shape((count * rows, columns), bf16), shape((count * spare, columns), bf16),
            shape((count * rows, rest), bf16), shape((count * rows, rest), bf16),
        ],
        pieces,
        scalars=[jnp.concatenate(orders)],
    )


def gather_near(shard):
    size = lax.axis_size("fsdp")
    return [shard] + [over_fsdp(shard, 2 * k) for k in range(1, size // 2)]


def gather_far(near):
    pieces = []
    for value in near:
        pieces += [value, over_fsdp(value, 1)]
    return pieces


def gather_tokens(own):
    have, mask = own, 1
    while 2 * mask < lax.axis_size("ctx"):
        got = over_ctx(have, 2 * mask)
        if lax.axis_size("ctx") == 4:
            return got
        have = jnp.concatenate([have, got])
        mask *= 2
    return have[own.shape[0] :]


def reduce_tokens(own, rest):
    ways = lax.axis_size("ctx") // 2
    if ways == 2:
        return own, over_ctx(rest, 2)
    have, mask = jnp.concatenate([own, rest.astype(f32)]), ways // 2
    while mask > 1:
        half = have.shape[0] // 2
        have = have[:half] + over_ctx(have[half:].astype(bf16), 2 * mask).astype(f32)
        mask //= 2
    half = have.shape[0] // 2
    return have[:half], over_ctx(have[half:].astype(bf16), 2)


def norm_parts(value):
    centred = value - jnp.mean(value, axis=-1, keepdims=True)
    inverse = lax.rsqrt(jnp.mean(centred * centred, axis=-1, keepdims=True) + EPS)
    return centred * inverse, inverse


def norm_back(grad, normal, inverse, gain):
    inner = grad * gain
    return inverse * (
        inner
        - jnp.mean(inner, axis=-1, keepdims=True)
        - normal * jnp.mean(inner * normal, axis=-1, keepdims=True)
    )


def column_sums(*values):
    rows = [jnp.sum(value, axis=0, keepdims=True) for value in values]
    return jnp.concatenate(rows + [jnp.zeros_like(rows[0])] * (8 - len(rows)))


def out_kernel(
    core_ref, att_ref, mine_ref, other_ref, x_ref, vec_ref, normal_ref, inverse_ref, normed_ref, hidden_ref
):
    half = mine_ref.shape[1]
    core = core_ref[0]
    for way, ref in ((core, mine_ref), (1 - core, other_ref)):
        hidden_ref[:, pl.ds(pl.multiple_of(way * half, half), half)] = dot(att_ref[...], ref[...])
    hidden1 = hidden_ref[...] + (x_ref[...].astype(f32) + vec_ref[0:1, :]) + vec_ref[1:2, :]
    normal, inverse = norm_parts(hidden1)
    normal_ref[...] = normal
    inverse_ref[...] = inverse
    normed_ref[...] = (normal * vec_ref[2:3, :] + vec_ref[3:4, :]).astype(bf16)


def views(refs, width):
    if len(refs) == 2:
        return refs
    return refs[0].at[:, : refs[0].shape[1] - width], refs[0].at[:, refs[0].shape[1] - width :]


def forward_kernel(count, first, rows_ref, bias_ref, *refs):
    up_ref, down_ref = views(refs[:count], rows_ref.shape[1])
    act_ref, slope_ref, feed_ref = refs[-3:]
    upward = dot(rows_ref[...], up_ref[...]) + bias_ref[...]
    lower = 0.5 + 0.5 * lax.erf(upward * math.sqrt(0.5))
    density = jnp.exp2(upward * upward * (-0.5 * LOG2E)) * (1.0 / math.sqrt(2.0 * math.pi))
    act = (upward * lower).astype(bf16)
    act_ref[...] = act
    slope_ref[...] = lower + upward * density
    feed = dot(act, down_ref[...])
    if not first:
        feed = feed + refs[count][...]
    feed_ref[...] = feed.astype(feed_ref.dtype)


def feed_forward(rows, weights, bias, feed, dtype):
    count, group_ff = rows.shape[0], bias.shape[1]
    return kernel_call(
        functools.partial(forward_kernel, len(weights), feed is None),
        [shape((count, group_ff), bf16), shape((count, group_ff)), shape(rows.shape, dtype)],
        [rows, bias, *weights] + ([] if feed is None else [feed]),
    )


def backward_kernel(count, first, rows_ref, slope_ref, *refs):
    up_ref, down_ref = views(refs[:count], rows_ref.shape[1])
    d_up_ref, sum_ref, total_ref = refs[-3:]
    d_up = (dot(rows_ref[...], down_ref[...], ((1,), (1,))) * slope_ref[...]).astype(bf16)
    d_up_ref[...] = d_up
    sum_ref[...] = column_sums(d_up.astype(f32))
    total = dot(d_up, up_ref[...], ((1,), (1,)))
    if not first:
        total = total + refs[count][...]
    total_ref[...] = total.astype(total_ref.dtype)


def feed_backward(rows, weights, slope, total, dtype):
    count, group_ff = slope.shape
    return kernel_call(
        functools.partial(backward_kernel, len(weights), total is None),
        [shape((count, group_ff), bf16), shape((8, group_ff)), shape(rows.shape, dtype)],
        [rows, slope, *weights] + ([] if total is None else [total]),
    )


def turn_kernel(
    normal_ref, feed_ref, got_ref, cot_ref, vec_ref, keep_ref, send_ref, d_hidden_ref, d_feed_ref, sum_ref
):
    normed1 = normal_ref[...] * vec_ref[2:3, :] + vec_ref[3:4, :]
    hidden2 = normed1 + (feed_ref[...] + got_ref[...].astype(f32) + vec_ref[4:5, :])
    normal, inverse = norm_parts(hidden2)
    gain = vec_ref[5:6, :]
    result = (normal * gain + vec_ref[6:7, :]).astype(bf16)
    keep_ref[...] = result[: keep_ref.shape[0]]
    send_ref[...] = result[keep_ref.shape[0] :]
    cot = cot_ref[...].astype(f32)
    d_hidden2 = norm_back(cot, normal, inverse, gain)
    d_hidden_ref[...] = d_hidden2
    d_feed = d_hidden2.astype(bf16)
    d_feed_ref[...] = d_feed
    sum_ref[...] = column_sums(cot * normal, cot, d_feed.astype(f32))


def branch_kernel(
    core_ref, d_hidden2_ref, own_ref, got_ref, normal_ref, inverse_ref, mine_ref, other_ref, vec_ref,
    d_hidden1_ref, d_branch_ref, near_ref, far_ref, sum_ref,
):
    core, half, near = core_ref[0], mine_ref.shape[1], near_ref.shape[1]
    d_normed = d_hidden2_ref[...] + (own_ref[...] + got_ref[...].astype(f32))
    normal = normal_ref[...]
    d_hidden1 = norm_back(d_normed, normal, inverse_ref[...], vec_ref[2:3, :])
    d_hidden1_ref[...] = d_hidden1
    d_branch = d_hidden1.astype(bf16)
    d_branch_ref[...] = d_branch
    first = d_branch_ref[:, pl.ds(pl.multiple_of(core * half, half), half)]
    second = d_branch_ref[:, pl.ds(pl.multiple_of((1 - core) * half, half), half)]
    for ref, start in ((far_ref, near), (near_ref, 0)):
        span = slice(start, start + ref.shape[1])
        ref[...] = (
            dot(first, mine_ref[span, :], ((1,), (1,)))
            + dot(second, other_ref[span, :], ((1,), (1,)))
        ).astype(bf16)
    sum_ref[...] = column_sums(d_normed * normal, d_normed, d_branch.astype(f32))


def grad_kernel(one_ref, two_ref, left_ref, right_ref, out_ref):
    out_ref[...] = (
        dot(one_ref[...], left_ref[...], ((0,), (0,))) + dot(two_ref[...], right_ref[...], ((0,), (0,)))
    ).astype(bf16)


def grad_split_kernel(shard, odd_ref, keep_ref, got_ref, near_ref, far_ref):
    odd = odd_ref[0]
    for parity, ref in ((1 - odd, far_ref), (odd, near_ref)):
        for j in range(ref.shape[0]):
            rows = pl.ds(pl.multiple_of((2 * j + parity) * shard, shard), shard)
            ref[j] = (keep_ref[rows, :].astype(f32) + got_ref[rows, :].astype(f32)).astype(bf16)


def add_kernel(near_ref, got_ref, out_ref):
    out_ref[...] = (near_ref[...].astype(f32) + got_ref[...].astype(f32)).astype(out_ref.dtype)


def out_grad_kernel(ctx_ref, att_ref, d_branch_ref, keep_ref, send_ref):
    ctx = ctx_ref[0]
    core = ctx_ref[1]
    group, half = ctx_ref_group(att_ref, keep_ref), keep_ref.shape[1]
    for way, ref in ((core, keep_ref), (1 - core, send_ref)):
        columns = d_branch_ref[:, pl.ds(pl.multiple_of(way * half, half), half)]
        grad = dot(att_ref[...], columns, ((0,), (0,)))
        for i in range(grad.shape[0] // group):
            start = pl.multiple_of((ctx ^ i) * group, group)
            ref[pl.ds(start, group), :] = grad[i * group : (i + 1) * group].astype(ref.dtype)


def ctx_ref_group(att_ref, keep_ref):
    return att_ref.shape[1] // lax.axis_size("ctx")


def split_kernel(bit_ref, keep_ref, got_ref, kept_ref, send_ref):
    half = kept_ref.shape[1]
    for way, ref in ((bit_ref[0], kept_ref), (1 - bit_ref[0], send_ref)):
        span = pl.ds(pl.multiple_of(way * half, half), half)
        ref[...] = (keep_ref[:, span] + got_ref[:, span].astype(f32)).astype(ref.dtype)


def pack(values):
    high = values.astype(bf16).astype(f32)
    return jnp.concatenate([high, values - high]).astype(bf16)


def unpack(rows):
    rows = rows.astype(f32)
    return rows[:VEC] + rows[VEC:]


def qkv_send_kernel(shard, r0_ref, dq_ref, dkv_ref, out_ref):
    width = dq_ref.shape[1]
    query = dot(r0_ref[...], dq_ref[...], ((0,), (0,)))
    pair = dot(r0_ref[...], dkv_ref[...], ((0,), (0,)))
    for block in range(out_ref.shape[0]):
        rows = slice(block * shard, (block + 1) * shard)
        out_ref[block, :, :width] = query[rows].astype(bf16)
        out_ref[block, :, width:] = pair[rows].astype(bf16)


def split_by_parity(shard, odd, grad_ref, got_ref, vec_ref, near_ref, far_ref):
    for parity, ref in ((1 - odd, far_ref), (odd, near_ref)):
        for j in range(ref.shape[0]):
            block = 2 * j + parity
            rows = pl.ds(pl.multiple_of(block * shard, shard), shard)
            ref[j, :shard] = (grad_ref[rows, :] + got_ref[block].astype(f32)).astype(ref.dtype)
            vec = vec_ref[block]
            ref[j, shard:] = vec if ref.dtype == f32 else pack(vec)


def qkv_keep_kernel(
    shard, odd_ref, r0_ref, dq_ref, dkv_ref, got_ref, vec_ref, near_ref, far_ref, grad_ref
):
    width = dq_ref.shape[1]
    grad_ref[:, :width] = dot(r0_ref[...], dq_ref[...], ((0,), (0,)))
    grad_ref[:, width:] = dot(r0_ref[...], dkv_ref[...], ((0,), (0,)))
    split_by_parity(shard, odd_ref[0], grad_ref, got_ref, vec_ref, near_ref, far_ref)


def qkv_vec_keep_kernel(
    shard, place_ref, r0_ref, dq_ref, dkv_ref, dq_other_ref, dkv_other_ref, got_ref, sums1_ref, sums2_ref,
    up_own_ref, up_rest_ref, up_own_other_ref, up_rest_other_ref, near_ref, far_ref, grad_ref, flat_ref,
    up_ref, vec_ref,
):
    odd, ctx = place_ref[0], place_ref[1]
    width = dq_ref.shape[1]
    size = vec_ref.shape[0]
    flat_ref[...] = jnp.zeros_like(flat_ref)
    up_ref[...] = jnp.zeros_like(up_ref)
    vec_ref[...] = jnp.zeros_like(vec_ref)
    cut = up_own_ref.shape[1] // size
    pairs = (
        (dq_ref, dkv_ref, up_own_ref, up_rest_ref),
        (dq_other_ref, dkv_other_ref, up_own_other_ref, up_rest_other_ref),
    )
    for i, (query, pair, own, rest) in enumerate(pairs):
        who = ctx ^ i
        span = pl.ds(pl.multiple_of(who * width, width), width)
        flat_ref[0:1, span] = jnp.sum(query[...].astype(f32), axis=0, keepdims=True)
        flat_ref[1:2, span] = jnp.sum(pair[:, width:].astype(f32), axis=0, keepdims=True)
        for f in range(size):
            start = pl.multiple_of((f * (up_ref.shape[1] // cut // size) + who) * cut, cut)
            here = slice(f * cut, (f + 1) * cut)
            up_ref[0:1, pl.ds(start, cut)] = own[0:1, here] + rest[0:1, here]
    full = flat_ref.shape[1]
    model = (flat_ref[0:1], flat_ref[1:2], sums1_ref[2:3], sums2_ref[2:3])
    rows = (model, (up_ref[0:1],), (sums1_ref[0:1], sums2_ref[0:1]), (sums1_ref[1:2], sums2_ref[1:2]))
    for row, sources in enumerate(rows):
        length = sources[0].shape[1]
        part = len(sources) * length // size
        for f in range(size):
            source, start = sources[f * part // length], f * part % length
            vec_ref[f, row : row + 1, :part] = source[:, start : start + part]
    grad_ref[:, :width] = dot(r0_ref[...], dq_ref[...], ((0,), (0,)))
    grad_ref[:, width:] = dot(r0_ref[...], dkv_ref[...], ((0,), (0,)))
    split_by_parity(shard, odd, grad_ref, got_ref, vec_ref, near_ref, far_ref)


def input_kernel(dq_ref, dkv_ref, dq_other_ref, dkv_other_ref, mine_ref, other_ref, own_ref, rest_ref):
    width = dq_ref.shape[1]
    cut = own_ref.shape[0]
    for ref, rows in ((rest_ref, slice(cut, dq_ref.shape[0])), (own_ref, slice(0, cut))):
        total = 0.0
        for query, pair, weights in (
            (dq_ref, dkv_ref, mine_ref), (dq_other_ref, dkv_other_ref, other_ref)
        ):
            total = total + dot(query[rows, :], weights[:, :width], ((1,), (1,)))
            total = total + dot(pair[rows, :], weights[:, width:], ((1,), (1,)))
        ref[...] = total.astype(ref.dtype)


def input_sum_kernel(one_ref, two_ref, got_ref, keep_ref, send_ref):
    total = one_ref[...] + (two_ref[...] + got_ref[...].astype(f32))
    keep_ref[...] = total[: keep_ref.shape[0]]
    send_ref[...] = total[keep_ref.shape[0] :]


def out_keep_kernel(shard, odd_ref, keep_ref, got_ref, near_ref, far_ref):
    odd = odd_ref[0]
    for parity, ref in ((1 - odd, far_ref), (odd, near_ref)):
        for j in range(ref.shape[0]):
            rows = pl.ds(pl.multiple_of((2 * j + parity) * shard, shard), shard)
            ref[j] = (keep_ref[rows, :] + got_ref[rows, :].astype(f32)).astype(ref.dtype)


def z_send_kernel(shard, z_ref, near_ref, got_ref, out_near_ref, out_got_ref, *outs):
    z = z_ref[0]
    columns = near_ref.shape[2]
    for k, ref in enumerate(outs):
        block = z ^ k
        got = got_ref[block]
        near = near_ref[block]
        ref[:shard, :columns] = (near[:shard] + got[:shard].astype(f32)).astype(ref.dtype)
        ref[:shard, columns:] = (
            out_near_ref[block] + out_got_ref[block].astype(f32)
        ).astype(ref.dtype)
        vec = near[shard:] + unpack(got[shard:])
        ref[shard:, :columns] = vec if ref.dtype == f32 else pack(vec)
        ref[shard:, columns:] = jnp.zeros_like(ref[shard:, columns:])


def z_sum_kernel(shard, mine_ref, *refs):
    gots, out_ref = refs[:-1], refs[-1]
    value, vec = mine_ref[:shard], mine_ref[shard:]
    for ref in gots:
        value = value + ref[:shard].astype(f32)
        vec = vec + unpack(ref[shard:])
    out_ref[:shard] = value.astype(bf16)
    out_ref[shard:] = pack(vec)


def tail_kernel(shard, group, ctx_ref, *refs):
    pieces, (qkv_ref, out_ref, vec_ref) = refs[:4], refs[4:]
    ctx = ctx_ref[0]
    width = 4 * group
    for i, piece in enumerate(pieces):
        who = ctx ^ i
        for third in range(3):
            start = pl.multiple_of(third * width + who * group, group)
            qkv_ref[:, pl.ds(start, group)] = piece[
                :shard, third * group : (third + 1) * group
            ].astype(f32)
        start = pl.multiple_of(((who % 2) * 2 + who // 2) * group, group)
        out_ref[:, pl.ds(start, group)] = piece[:shard, 3 * group :].astype(f32)
    vec = [unpack(piece[shard:, : 3 * group]) for piece in pieces]
    vec_ref[...] = (vec[0] + vec[1]) + (vec[2] + vec[3])


def rows_tail_kernel(rows, ctx_ref, *refs):
    pieces, out_ref = refs[:-1], refs[-1]
    for i, piece in enumerate(pieces):
        start = pl.multiple_of((ctx_ref[0] ^ i) * rows, rows)
        out_ref[pl.ds(start, rows), :] = piece[...].astype(f32)


def columns_tail_kernel(cut, ctx_ref, *refs):
    pieces, out_ref = refs[:-1], refs[-1]
    for i, piece in enumerate(pieces):
        for block in range(piece.shape[1] // cut):
            start = pl.multiple_of((block * len(pieces) + (ctx_ref[0] ^ i)) * cut, cut)
            out_ref[:, pl.ds(start, cut)] = piece[:, block * cut : (block + 1) * cut].astype(f32)


def per_device(
    inputs, timestep, doc_ids, w_qkv, w_out, w_up, w_down, bias_model, bias_up,
    norm_gains, norm_shifts, cotangent,
):
    ctx, ctx_size = lax.axis_index("ctx"), lax.axis_size("ctx")
    fsdp, fsdp_size = lax.axis_index("fsdp"), lax.axis_size("fsdp")
    core, ways = ctx % 2, ctx_size // 2
    tokens, width = inputs.shape[2], w_out.shape[1]
    hidden = w_up.shape[1]
    head_size = width // HEADS
    own_rows = 2 * tokens
    rest_rows = (ways - 1) * own_rows
    group = width // ctx_size
    columns = 3 * group
    group_ff = hidden // ctx_size
    shard = w_out.shape[0]
    shard_ff = w_down.shape[0]
    cut_ff = hidden // (fsdp_size * ctx_size)
    fsdp_range = jnp.arange(fsdp_size)
    natural = fsdp_range ^ fsdp

    small = jnp.concatenate([bias_model, bias_up, norm_gains, norm_shifts])
    small_count = small.shape[0]
    qkv_group = lax.dynamic_index_in_dim(
        w_qkv.reshape(shard, 3, ctx_size, group), ctx, 2, False
    ).reshape(shard, columns)
    small_rows = jnp.pad(small, (0, PAD * columns - small_count)).reshape(PAD, columns)
    out_send = lax.dynamic_index_in_dim(w_out.reshape(shard, 2, width // 2), core, 1, False)
    first_send = jnp.concatenate(
        [
            jnp.concatenate([qkv_group, small_rows]),
            jnp.concatenate([out_send, jnp.zeros((PAD, width // 2), bf16)]),
        ],
        axis=1,
    )
    first_pieces = gather_far(gather_near(first_send))
    up_send = lax.dynamic_index_in_dim(
        w_up.reshape(shard, fsdp_size, ctx_size, cut_ff), ctx, 2, False
    ).reshape(shard, group_ff)
    down_send = lax.dynamic_index_in_dim(
        w_down.reshape(ctx_size, shard_ff // ctx_size, width), ctx, 0, False
    )
    merged = up_send.shape == down_send.shape and ctx_size == 4 and cut_ff % 128 == 0
    feed_sends = [jnp.concatenate([up_send, down_send], axis=1)] if merged else [up_send, down_send]
    feed_mine = [lax.all_gather(send, "fsdp", axis=0, tiled=True) for send in feed_sends]

    docs = doc_ids[:, 0].astype(bf16)
    doc_rows = jnp.pad(docs[:, None, :], ((0, 0), (0, PAD - 1), (0, width - tokens)))
    mine, theirs = (
        [lax.dynamic_index_in_dim(a, c, 0, False) for a in (inputs[:, 0], doc_rows, cotangent[:, 0])]
        for c in (core, 1 - core)
    )
    swapped = over_ctx(jnp.concatenate(theirs), 1)
    x_own = jnp.concatenate([mine[0], swapped[:tokens]])
    cot_own = jnp.concatenate([mine[2], swapped[tokens + PAD :]])
    doc_own = jnp.concatenate([mine[1][:1, :tokens], swapped[tokens : tokens + 1, :tokens]], axis=1)
    packed = jnp.concatenate([x_own, jnp.pad(doc_own, ((0, PAD - 1), (0, width - own_rows)))])
    rest = gather_tokens(packed).reshape(ways - 1, own_rows + PAD, width)
    x_rest = rest[:, :own_rows].reshape(rest_rows, width)
    doc_all = jnp.concatenate([doc_own[0], rest[:, own_rows, :own_rows].reshape(-1)]).astype(f32)
    key_docs, query_docs = doc_all[:, None], doc_all[None, :]
    time_row = lax.dynamic_index_in_dim(timestep[:, 0], core, 0, True).astype(f32)
    rounded0 = (jnp.concatenate([x_own, x_rest]).astype(f32) + time_row).astype(bf16)

    ratio = fsdp_size // ctx_size
    orders = [natural] + [
        ((natural // ratio) ^ who) * ratio + natural % ratio for who in (ctx, ctx ^ 1)
    ]
    w_qkv_mine, small_all, out_mine, out_theirs = place(first_pieces, orders, shard, columns)
    w_qkv_pair = (w_qkv_mine, over_ctx(w_qkv_mine, 1))
    small_all = small_all.reshape(fsdp_size, PAD * columns)[:, :small_count].astype(f32)
    starts = [0, bias_model.shape[0]]
    starts.append(starts[1] + bias_up.shape[0])
    starts.append(starts[2] + norm_gains.shape[0])
    starts.append(small_count)
    b_model, b_up, gains, shifts = (
        small_all[:, a:b].reshape(-1) for a, b in zip(starts[:-1], starts[1:])
    )
    vecs = jnp.stack(
        [
            time_row[0], b_model[2 * width : 3 * width], gains[:width], shifts[:width],
            b_model[3 * width :], gains[width:], shifts[width:], jnp.zeros((width,), f32),
        ]
    )
    b_up_groups = b_up.reshape(fsdp_size, ctx_size, cut_ff)

    b_up_pair = [
        lax.dynamic_index_in_dim(b_up_groups, ctx ^ i, 1, False).reshape(1, group_ff)
        for i in range(2)
    ]

    projected, attended, logs = [], [], []
    for i in range(2):
        who = ctx ^ i
        b_query = lax.dynamic_slice_in_dim(b_model, who * group, group)
        b_value = lax.dynamic_slice_in_dim(b_model, width + who * group, group)
        bias = jnp.concatenate([b_query, jnp.zeros_like(b_query), b_value])
        weights = after(w_qkv_pair[i], *attended, *b_up_pair, vecs, cot_own)
        proj = (dot(rounded0, weights) + bias[None]).astype(bf16)
        out, log = attend(proj, key_docs, query_docs, head_size)
        projected.append(proj)
        attended.append(out)
        logs.append(log)
    attended_pair = jnp.concatenate(attended, axis=1)
    attended_cols = [attended_pair[:own_rows]]
    for k in range(1, ways):
        attended_cols.append(over_ctx(attended_pair[k * own_rows : (k + 1) * own_rows], 2 * k))
    attended_own = jnp.concatenate(attended_cols, axis=1)

    out_other = over_ctx(out_theirs, 1)
    normal1, inverse1, normed_own = kernel_call(
        out_kernel,
        [shape((own_rows, width)), shape((own_rows, 1)), shape((own_rows, width), bf16)],
        [attended_own, out_mine, out_other, x_own, vecs],
        scalars=[core],
        scratch=[pltpu.VMEM((own_rows, width), f32)],
    )
    normed_rest = gather_tokens(normed_own)

    feed_mine = [after(w, normed_rest) for w in feed_mine]
    feed_pair = (feed_mine, [over_ctx(w, 1) for w in feed_mine])
    acts, slopes, feeds = {}, {}, {"rest": None, "own": None}
    token = normed_own
    for part, i in (("own", 0), ("rest", 0), ("rest", 1), ("own", 1)):
        rows = normed_own if part == "own" else normed_rest
        acts[part, i], slopes[part, i], feeds[part] = feed_forward(
            after(rows, token), feed_pair[i], b_up_pair[i], feeds[part],
            bf16 if i == 1 and part == "rest" else f32,
        )
        token = acts[part, i]
    feed_own, feed_got = reduce_tokens(feeds["own"], feeds["rest"])

    result_keep, result_send, d_hidden2, d_feed_own, sums2 = kernel_call(
        turn_kernel,
        [
            shape((tokens, width), bf16), shape((tokens, width), bf16), shape((own_rows, width)),
            shape((own_rows, width), bf16), shape((8, width)),
        ],
        [normal1, feed_own, feed_got, cot_own, vecs],
    )
    d_feed_rest = gather_tokens(d_feed_own)

    def gradient(args, flops=30_000_000_000):
        return kernel_call(grad_kernel, [shape((width, width), bf16)], args, flops=flops)[0]

    def split(kept, got):
        return kernel_call(
            functools.partial(grad_split_kernel, shard),
            [shape((fsdp_size // 2, shard, width), bf16)] * 2,
            [kept, got],
            scalars=[fsdp % 2],
        )

    sides = [[2 * k + p for k in range(fsdp_size // 2)] for p in range(2)]

    def finish(near, got):
        mixed = kernel_call(add_kernel, [shape(near.shape, bf16)], [near, got])[0]
        return mixed, lax.psum_scatter(
            mixed.reshape(-1, width), "fsdp", scatter_dimension=0, tiled=True,
            axis_index_groups=sides,
        )

    d_ups, d_up_sums, d_normed = {}, {}, {}
    token = d_feed_own
    for part, rows in (("own", d_feed_own), ("rest", d_feed_rest)):
        total = None
        if merged and part == "rest":
            down_args = [
                [acts["own", i], acts["rest", i], after(d_feed_own, token), d_feed_rest] for i in range(2)
            ]
            down_away = gradient(down_args[1])
            token = down_away
        for i in range(2):
            d_ups[part, i], d_up_sums[part, i], total = feed_backward(
                after(rows, token), feed_pair[i], slopes[part, i], total,
                bf16 if i == 1 and part == "rest" else f32,
            )
            token = d_ups[part, i]
        d_normed[part] = total
    dn_own, dn_got = reduce_tokens(d_normed["own"], d_normed["rest"])

    if merged:
        down_args[0][2] = after(d_feed_own, token)
        down_near, down_far = split(gradient(down_args[0]), over_ctx(down_away, 1))
        up_args = [
            [after(normed_own, down_far), normed_rest, d_ups["own", i], d_ups["rest", i]] for i in range(2)
        ]
        up_away = gradient(up_args[1], 0)
        up_near, up_far = split(gradient(up_args[0], 0), over_ctx(up_away, 1))
        dn_got = after(dn_got, up_far)
        down_got = over_fsdp(down_far, 1)
    else:
        totals = []
        for left, right in ((acts, None), (None, d_ups)):
            grads = []
            for i in range(2):
                one = jnp.concatenate([left["own", i], left["rest", i]]) if left else (
                    jnp.concatenate([normed_own, normed_rest])
                )
                two = jnp.concatenate([right["own", i], right["rest", i]]) if right else (
                    jnp.concatenate([d_feed_own, d_feed_rest])
                )
                grads.append(dot(one, two, ((0,), (0,))))
            mixed = (grads[0] + over_ctx(grads[1].astype(bf16), 1).astype(f32)).astype(bf16)
            totals.append(lax.psum_scatter(mixed, "fsdp", scatter_dimension=0, tiled=True))

    d_hidden1, d_branch, d_att_near, d_att_far, sums1 = kernel_call(
        branch_kernel,
        [
            shape((own_rows, width)), shape((own_rows, width), bf16),
            shape((own_rows, 2 * group), bf16), shape((own_rows, width - 2 * group), bf16),
            shape((8, width)),
        ],
        [d_hidden2, dn_own, dn_got, normal1, inverse1, out_mine, out_other, vecs],
        scalars=[core],
        flops=0,
    )
    if ways == 2:
        d_attended = [d_att_near, over_ctx(d_att_far, 2)]
    else:
        d_attended = [d_att_near] + [
            over_ctx(d_att_far[:, 2 * (k - 1) * group : 2 * k * group], 2 * k)
            for k in range(1, ways)
        ]

    d_projected = [None, None]
    for i in (1, 0):
        d_query, d_pair = attend_back(
            projected[i], d_attended, i * group, key_docs, query_docs, logs[i], head_size,
        )
        d_projected[i] = (d_query, d_pair)
        if i:
            if merged:
                down_mixed, down_total = finish(down_near, after(down_got, d_query))
                up_got = over_fsdp(after(up_far, down_mixed), 1)
                d_query = after(d_query, down_mixed)
            qkv_away = kernel_call(
                functools.partial(qkv_send_kernel, shard),
                [shape((fsdp_size, shard, columns), bf16)],
                [rounded0, d_query, d_pair],
            )[0]
            out_keep, out_away = kernel_call(
                out_grad_kernel,
                [shape((width, width // 2)), shape((width, width // 2), bf16)],
                [after(attended_own, qkv_away), d_branch],
                scalars=[jnp.stack([ctx, core])],
            )
            out_got = over_ctx(out_away, 1)
            for k in range(int(math.log2(ways))):
                half = out_keep.shape[1] // 2
                bit = (ctx >> (k + 1)) % 2
                if half % 128 == 0:
                    out_keep, out_away = kernel_call(
                        split_kernel, [shape((width, half)), shape((width, half), bf16)],
                        [out_keep, out_got], scalars=[bit],
                    )
                else:
                    both = (out_keep + out_got.astype(f32)).reshape(width, 2, half)
                    out_keep = lax.dynamic_index_in_dim(both, bit, 1, False)
                    out_away = lax.dynamic_index_in_dim(both, 1 - bit, 1, False).astype(bf16)
                out_got = over_ctx(out_away, 2 << k)
            d_attended[0] = after(d_attended[0], out_away)

    qkv_got = over_ctx(qkv_away, 1)
    keep_outs = [
        shape((fsdp_size // 2, shard + VEC, columns)),
        shape((fsdp_size // 2, shard + PAD, columns), bf16),
    ]
    quarter = out_keep.shape[1]
    if merged:
        near, far = kernel_call(
            functools.partial(qkv_vec_keep_kernel, shard),
            keep_outs,
            [
                rounded0, *d_projected[0], *d_projected[1], qkv_got, sums1, sums2,
                *(d_up_sums[part, i] for i in range(2) for part in ("own", "rest")),
            ],
            scalars=[jnp.stack([fsdp % 2, ctx])],
            scratch=[
                pltpu.VMEM((width, columns), f32), pltpu.VMEM((8, width), f32),
                pltpu.VMEM((8, hidden), f32), pltpu.VMEM((fsdp_size, VEC, columns), f32),
            ],
        )
    else:
        def in_groups(pair, size):
            stacked = jnp.stack(pair)
            ordered = jnp.where(core == 0, stacked, stacked[::-1])
            return lax.dynamic_update_slice_in_dim(
                jnp.zeros((ctx_size, size), f32), ordered, ctx - core, 0
            )

        column = lambda value: jnp.sum(value.astype(f32), axis=0)
        vec_query = in_groups([column(d[0]) for d in d_projected], group).reshape(-1)
        vec_value = in_groups([column(d[1][:, group:]) for d in d_projected], group).reshape(-1)
        vec_up = jnp.swapaxes(
            in_groups(
                [d_up_sums["own", i][0] + d_up_sums["rest", i][0] for i in range(2)], group_ff
            ).reshape(ctx_size, fsdp_size, cut_ff), 0, 1,
        ).reshape(fsdp_size, -1)
        vec_model = jnp.concatenate([vec_query, vec_value, sums1[2], sums2[2]]).reshape(fsdp_size, -1)
        vec_gain = jnp.concatenate([sums1[0], sums2[0]]).reshape(fsdp_size, -1)
        vec_shift = jnp.concatenate([sums1[1], sums2[1]]).reshape(fsdp_size, -1)
        vectors = jnp.concatenate([vec_model, vec_up, vec_gain, vec_shift], axis=1)
        vectors = jnp.pad(vectors, ((0, 0), (0, VEC * columns - small_count))).reshape(
            fsdp_size, VEC, columns
        )
        near, far = kernel_call(
            functools.partial(qkv_keep_kernel, shard),
            keep_outs,
            [rounded0, *d_projected[0], qkv_got, vectors],
            scalars=[fsdp % 2],
            scratch=[pltpu.VMEM((width, columns), f32)],
        )
    got = over_fsdp(far, 1)
    if merged:
        up_mixed, up_total = finish(up_near, after(up_got, far))
    out_near, out_far = kernel_call(
        functools.partial(out_keep_kernel, shard),
        [
            shape((fsdp_size // 2, shard, quarter)),
            shape((fsdp_size // 2, shard, quarter), bf16),
        ],
        [after(out_keep, far), out_got],
        scalars=[fsdp % 2],
    )
    out_cross = over_fsdp(out_far, 1)

    dx_own, dx_rest = kernel_call(
        input_kernel,
        [shape((own_rows, width)), shape((rest_rows, width), bf16)],
        [after(d_projected[0][0], out_far, got), d_projected[0][1], *d_projected[1], *w_qkv_pair],
    )
    sends = kernel_call(
        functools.partial(z_send_kernel, shard),
        [shape((shard + VEC, columns + quarter))]
        + [shape((shard + PAD, columns + quarter), bf16)] * (fsdp_size // 2 - 1),
        [near, got, out_near, out_cross],
        scalars=[fsdp // 2],
    )
    mine_block = sends[0]
    if merged:
        up_spread = over_ctx(up_total, 2)
        mine_block = after(mine_block, up_spread)
    total = kernel_call(
        functools.partial(z_sum_kernel, shard),
        [shape((shard + PAD, columns + quarter), bf16)],
        [mine_block, *(over_fsdp(value, 2 * k) for k, value in enumerate(sends[1:], 1))],
    )[0]

    dx_own, dx_got = reduce_tokens(dx_own, dx_rest)
    input_keep, input_send = kernel_call(
        input_sum_kernel, [shape((tokens, width))] * 2, [d_hidden1, dx_own, dx_got]
    )

    if merged:
        def quarters(own, far_own):
            return [own, over_ctx(own, 1), far_own, over_ctx(far_own, 1)]

        grad_down = kernel_call(
            functools.partial(rows_tail_kernel, shard),
            [shape((shard_ff, width))],
            quarters(down_total, over_ctx(after(down_total, up_mixed), 2)),
            scalars=[ctx],
        )[0]
        grad_up = kernel_call(
            functools.partial(columns_tail_kernel, cut_ff),
            [shape((shard, hidden))],
            quarters(up_total, up_spread),
            scalars=[ctx],
        )[0]
        grad_qkv, grad_out, vec_done = kernel_call(
            functools.partial(tail_kernel, shard, group),
            [shape((shard, 3 * width)), shape((shard, width)), shape((VEC, columns))],
            quarters(total, over_ctx(total, 2)),
            scalars=[ctx],
        )
        counts = [b - a for a, b in zip(starts[:-1], starts[1:])]
        vectors = [vec_done[row, :count] for row, count in enumerate(counts)]
    else:
        spread = lambda own: lax.all_gather(own, "ctx", axis=0)
        tail = spread(total)
        grad_qkv = jnp.transpose(
            tail[:, :shard, :columns].reshape(ctx_size, shard, 3, group), (1, 2, 0, 3)
        ).reshape(shard, 3 * width).astype(f32)
        order = []
        levels = int(math.log2(ctx_size))
        for place_index in range(ctx_size):
            order.append(
                sum(((place_index >> (levels - 1 - b)) & 1) << b for b in range(levels))
            )
        grad_out = jnp.concatenate([tail[d, :shard, columns:] for d in order], axis=1).astype(f32)
        vec = tail[:, shard:, :columns].astype(f32)
        vec_done = jnp.sum(vec[:, :VEC] + vec[:, VEC:], axis=0).reshape(-1)
        vectors = [vec_done[a:b] for a, b in zip(starts[:-1], starts[1:])]
        grad_down = spread(totals[0]).reshape(shard_ff, width).astype(f32)
        grad_up = jnp.transpose(
            spread(totals[1]).reshape(ctx_size, shard, fsdp_size, cut_ff), (1, 2, 0, 3)
        ).reshape(shard, hidden).astype(f32)

    def give_back(keep, send):
        got = over_ctx(send, 1)
        return jnp.stack([jnp.where(core == 0, keep, got), jnp.where(core == 0, got, keep)])

    block_output = give_back(result_keep, result_send)[:, None]
    input_grad = give_back(input_keep, input_send)[:, None]
    return (
        block_output, input_grad, grad_qkv, grad_out, grad_up, grad_down,
        *vectors,
    )


def solution(mesh):
    token = P(None, "fsdp", "ctx", None)
    rows = P("fsdp", None)
    flat = P("fsdp")
    return jax.shard_map(
        per_device,
        mesh=mesh,
        in_specs=(
            token, P(None, "fsdp", None), P(None, "fsdp", "ctx"), rows, rows, rows, rows,
            flat, flat, flat, flat, token,
        ),
        out_specs=(token, token, rows, rows, rows, rows, flat, flat, flat, flat),
        check_vma=False,
    )
```
